32 devices in a mesh: dp: 8 (over z, x), mp: 4 (over y, core).
Axes of the slice: x: 2, y: 2, z: 4, core: 2. Of those that a mesh axis runs over, the one named last changes fastest.
Arguments:
- hidden: bfloat16 [8, 2048, 768], P('dp', 'mp'), may hold values from -6 to 6
- past_states: bfloat16 [8, 512, 768], P('dp'), may hold values from -6 to 6
- reset_flags: int32 [8], P('dp'), may hold values 0 or 1
- sample_positions: int32 [8, 4, 512], P('dp', 'mp'), may hold values from 0 to 511
- norm1_gain: float32 [768], replicated, may hold values from 0.25 to 1.75
- norm1_shift: float32 [768], replicated, may hold values from -1.75 to 1.75
- w_query: bfloat16 [768, 768], replicated, may hold values from -0.21875 to 0.21875
- bias_query: float32 [768], replicated, may hold values from -1.75 to 1.75
- w_key: bfloat16 [768, 768], replicated, may hold values from -0.21875 to 0.21875
- w_value: bfloat16 [768, 768], replicated, may hold values from -0.21875 to 0.21875
- bias_value: float32 [768], replicated, may hold values from -0.625 to 0.625
- w_attn_out: bfloat16 [768, 768], replicated, may hold values from -1.75 to 1.75
- bias_attn_out: float32 [768], replicated, may hold values from -1.75 to 1.75
- norm2_gain: float32 [768], replicated, may hold values from 0.25 to 1.75
- norm2_shift: float32 [768], replicated, may hold values from -1.75 to 1.75
- w_mlp_in: bfloat16 [768, 3072], P(None, 'mp'), may hold values from -0.21875 to 0.21875
- bias_mlp_in: float32 [3072], P('mp'), may hold values from -1.75 to 1.75
- w_mlp_out: bfloat16 [3072, 768], P('mp'), may hold values from -0.109375 to 0.109375
- bias_mlp_out: float32 [768], replicated, may hold values from -1.75 to 1.75
- cotangent: bfloat16 [8, 2048, 768], P('dp', 'mp'), may hold values from -6 to 6
Outputs:
- output: bfloat16 [8, 2048, 768], P('dp', 'mp')
- grad_hidden: float32 [8, 2048, 768], P('dp', 'mp')
- grad_norm1_gain: float32 [768], replicated
- grad_norm1_shift: float32 [768], replicated
- grad_w_query: float32 [768, 768], replicated
- grad_bias_query: float32 [768], replicated
- grad_w_key: float32 [768, 768], replicated
- grad_w_value: float32 [768, 768], replicated
- grad_bias_value: float32 [768], replicated
- grad_w_attn_out: float32 [768, 768], replicated
- grad_bias_attn_out: float32 [768], replicated
- grad_norm2_gain: float32 [768], replicated
- grad_norm2_shift: float32 [768], replicated
- grad_w_mlp_in: float32 [768, 3072], P(None, 'mp')
- grad_bias_mlp_in: float32 [3072], P('mp')
- grad_w_mlp_out: float32 [3072, 768], P('mp')
- grad_bias_mlp_out: float32 [768], replicated
The draws below stay inside these ranges and needn't reach their ends.
All inputs are finite; a program needn't handle non-finite values. No bound on the sum of `reset_flags` on one device may be relied on, other than what follows from the above.
Results may differ from the reference program's by a relative error of at most 0.014.
Values may be sent and summed in bfloat16 or wider, within the bound.
No kernel may reach another device: no remote copies, remote signals or barrier semaphores. Data moves between devices by JAX's collectives and lax.ppermute only.
A program may use at most 192 MiB of HBM per device.

```python
import math
import jax
import jax.numpy as jnp
from jax import lax

D = 768
HEADS = 12
HD = 64
FF = 3072
NB = 512
SEG = 512
SAMPLES = 512
SEQ_LEN = 2048
SEGS_ALL = 4
SEQS = 8


def place_ends(array, key, smallest, high):
    shape = array.shape
    spot = [jax.random.randint(jax.random.fold_in(key, axis), (), 0, shape[axis]) for axis in range(len(shape))]
    array = array.at[tuple(spot)].set(smallest)
    longest = shape.index(max(shape))
    spot[longest] = (spot[longest] + 1) % shape[longest]
    return array.at[tuple(spot)].set(high)


def block_scale(key, extent, split, low, high):
    factor_of, own = 1.0, jax.random.fold_in(key, 6)
    for position, parts in split:
        heights = jnp.exp(jax.random.uniform(jax.random.fold_in(own, position), (parts,), jnp.float32, low / len(split), high / len(split)))
        factor_of = factor_of * jnp.repeat(heights, extent[position] // parts).reshape([-1 if axis == position else 1 for axis in range(len(extent))])
    return factor_of


def centred(own_key, dims, width, most, split=(), kind=jnp.bfloat16):
    loudness = block_scale(own_key, dims, split, -0.22, 0.18) if split else 1.0
    array = jax.random.normal(own_key, dims, jnp.float32) * width * loudness
    return jnp.minimum(jnp.maximum(array, -most), most).astype(kind)


def setup_inputs(seed: int = 0) -> dict:
    splits = jax.random.split(jax.random.key(seed), 21)
    hidden = centred(splits[0], (SEQS, SEQ_LEN, D), 1.0, 6.0, ((0, 8), (1, 4)))
    past_states = centred(splits[1], (SEQS, SEG, D), 1.0, 6.0, ((0, 8),))
    reset_flags = place_ends((jax.random.randint(splits[2], (SEQS,), 0, 2) < 1).astype(jnp.int32), jax.random.fold_in(splits[2], 1), 0, 1)
    sample_positions = place_ends(jax.random.randint(splits[3], (SEQS, SEGS_ALL, SAMPLES), 0, SEG), jax.random.fold_in(splits[3], 1), 0, SEG - 1).astype(jnp.int32)
    norm1_gain = jnp.clip(1.0 + 0.15 * jax.random.normal(splits[4], (D,), jnp.float32), 0.25, 1.75)
    norm1_shift = centred(splits[5], (D,), 0.3, 1.75, (), jnp.float32)
    w_query = centred(splits[6], (D, D), D ** -0.5, 0.21875)
    bias_query = centred(splits[7], (D,), 0.3, 1.75, (), jnp.float32)
    w_key = centred(splits[8], (D, D), D ** -0.5, 0.21875)
    w_value = centred(splits[9], (D, D), D ** -0.5, 0.21875)
    bias_value = centred(splits[10], (D,), 0.1, 0.625, (), jnp.float32)
    w_attn_out = centred(splits[11], (D, D), (max(D // 64, 1)) ** -0.5, 1.75)
    bias_attn_out = centred(splits[12], (D,), 0.3, 1.75, (), jnp.float32)
    norm2_gain = jnp.clip(1.0 + 0.15 * jax.random.normal(splits[13], (D,), jnp.float32), 0.25, 1.75)
    norm2_shift = centred(splits[14], (D,), 0.3, 1.75, (), jnp.float32)
    w_mlp_in = centred(splits[15], (D, FF), D ** -0.5, 0.21875, ((1, 4),))
    bias_mlp_in = centred(splits[16], (FF,), 0.3, 1.75, ((0, 4),), jnp.float32)
    w_mlp_out = centred(splits[17], (FF, D), FF ** -0.5, 0.109375, ((0, 4),))
    bias_mlp_out = centred(splits[18], (D,), 0.3, 1.75, (), jnp.float32)
    cotangent = centred(splits[19], (SEQS, SEQ_LEN, D), 1.0, 6.0, ((0, 8), (1, 4)))
    return dict(hidden=hidden, past_states=past_states, reset_flags=reset_flags, sample_positions=sample_positions, norm1_gain=norm1_gain, norm1_shift=norm1_shift, w_query=w_query, bias_query=bias_query, w_key=w_key, w_value=w_value, bias_value=bias_value, w_attn_out=w_attn_out, bias_attn_out=bias_attn_out, norm2_gain=norm2_gain, norm2_shift=norm2_shift, w_mlp_in=w_mlp_in, bias_mlp_in=bias_mlp_in, w_mlp_out=w_mlp_out, bias_mlp_out=bias_mlp_out, cotangent=cotangent)


PRECISION_TOP = lax.Precision.HIGHEST
NORM_EPSILON = 1e-05
RIDGE_WEIGHT = 0.1

@jax.custom_vjp
def cast_lower(v):
    return lax.optimization_barrier(v.astype(jnp.bfloat16)).astype(jnp.float32)

@jax.custom_vjp
def cast_lower_backward(v):
    return v

def low_keep(v):
    return (cast_lower(v), None)

def low_pass(kept, grad):
    return (grad,)

def back_keep(v):
    return (v, None)

def back_low(kept, grad):
    return (cast_lower(grad),)
cast_lower.defvjp(low_keep, low_pass)
cast_lower_backward.defvjp(back_keep, back_low)

def layer_norm(values, weight_gain, bias_shift):
    row_mean = lax.optimization_barrier(jnp.mean(values, axis=-1, keepdims=True))
    centered = values - row_mean
    row_var = lax.optimization_barrier(jnp.mean(centered * centered, axis=-1, keepdims=True))
    return centered * lax.rsqrt(row_var + NORM_EPSILON) * weight_gain + bias_shift

def fit_table(positions, seg_len, basis):
    spread = 1.0 / basis
    centers = (jnp.arange(basis, dtype=jnp.float32) + 0.5) / basis
    grid_times = (jnp.arange(seg_len, dtype=jnp.float32) + 0.5) / seg_len
    design = jnp.exp(-jnp.square(grid_times[:, None] - centers[None, :]) / (2.0 * spread * spread))
    gram_matrix = jnp.dot(design.T, design, precision=PRECISION_TOP) + RIDGE_WEIGHT * jnp.eye(basis, dtype=jnp.float32)
    factor = jnp.linalg.cholesky(gram_matrix)
    halfway = lax.linalg.triangular_solve(factor, design.T, left_side=True, lower=True)
    solved = lax.linalg.triangular_solve(factor, halfway, left_side=True, lower=True, transpose_a=True)
    sample_time = (positions.astype(jnp.float32) + 0.5) / seg_len
    sampled = jnp.exp(-jnp.square(sample_time[..., None] - centers) / (2.0 * spread * spread))
    return jnp.einsum('smb,bl->sml', sampled, solved, precision=PRECISION_TOP)

def matmul(left, right):
    return jnp.dot(left, right, precision=PRECISION_TOP)

def attend(block):
    query_block, key_block, value_block = block
    score_scale = 1.0 / math.sqrt(HD)
    scores = cast_lower_backward(jnp.einsum('qhd,khd->hqk', query_block, key_block, precision=PRECISION_TOP) * score_scale)
    row_index = lax.broadcasted_iota(jnp.int32, (SEG, SEG + SAMPLES), 0)
    col_index = lax.broadcasted_iota(jnp.int32, (SEG, SEG + SAMPLES), 1)
    blocked = (col_index > row_index) & (col_index < SEG)
    scores = jnp.where(blocked[None], -1e+30, scores)
    weights = cast_lower(jax.nn.softmax(scores, axis=-1))
    return cast_lower(cast_lower_backward(jnp.einsum('hqk,khd->qhd', weights, value_block, precision=PRECISION_TOP)))

def run_layer(hidden_rows, block_parameters, earlier, positions):
    norm1_gain, norm1_shift, w_query, bias_query, w_key, w_value, bias_value, w_attn_out, bias_attn_out, norm2_gain, norm2_shift, w_mlp_in, bias_mlp_in, w_mlp_out, bias_mlp_out = block_parameters
    ridge_fit_rows = cast_lower(fit_table(positions, SEG, NB))
    normed_low = cast_lower(layer_norm(hidden_rows, norm1_gain, norm1_shift))
    segments = normed_low.reshape(SEGS_ALL, SEG, D)
    memory_coefficients = jnp.concatenate([earlier[None], cast_lower_backward(segments[:SEGS_ALL - 1])], axis=0)
    memory_readout = cast_lower(cast_lower_backward(jnp.einsum('yaw,ywg->yag', ridge_fit_rows, memory_coefficients, precision=PRECISION_TOP)))
    recalled_rows = memory_readout.reshape(SEGS_ALL * SAMPLES, D)
    query = cast_lower(cast_lower_backward(matmul(normed_low, w_query) + bias_query))
    key_local = cast_lower(cast_lower_backward(matmul(normed_low, w_key)))
    value_local = cast_lower(cast_lower_backward(matmul(normed_low, w_value) + bias_value))
    key_memory = cast_lower(cast_lower_backward(matmul(recalled_rows, w_key)))
    value_memory = cast_lower(cast_lower_backward(matmul(recalled_rows, w_value) + bias_value))
    queries = query.reshape(SEGS_ALL, SEG, HEADS, HD)
    keys = jnp.concatenate([key_local.reshape(SEGS_ALL, SEG, HEADS, HD), key_memory.reshape(SEGS_ALL, SAMPLES, HEADS, HD)], axis=1)
    values = jnp.concatenate([value_local.reshape(SEGS_ALL, SEG, HEADS, HD), value_memory.reshape(SEGS_ALL, SAMPLES, HEADS, HD)], axis=1)
    mixed = lax.map(jax.checkpoint(attend), (queries, keys, values))
    attn = cast_lower_backward(matmul(mixed.reshape(SEQ_LEN, D), w_attn_out) + bias_attn_out)
    resid = hidden_rows + attn
    normed2 = cast_lower(layer_norm(resid, norm2_gain, norm2_shift))
    preact = cast_lower_backward(matmul(normed2, w_mlp_in) + bias_mlp_in)
    activated = cast_lower(jax.nn.gelu(preact, approximate=True))
    return resid + matmul(activated, w_mlp_out) + bias_mlp_out

def reference(hidden, past_states, reset_flags, sample_positions, norm1_gain, norm1_shift, w_query, bias_query, w_key, w_value, bias_value, w_attn_out, bias_attn_out, norm2_gain, norm2_shift, w_mlp_in, bias_mlp_in, w_mlp_out, bias_mlp_out, cotangent):
    block_parameters = tuple((p.astype(jnp.float32) for p in (norm1_gain, norm1_shift, w_query, bias_query, w_key, w_value, bias_value, w_attn_out, bias_attn_out, norm2_gain, norm2_shift, w_mlp_in, bias_mlp_in, w_mlp_out, bias_mlp_out)))

    def per_sequence(running, sequence):
        hidden_rows, past_rows, flag, positions, grad_rows = sequence
        earlier = past_rows.astype(jnp.float32) * (1 - flag).astype(jnp.float32)

        def layer_only(rows_in, params_in):
            return run_layer(rows_in, params_in, earlier, positions)
        result, pullback = jax.vjp(layer_only, hidden_rows.astype(jnp.float32), block_parameters)
        grad_input, grad_params = pullback(grad_rows.astype(jnp.float32))
        running = jax.tree.map(jnp.add, running, grad_params)
        return (running, (result.astype(jnp.bfloat16), grad_input))
    initial = jax.tree.map(jnp.zeros_like, block_parameters)
    totals, (output, grad_hidden) = lax.scan(per_sequence, initial, (hidden, past_states, reset_flags, sample_positions, cotangent))
    return (output, grad_hidden, totals[0], totals[1], totals[2], totals[3], totals[4], totals[5], totals[6], totals[7], totals[8], totals[9], totals[10], totals[11], totals[12], totals[13], totals[14])
```

```python
import math

import jax
import jax.numpy as jnp
from jax import lax
from jax.experimental import pallas as pl
from jax.experimental.pallas import tpu as pltpu
from jax.sharding import PartitionSpec as P

HD = 64
NORM_EPSILON = 1e-05
RIDGE_WEIGHT = 0.1
NOTHING = -1e30
GELU_SLOPE = math.sqrt(2.0 / math.pi)
GELU_CUBE = 0.044715
F32 = jnp.float32
BF16 = jnp.bfloat16
MEBI = 1 << 20


def mm(left, right):
    return jnp.dot(left, right, preferred_element_type=F32)


def mt(left, right):
    return lax.dot_general(left, right, (((1,), (1,)), ((), ())), preferred_element_type=F32)


def tm(left, right):
    return lax.dot_general(left, right, (((0,), (0,)), ((), ())), preferred_element_type=F32)


def column_sum(values):
    return jnp.sum(values, axis=0, keepdims=True)


def normalized(values):
    row_mean = jnp.mean(values, axis=-1, keepdims=True)
    centered = values - row_mean
    row_var = jnp.mean(centered * centered, axis=-1, keepdims=True)
    inverse = lax.rsqrt(row_var + NORM_EPSILON)
    return centered * inverse, inverse


def norm_back(xhat, inverse, incoming, gain):
    g = incoming * gain
    mean_g = jnp.mean(g, axis=-1, keepdims=True)
    mean_gx = jnp.mean(g * xhat, axis=-1, keepdims=True)
    return inverse * (g - mean_g - xhat * mean_gx)


def kernel_call(body, outs, name, grid=None, in_specs=None, out_specs=None, scratch=(), limit=32, flops=0, nbytes=0):
    options = dict(
        out_shape=[jax.ShapeDtypeStruct(shape, dtype) for shape, dtype in outs],
        compiler_params=pltpu.CompilerParams(vmem_limit_bytes=limit * MEBI),
        scratch_shapes=list(scratch),
        name=name,
        cost_estimate=pl.CostEstimate(flops=int(flops), bytes_accessed=int(nbytes), transcendentals=0),
    )
    if grid is not None:
        options.update(grid=grid, in_specs=in_specs, out_specs=out_specs)
    return pl.pallas_call(body, **options)


def fit_kernel(size, fit_ref):
    half = size // 2
    spread = 1.0 / size
    row = lax.broadcasted_iota(jnp.int32, (half, half), 0)
    col = lax.broadcasted_iota(jnp.int32, (half, half), 1)
    eye = jnp.where(row == col, 1.0, 0.0).astype(F32)
    flip = jnp.where(row + col == half - 1, 1.0, 0.0).astype(BF16)

    def design(columns):
        apart = (row.astype(F32) + 0.5) / size - (columns.astype(F32) + 0.5) / size
        return jnp.exp(-(apart * apart) / (2.0 * spread * spread))

    def exact(left, right):
        return jnp.dot(left, right, precision=lax.Precision.HIGHEST, preferred_element_type=F32)

    direct, mirrored = design(col), design(size - 1 - col)
    brackets, guesses = [], []
    for part in (direct + mirrored, direct - mirrored):
        brackets.append(exact(part, part) + RIDGE_WEIGHT * eye)
        guesses.append(eye * (2.0 / 6.5))
    for step in range(9):
        for which in range(2):
            bracket, guess = brackets[which], guesses[which]
            if step < 7:
                low = guess.astype(BF16)
                left = 2.0 * eye - mm(bracket.astype(BF16), low)
                guesses[which] = mm(low, left.astype(BF16))
            else:
                guesses[which] = exact(guess, 2.0 * eye - exact(bracket, guess))
    even, odd = (eye - RIDGE_WEIGHT * guess for guess in guesses)
    inner = (0.5 * (even + odd)).astype(BF16)
    outer = (0.5 * (even - odd)).astype(BF16)
    fit_ref[0:half, 0:half] = inner
    fit_ref[0:half, half:size] = mm(outer, flip).astype(BF16)
    fit_ref[half:size, 0:half] = mm(flip, outer).astype(BF16)
    fit_ref[half:size, half:size] = mm(flip, mm(inner, flip).astype(BF16)).astype(BF16)


def front_kernel(hidden, gain, shift, wq, bq, wk, wv, bv, normed, q, k, v):
    xhat, _ = normalized(hidden[...].astype(F32))
    low = (xhat * gain[...] + shift[...]).astype(BF16)
    normed[...] = low
    scale = 1.0 / math.sqrt(HD)
    q[...] = (mm(low, wq[...]) + bq[...]).astype(BF16) * jnp.asarray(scale, BF16)
    k[...] = mm(low, wk[...]).astype(BF16)
    v[...] = (mm(low, wv[...]) + bv[...]).astype(BF16)


def memory_kernel(arrived, past, keep, first, positions, gain, shift, fit, wk, wv, bv, recalled, km, vm, often):
    size = fit.shape[0]
    xhat, _ = normalized(arrived[...].astype(F32))
    before = xhat * gain[...] + shift[...]
    kept = past[...].astype(F32) * keep[0, 0]
    earlier = jnp.where(first[0, 0] > 0, kept, before).astype(BF16)
    low = mm(fit[...], earlier).astype(BF16)
    recalled[...] = low
    km[...] = mm(low, wk[...]).astype(BF16)
    vm[...] = (mm(low, wv[...]) + bv[...]).astype(BF16)
    place = lax.broadcasted_iota(jnp.int32, (size, positions.shape[1]), 0)
    hit = jnp.where(place == positions[...], 1.0, 0.0).astype(BF16)
    count = mt(jnp.ones((8, positions.shape[1]), BF16), hit)
    often[...] = jnp.where(count > 0.5, jnp.log(jnp.maximum(count, 1.0)), NOTHING)


def attend_kernel(q, k, v, km, vm, often, wo, bo, hidden, gain, shift, e, mixed, linv, resid, normed2):
    pair = pl.program_id(0)
    rows = q.shape[0]
    half = rows // 2
    lane = lax.broadcasted_iota(jnp.int32, (1, 2 * HD), 1)
    row = lax.broadcasted_iota(jnp.int32, (half, half), 0)
    col = lax.broadcasted_iota(jnp.int32, (half, half), 1)
    log_count = often[0:1, :]
    at = pl.ds(pl.multiple_of(pair * 2 * HD, 2 * HD), 2 * HD)
    for part in range(2):
        here = slice(part * half, (part + 1) * half)
        seen = (part + 1) * half
        results = []
        for head in range(2):
            mine = (lane >= head * HD) & (lane < (head + 1) * HD)
            query = jnp.where(mine, q[here, :], jnp.zeros((), BF16))
            near = mt(query, k[0:seen, :])
            edge = jnp.where(col > row, NOTHING, near[:, part * half :])
            far = mt(query, km[...]) + log_count
            top = jnp.maximum(jnp.max(edge, axis=-1, keepdims=True), jnp.max(far, axis=-1, keepdims=True))
            if part:
                top = jnp.maximum(top, jnp.max(near[:, : part * half], axis=-1, keepdims=True))
            edge = jnp.exp(edge - top)
            far = jnp.exp(far - top)
            total = jnp.sum(edge, axis=-1, keepdims=True) + jnp.sum(far, axis=-1, keepdims=True)
            edge_low, far_low = edge.astype(BF16), far.astype(BF16)
            e[head, here, part * half : seen] = edge_low
            e[head, here, rows:] = far_low
            out = mm(edge_low, v[part * half : seen, :]) + mm(far_low, vm[...])
            if part:
                start = jnp.exp(near[:, : part * half] - top)
                total = total + jnp.sum(start, axis=-1, keepdims=True)
                start_low = start.astype(BF16)
                e[head, here, 0 : part * half] = start_low
                out = out + mm(start_low, v[0 : part * half, :])
            inverse = 1.0 / total
            results.append((out * inverse, inverse))
        first = lane < HD
        mixed[here, at] = jnp.where(first, results[0][0], results[1][0]).astype(BF16)
        linv[here, at] = jnp.where(first, results[0][1], results[1][1])

    @pl.when(pair == pl.num_programs(0) - 1)
    def _():
        total = hidden[...].astype(F32) + mm(mixed[...], wo[...]) + bo[...]
        resid[...] = total
        xhat, _ = normalized(total)
        normed2[...] = (xhat * gain[...] + shift[...]).astype(BF16)


def mlp_kernel(x, cot, w_in, b_in, w_out, out, gx, gw_in, gw_out, gb_in):
    step = pl.program_id(0)

    @pl.when(step == 0)
    def _():
        gw_in[...] = jnp.zeros_like(gw_in)
        gw_out[...] = jnp.zeros_like(gw_out)
        gb_in[...] = jnp.zeros_like(gb_in)

    pre = mm(x[...], w_in[...]) + b_in[...]
    square = pre * pre
    bend = jnp.tanh(GELU_SLOPE * pre * (1.0 + GELU_CUBE * square))
    act = (0.5 * pre * (1.0 + bend)).astype(BF16)
    slope = 0.5 * (1.0 + bend) + (0.5 * GELU_SLOPE) * pre * (1.0 - bend * bend) * (1.0 + 3.0 * GELU_CUBE * square)
    gpre_full = mt(cot[...], w_out[...]) * slope
    gpre = gpre_full.astype(BF16)
    out[...] = mm(act, w_out[...]).astype(BF16)
    gx[...] = mt(gpre, w_in[...]).astype(BF16)
    gw_in[...] += tm(x[...], gpre)
    gw_out[...] += tm(act, cot[...])
    gb_in[...] += column_sum(gpre.astype(F32))


def middle_kernel(gx, resid, cot, gain, mixed, wo, grad_resid, grad_mixed, gwo, vecs):
    xhat, inverse = normalized(resid[...])
    n = gx[...].astype(F32)
    cot_full = cot[...].astype(F32)
    total = cot_full + norm_back(xhat, inverse, n, gain[...])
    grad_resid[...] = total
    low = total.astype(BF16)
    grad_mixed[...] = mt(low, wo[...]).astype(BF16)
    gwo[...] = tm(mixed[...], low)
    vecs[...] = jnp.concatenate(
        [
            column_sum(low.astype(F32)),
            column_sum(n * xhat),
            column_sum(n),
            column_sum(cot_full),
            jnp.zeros((4, n.shape[1]), F32),
        ],
        axis=0,
    )


def attend_back_kernel(q, k, v, km, vm, e, linv, mixed, gmix, dq, dk, dv, dkm, dvm):
    rows = q.shape[0]
    half = rows // 2
    lane = lax.broadcasted_iota(jnp.int32, (1, 2 * HD), 1)
    scale = 1.0 / math.sqrt(HD)
    sums = {}

    def add(name, value):
        sums[name] = sums[name] + value if name in sums else value

    for part in range(2):
        here = slice(part * half, (part + 1) * half)
        seen = (part + 1) * half
        grad = gmix[here, :].astype(F32) * linv[here, :]
        product = grad * mixed[here, :].astype(F32)
        queries = []
        for head in range(2):
            mine = (lane >= head * HD) & (lane < (head + 1) * HD)
            query = jnp.where(mine, q[here, :], jnp.zeros((), BF16))
            grad_low = jnp.where(mine, grad, 0.0).astype(BF16)
            dot = jnp.sum(jnp.where(mine, product, 0.0), axis=-1, keepdims=True)
            near_e, far_e = e[head, here, 0:seen], e[head, here, rows:]
            near = (near_e.astype(F32) * (mt(grad_low, v[0:seen, :]) - dot)).astype(BF16)
            far = (far_e.astype(F32) * (mt(grad_low, vm[...]) - dot)).astype(BF16)
            queries.append(mm(near, k[0:seen, :]) + mm(far, km[...]))
            dk_near, dv_near = tm(near, query), tm(near_e, grad_low)
            for block in range(part + 1):
                where = slice(block * half, (block + 1) * half)
                add(("k", block), dk_near[where])
                add(("v", block), dv_near[where])
            add("km", tm(far, query))
            add("vm", tm(far_e, grad_low))
        dq[here, :] = (jnp.where(lane < HD, queries[0], queries[1]) * scale).astype(BF16)
    for block in range(2):
        where = slice(block * half, (block + 1) * half)
        dk[where, :] = sums["k", block].astype(BF16)
        dv[where, :] = sums["v", block].astype(BF16)
    dkm[...] = sums["km"].astype(BF16)
    dvm[...] = sums["vm"].astype(BF16)


def recall_back_kernel(dkm, dvm, wk, wv, fit, arrived, first, grad_memory, vecs):
    grad_recalled = (mt(dkm[...], wk[...]) + mt(dvm[...], wv[...])).astype(BF16)
    handed = tm(fit[...], grad_recalled).astype(BF16)
    grad_memory[...] = handed
    xhat, _ = normalized(arrived[...].astype(F32))
    n = jnp.where(first[0, 0] > 0, 0.0, handed.astype(F32))
    vecs[...] = jnp.concatenate([column_sum(n * xhat), column_sum(n), jnp.zeros((6, n.shape[1]), F32)], axis=0)


def project_back_kernel(hidden, normed, recalled, dq, dk, dv, dkm, dvm, wq, wk, wv, gwq, gwk, gwv, gn, vecs):
    low, rec = normed[...], recalled[...]
    gwq[...] = tm(low, dq[...])
    gwk[...] = tm(low, dk[...]) + tm(rec, dkm[...])
    gwv[...] = tm(low, dv[...]) + tm(rec, dvm[...])
    n = mt(dq[...], wq[...]) + mt(dk[...], wk[...]) + mt(dv[...], wv[...])
    gn[...] = n
    xhat, _ = normalized(hidden[...].astype(F32))
    vecs[...] = jnp.concatenate(
        [
            column_sum(n * xhat),
            column_sum(n),
            column_sum(dq[...].astype(F32)),
            column_sum(dv[...].astype(F32)) + column_sum(dvm[...].astype(F32)),
            jnp.zeros((4, n.shape[1]), F32),
        ],
        axis=0,
    )


def last_kernel(hidden, gain, gn, handed, grad_resid, grad_hidden):
    xhat, inverse = normalized(hidden[...].astype(F32))
    n = gn[...] + handed[...].astype(F32)
    grad_hidden[...] = grad_resid[...] + norm_back(xhat, inverse, n, gain[...])


def from_behind(value, axis, steps):
    count = lax.axis_size(axis)
    leading, last = (max(0, -steps), min(count, count - steps))
    return lax.ppermute(value, axis, [(source, source + steps) for source in range(leading, last)])


def local(
    hidden,
    past_states,
    reset_flags,
    sample_positions,
    norm1_gain,
    norm1_shift,
    w_query,
    bias_query,
    w_key,
    w_value,
    bias_value,
    w_attn_out,
    bias_attn_out,
    norm2_gain,
    norm2_shift,
    w_mlp_in,
    bias_mlp_in,
    w_mlp_out,
    bias_mlp_out,
    cotangent,
):
    rows, width = hidden.shape[1], hidden.shape[2]
    size = past_states.shape[1]
    units = w_mlp_in.shape[1]
    assert rows == size and sample_positions.shape[2] == size
    pairs = width // (2 * HD)
    arr, cot = hidden[0], cotangent[0]
    gain1, shift1, gain2, shift2, b_q, b_v, b_o, b_in, b_out = (
        vector[None]
        for vector in (
            norm1_gain,
            norm1_shift,
            norm2_gain,
            norm2_shift,
            bias_query,
            bias_value,
            bias_attn_out,
            bias_mlp_in,
            bias_mlp_out,
        )
    )
    row_bf, row_f = ((rows, width), BF16), ((rows, width), F32)
    square_f, vec_f = ((width, width), F32), ((8, width), F32)

    arrived = from_behind(arr, "mp", 1)
    cot_all = lax.all_gather(cot, "mp", axis=0, tiled=True)
    first = (lax.axis_index("mp") == 0).astype(jnp.int32).reshape(1, 1)
    keep = (1 - reset_flags).astype(F32).reshape(1, 1)

    unit = 2 * rows * width * width
    (fit,) = kernel_call(lambda ref: fit_kernel(size, ref), [((size, size), BF16)], "fit", flops=20e9)()
    normed, q, k, v = kernel_call(front_kernel, [row_bf] * 4, "front", flops=3 * unit)(
        arr, gain1, shift1, w_query, b_q, w_key, w_value, b_v
    )
    recalled, km, vm, often = kernel_call(memory_kernel, [row_bf] * 3 + [((8, size), F32)], "memory", flops=3 * unit)(
        arrived, past_states[0], keep, first, sample_positions[0], gain1, shift1, fit, w_key, w_value, b_v
    )

    whole = lambda shape: pl.BlockSpec(shape, lambda i: (0,) * len(shape))
    column = pl.BlockSpec((rows, 2 * HD), lambda i: (0, i))
    e_block = pl.BlockSpec((2, rows, rows + size), lambda i: (i, 0, 0))
    vec1 = whole((1, width))
    e, mixed, linv, resid, normed2 = kernel_call(
        attend_kernel,
        [((2 * pairs, rows, rows + size), BF16), row_bf, row_f, row_f, row_bf],
        "attend",
        grid=(pairs,),
        in_specs=[column] * 5
        + [whole((8, size)), whole((width, width)), vec1, whole((rows, width)), vec1, vec1],
        out_specs=[e_block] + [whole((rows, width))] * 4,
        flops=12 * unit,
    )(q, k, v, km, vm, often, w_attn_out, b_o, arr, gain2, shift2)

    gathered = lax.all_gather(normed2, "mp", axis=0, tiled=True)
    blocks = gathered.shape[0] // rows
    block = pl.BlockSpec((rows, width), lambda i: (i, 0))
    all_rows = ((gathered.shape[0], width), BF16)
    out_part, gx_part, gw_in, gw_out, gb_in = kernel_call(
        mlp_kernel,
        [all_rows, all_rows, ((width, units), F32), ((units, width), F32), ((1, units), F32)],
        "mlp",
        grid=(blocks,),
        in_specs=[block, block, whole((width, units)), whole((1, units)), whole((units, width))],
        out_specs=[block, block, whole((width, units)), whole((units, width)), whole((1, units))],
        limit=48,
        flops=24 * unit,
    )(gathered, cot_all, w_mlp_in, b_in, w_mlp_out)

    gx = lax.psum_scatter(gx_part, "mp", scatter_dimension=0, tiled=True)
    mlp_rows = lax.psum_scatter(out_part, "mp", scatter_dimension=0, tiled=True)
    output = (resid + mlp_rows.astype(F32) + b_out).astype(BF16)[None]

    grad_resid, grad_mixed, gwo, vecs_mid = kernel_call(
        middle_kernel, [row_f, row_bf, square_f, vec_f], "middle", flops=2 * unit
    )(gx, resid, cot, gain2, mixed, w_attn_out)
    dq, dk, dv, dkm, dvm = kernel_call(
        attend_back_kernel,
        [row_bf] * 5,
        "attend_back",
        grid=(pairs,),
        in_specs=[column] * 5 + [e_block] + [column] * 3,
        out_specs=[column] * 5,
        flops=24 * unit,
    )(q, k, v, km, vm, e, linv, mixed, grad_mixed)
    grad_memory, vecs_rec = kernel_call(recall_back_kernel, [row_bf, vec_f], "recall_back", flops=3 * unit)(
        dkm, dvm, w_key, w_value, fit, arrived, first
    )
    handed = from_behind(grad_memory, "mp", -1)
    gwq, gwk, gwv, gn, vecs_proj = kernel_call(
        project_back_kernel, [square_f] * 3 + [row_f, vec_f], "project_back", limit=40, flops=8 * unit
    )(arr, normed, recalled, dq, dk, dv, dkm, dvm, w_query, w_key, w_value)
    (grad_hidden,) = kernel_call(last_kernel, [row_f], "last")(arr, gain1, gn, handed, grad_resid)

    gw_in, gw_out = (t.astype(BF16) for t in (gw_in, gw_out))
    gw_in, gw_out, gb_in = lax.psum((gw_in, gw_out, gb_in), "dp")
    squares = lax.psum(tuple(t.astype(BF16) for t in (gwq, gwk, gwv, gwo)), ("dp", "mp"))
    gwq, gwk, gwv, gwo = (t.astype(F32) for t in squares)
    vecs = jnp.concatenate([vecs_proj[:2] + vecs_rec[:2], vecs_proj[2:4], vecs_mid[:4]], axis=0)
    vecs = lax.psum(vecs, ("dp", "mp"))
    return (
        output,
        grad_hidden[None],
        vecs[0],
        vecs[1],
        gwq,
        vecs[2],
        gwk,
        gwv,
        vecs[3],
        gwo,
        vecs[4],
        vecs[5],
        vecs[6],
        gw_in.astype(F32),
        gb_in[0],
        gw_out.astype(F32),
        vecs[7],
    )


def solution(mesh):
    rows = P("dp", "mp", None)
    placed = (rows, P("dp", None, None), P("dp"), rows) + (P(),) * 11
    placed += (P(None, "mp"), P("mp"), P("mp", None), P(), rows)
    return jax.shard_map(
        local,
        mesh=mesh,
        in_specs=placed,
        out_specs=(rows, rows) + (P(),) * 11 + (P(None, "mp"), P("mp"), P("mp", None), P()),
        check_vma=False,
    )
```

```python
import math

import jax
import jax.numpy as jnp
from jax import lax
from jax.experimental import pallas as pl
from jax.experimental.pallas import tpu as pltpu
from jax.sharding import PartitionSpec as P

HD = 64
NORM_EPSILON = 1e-05
RIDGE_WEIGHT = 0.1
NOTHING = -1e30
GELU_SLOPE = math.sqrt(2.0 / math.pi)
GELU_CUBE = 0.044715
F32 = jnp.float32
BF16 = jnp.bfloat16
MEBI = 1 << 20


def mm(left, right):
    return jnp.dot(left, right, preferred_element_type=F32)


def mt(left, right):
    return lax.dot_general(left, right, (((1,), (1,)), ((), ())), preferred_element_type=F32)


def tm(left, right):
    return lax.dot_general(left, right, (((0,), (0,)), ((), ())), preferred_element_type=F32)


def column_sum(values):
    return jnp.sum(values, axis=0, keepdims=True)


def normalized(values):
    row_mean = jnp.mean(values, axis=-1, keepdims=True)
    centered = values - row_mean
    row_var = jnp.mean(centered * centered, axis=-1, keepdims=True)
    inverse = lax.rsqrt(row_var + NORM_EPSILON)
    return centered * inverse, inverse


def norm_back(xhat, inverse, incoming, gain):
    g = incoming * gain
    mean_g = jnp.mean(g, axis=-1, keepdims=True)
    mean_gx = jnp.mean(g * xhat, axis=-1, keepdims=True)
    return inverse * (g - mean_g - xhat * mean_gx)


SMALL = pl.BlockSpec(memory_space=pltpu.SMEM)
VMEM = pl.BlockSpec(memory_space=pltpu.VMEM)
ANY = pl.BlockSpec(memory_space=pl.ANY)
HBM = pl.BlockSpec(memory_space=pltpu.HBM)


class Arriving:
    def __init__(self, source, held, sem):
        self.held, self.copy = held, pltpu.make_async_copy(source, held, sem)
        self.shape, self.dtype = held.shape, held.dtype
        self.here = False
        self.copy.start()

    def wait(self):
        if not self.here:
            self.copy.wait()
            self.here = True
        return self.held

    @property
    def at(self):
        return self.wait().at

    def __getitem__(self, index):
        return self.wait()[index]


class Leaving:
    def __init__(self, target, held, sem):
        self.held, self.copy = held, pltpu.make_async_copy(held, target, sem)
        self.shape, self.dtype = held.shape, held.dtype
        self.gone = False

    def leave(self):
        if not self.gone:
            self.copy.start()
            self.gone = True

    def __getitem__(self, index):
        return self.held[index]

    def __setitem__(self, index, value):
        self.held[index] = value
        if index is Ellipsis:
            self.leave()


class Line:
    def __init__(self):
        self.last = None

    def start(self, body, outs, name, operands, grid, in_specs, out_specs, scratch, after=(), aliases=None, far=(), limit=32, there=()):
        waits = [w for w in list(after) + [self.last] if w is not None and not any(w is o for o in operands)]
        operands = [pltpu.with_memory_space_constraint(o, pltpu.HBM) if i in there else o for i, o in enumerate(operands)]
        known, gone = len(operands), len(operands) + len(waits)
        results = pl.pallas_call(
            lambda *refs: body(*refs[:known], *refs[gone:]),
            out_shape=[(pltpu.HBM if i in far else pltpu.VMEM)(shape, dtype) for i, (shape, dtype) in enumerate(outs)],
            grid=grid,
            in_specs=list(in_specs) + [ANY] * len(waits),
            out_specs=out_specs,
            scratch_shapes=list(scratch),
            input_output_aliases=aliases or {},
            compiler_params=pltpu.CompilerParams(vmem_limit_bytes=limit * MEBI),
            cost_estimate=pl.CostEstimate(flops=0, bytes_accessed=0, transcendentals=0),
            name=name,
        )(*operands, *waits)
        near = [result for i, result in enumerate(results) if i not in far]
        self.last = near[0] if near else pltpu.with_memory_space_constraint(results[0], pltpu.HBM)
        return results

    def blocks(self, body, outs, name, operands, grid, in_specs, out_specs, scratch=(), **more):
        return self.start(body, outs, name, operands, grid, in_specs, out_specs, scratch, **more)

    def call(self, body, outs, name, operands, small=0, direct=(), stream=(), far=(), scratch=(), after=(), limit=16):
        stream = tuple(stream) + tuple(i for i, o in enumerate(operands) if o.ndim == 1)
        in_specs = [SMALL if i < small else HBM if i in direct or i in stream else VMEM for i in range(len(operands))]
        out_specs = [HBM if i in far else VMEM for i in range(len(outs))]
        own = len(scratch)
        held = [pltpu.VMEM(operands[i].shape, operands[i].dtype) for i in stream]
        held += [pltpu.VMEM(*outs[i]) for i in far]
        sems = [pltpu.SemaphoreType.DMA((len(held),))] if held else []

        def run(*refs):
            ins, targets, rest = refs[: len(operands)], refs[len(operands) : len(operands) + len(outs)], refs[len(operands) + len(outs) :]
            mine, buffers, sem = rest[:own], rest[own:], rest[-1] if held else None
            ins, targets = list(ins), list(targets)
            for slot, i in enumerate(stream):
                ins[i] = Arriving(ins[i], buffers[slot], sem.at[slot])
            for slot, i in enumerate(far, len(stream)):
                targets[i] = Leaving(targets[i], buffers[slot], sem.at[slot])
            body(*ins, *targets, *mine)
            for i in stream:
                ins[i].wait()
            for i in far:
                targets[i].leave()
            for i in far:
                targets[i].copy.wait()

        return self.start(
            run, outs, name, operands, (1,), in_specs, out_specs, list(scratch) + held + sems, after, far=far, limit=limit,
            there=tuple(stream) + tuple(direct),
        )


def hold(value, *until):
    return lax.optimization_barrier((value,) + until)[0]


def at_half(bit, count):
    return pl.ds(pl.multiple_of(bit * count, count), count)


def fit_kernel(size, info, w_in, w_out, fit_ref, cut_in, cut_out, sems):
    count = cut_in.shape[0]
    copies = [
        pltpu.make_async_copy(weight.at[at_half(scalar(info, slot), count), :], cut.held, sems.at[which])
        for which, (slot, weight, cut) in enumerate((("cut_in", w_in, cut_in), ("cut_out", w_out, cut_out)))
    ]
    for copy in copies:
        copy.start()
    half = size // 2
    spread = 1.0 / size
    row = lax.broadcasted_iota(jnp.int32, (half, half), 0)
    col = lax.broadcasted_iota(jnp.int32, (half, half), 1)
    eye = jnp.where(row == col, 1.0, 0.0).astype(F32)
    flip = jnp.where(row + col == half - 1, 1.0, 0.0).astype(BF16)

    def design(columns):
        apart = (row.astype(F32) + 0.5) / size - (columns.astype(F32) + 0.5) / size
        return jnp.exp(-(apart * apart) / (2.0 * spread * spread))

    def exact(left, right):
        return jnp.dot(left, right, precision=lax.Precision.HIGHEST, preferred_element_type=F32)

    direct, mirrored = design(col), design(size - 1 - col)
    brackets, guesses = [], []
    for part in (direct + mirrored, direct - mirrored):
        brackets.append(exact(part, part) + RIDGE_WEIGHT * eye)
        guesses.append(eye * (2.0 / 6.5))
    for step in range(9):
        for which in range(2):
            bracket, guess = brackets[which], guesses[which]
            if step < 7:
                low = guess.astype(BF16)
                left = 2.0 * eye - mm(bracket.astype(BF16), low)
                guesses[which] = mm(low, left.astype(BF16))
            else:
                guesses[which] = exact(guess, 2.0 * eye - exact(bracket, guess))
    even, odd = (eye - RIDGE_WEIGHT * guess for guess in guesses)
    inner = (0.5 * (even + odd)).astype(BF16)
    outer = (0.5 * (even - odd)).astype(BF16)
    fit_ref[0:half, 0:half] = inner
    fit_ref[0:half, half:size] = mm(outer, flip).astype(BF16)
    fit_ref[half:size, 0:half] = mm(flip, outer).astype(BF16)
    fit_ref[half:size, half:size] = mm(flip, mm(inner, flip).astype(BF16)).astype(BF16)
    for copy in copies:
        copy.wait()
    cut_in.leave()
    cut_out.leave()


def front_kernel(hidden, gain, shift, wq, bq, wk, wv, bv, normed, q, k, v):
    xhat, _ = normalized(hidden[...].astype(F32))
    low = (xhat * gain[...] + shift[...]).astype(BF16)
    normed[...] = low
    scale = 1.0 / math.sqrt(HD)
    q[...] = (mm(low, wq[...]) + bq[...]).astype(BF16) * jnp.asarray(scale, BF16)
    k[...] = mm(low, wk[...]).astype(BF16)
    v[...] = (mm(low, wv[...]) + bv[...]).astype(BF16)


def memory_kernel(info, arrived, past, positions, gain, shift, fit, wk, wv, bv, recalled, km, vm, often):
    size = fit.shape[0]
    xhat, _ = normalized(arrived[...].astype(F32))
    before = xhat * gain[...] + shift[...]
    kept = past[...].astype(F32) * (1 - scalar(info, "reset")).astype(F32)
    earlier = jnp.where(scalar(info, "first") > 0, kept, before).astype(BF16)
    low = mm(fit[...], earlier).astype(BF16)
    recalled[...] = low
    km[...] = mm(low, wk[...]).astype(BF16)
    vm[...] = (mm(low, wv[...]) + bv[...]).astype(BF16)
    place = lax.broadcasted_iota(jnp.int32, (size, positions.shape[1]), 0)
    hit = jnp.where(place == positions[...], 1.0, 0.0).astype(BF16)
    count = mt(jnp.ones((8, positions.shape[1]), BF16), hit)
    often[...] = jnp.where(count > 0.5, jnp.log(jnp.maximum(count, 1.0)), NOTHING)


def attend_pair(q, k, v, km, vm, often, e, mixed, linv):
    rows = q.shape[0]
    half = rows // 2
    lane = lax.broadcasted_iota(jnp.int32, (1, 2 * HD), 1)
    row = lax.broadcasted_iota(jnp.int32, (half, half), 0)
    col = lax.broadcasted_iota(jnp.int32, (half, half), 1)
    log_count = often[0:1, :]
    for part in range(2):
        here = slice(part * half, (part + 1) * half)
        seen = (part + 1) * half
        results = []
        for head in range(2):
            mine = (lane >= head * HD) & (lane < (head + 1) * HD)
            query = jnp.where(mine, q[here, :], jnp.zeros((), BF16))
            near = mt(query, k[0:seen, :])
            edge = jnp.where(col > row, NOTHING, near[:, part * half :])
            far = mt(query, km[...]) + log_count
            top = jnp.maximum(jnp.max(edge, axis=-1, keepdims=True), jnp.max(far, axis=-1, keepdims=True))
            if part:
                top = jnp.maximum(top, jnp.max(near[:, : part * half], axis=-1, keepdims=True))
            edge = jnp.exp(edge - top)
            far = jnp.exp(far - top)
            total = jnp.sum(edge, axis=-1, keepdims=True) + jnp.sum(far, axis=-1, keepdims=True)
            edge_low, far_low = edge.astype(BF16), far.astype(BF16)
            e[head, here, part * half : seen] = edge_low
            e[head, here, rows:] = far_low
            out = mm(edge_low, v[part * half : seen, :]) + mm(far_low, vm[...])
            if part:
                start = jnp.exp(near[:, : part * half] - top)
                total = total + jnp.sum(start, axis=-1, keepdims=True)
                start_low = start.astype(BF16)
                e[head, here, 0 : part * half] = start_low
                out = out + mm(start_low, v[0 : part * half, :])
            inverse = 1.0 / total
            results.append((out * inverse, inverse))
        first = lane < HD
        mixed[here, :] = jnp.where(first, results[0][0], results[1][0]).astype(BF16)
        linv[here, :] = jnp.where(first, results[0][1], results[1][1])


def attend_kernel(q, k, v, km, vm, often, e, mixed, linv, done):
    done[...] = jnp.zeros_like(done)
    attend_pair(q, k, v, km, vm, often, e, mixed, linv)


def attend_more_kernel(
    q, k, v, km, vm, often, e_done, mixed_done, linv_done, wo, bo, hidden, gain, shift,
    e, mixed, linv, resid, normed2, every,
):
    step = pl.program_id(0)
    attend_pair(q, k, v, km, vm, often, e, mixed, linv)
    done, block = mixed_done.shape[1], mixed.shape[1]
    every[:, pl.ds(pl.multiple_of(done + step * block, block), block)] = mixed[...]

    @pl.when(step == pl.num_programs(0) - 1)
    def _():
        every[:, 0:done] = mixed_done[...]
        total = hidden[...].astype(F32) + mm(every[...], wo[...]) + bo[...]
        resid[...] = total
        xhat, _ = normalized(total)
        normed2[...] = (xhat * gain[...] + shift[...]).astype(BF16)


def mlp_block(x, cot, w_in, b_in, w_out):
    pre = mm(x, w_in) + b_in
    square = pre * pre
    bend = jnp.tanh(GELU_SLOPE * pre * (1.0 + GELU_CUBE * square))
    act = (0.5 * pre * (1.0 + bend)).astype(BF16)
    slope = 0.5 * (1.0 + bend) + (0.5 * GELU_SLOPE) * pre * (1.0 - bend * bend) * (1.0 + 3.0 * GELU_CUBE * square)
    gpre = (mt(cot, w_out) * slope).astype(BF16)
    return mm(act, w_out), mt(gpre, w_in), act, gpre


def mlp_rows(xs, cots, w_in, b_in, w_out, acts, gpres, emit):
    rows = xs[0].shape[0]
    block = rows // 2
    for which, (x, cot) in enumerate(zip(xs, cots)):
        for start in range(0, rows, block):
            here = slice(start, start + block)
            o, g, act, gpre = mlp_block(x[here, :], cot[here, :], w_in[...], b_in[...], w_out[...])
            emit(which, here, o, g)
            there = slice(which * rows + start, which * rows + start + block)
            acts[there, :] = act
            gpres[there, :] = gpre


def mlp_grads(xs, cots, acts, gpres, ga, gb, gc, g_bias):
    rows, third = xs[0].shape[0], ga.shape[0]
    cut = acts.shape[1] - third
    gw_in = (tm(xs[0][...], gpres[:rows, :]) + tm(xs[1][...], gpres[rows:, :])).astype(BF16)
    ga[...] = gw_in[:third]
    gb[0:cut, :] = gw_in[third:]
    gw_out = (tm(acts[:rows, :], cots[0][...]) + tm(acts[rows:, :], cots[1][...])).astype(BF16)
    gb[cut:, :] = gw_out[: third - cut]
    gc[...] = gw_out[third - cut :]
    g_bias[...] = column_sum(gpres[...].astype(F32))


def mlp_own_kernel(x0, x1, cot0, cot1, w_in, b_in, w_out, out, gx, ga, gb, gc, g_bias, acts, gpres):
    def emit(which, here, o, g):
        out[which, here, :], gx[which, here, :] = o.astype(BF16), g.astype(BF16)

    mlp_rows((x0, x1), (cot0, cot1), w_in, b_in, w_out, acts, gpres, emit)
    mlp_grads((x0, x1), (cot0, cot1), acts, gpres, ga, gb, gc, g_bias)


def mlp_far_kernel(
    x0, x1, cot0, cot1, w_in, b_in, w_out, out, gx, keep_gx, send_gx, keep_out, send_out, ra, rb, rc, g_bias, acts, gpres
):
    def emit(which, here, o, g):
        to_out, to_gx = ((keep_out, keep_gx), (send_out, send_gx))[which]
        to_out[here, :] = (o + out[which, here, :].astype(F32)).astype(BF16)
        to_gx[here, :] = (g + gx[which, here, :].astype(F32)).astype(BF16)

    mlp_rows((x0, x1), (cot0, cot1), w_in, b_in, w_out, acts, gpres, emit)
    mlp_grads((x0, x1), (cot0, cot1), acts, gpres, ra, rb, rc, g_bias)


def part_kernel(info, gb, gc, rb, rc, keep_b, send_b, keep_c, send_c):
    half = gb.shape[0] // 2
    for own, far, keep, send, link in ((gb, rb, keep_b, send_b, "x"), (gc, rc, keep_c, send_c, "z1")):
        mine, other = at_half(scalar(info, link), half), at_half(1 - scalar(info, link), half)
        keep[0], keep[1] = own[mine, :], far[mine, :]
        send[0], send[1] = own[other, :], far[other, :]


def middle_kernel(gx, gx_more, resid, cot, gain, mixed, wo, grad_mixed, grad_resid, gwo, vecs):
    xhat, inverse = normalized(resid[...])
    n = gx[...].astype(F32) + gx_more[...].astype(F32)
    cot_full = cot[...].astype(F32)
    total = cot_full + norm_back(xhat, inverse, n, gain[...])
    grad_resid[...] = total
    low = total.astype(BF16)
    grad_mixed[...] = mt(low, wo[...]).astype(BF16)
    gwo[...] = tm(mixed[...], low).astype(BF16)
    vecs[...] = jnp.concatenate(
        [
            column_sum(low.astype(F32)),
            column_sum(n * xhat),
            column_sum(n),
            column_sum(cot_full),
            jnp.zeros((4, n.shape[1]), F32),
        ],
        axis=0,
    )


def attend_back_kernel(q, k, v, km, vm, e, linv, mixed, gmix, *refs):
    dq, dk, dv, dkm, dvm = refs[-5:]
    rows = q.shape[0]
    half = rows // 2
    lane = lax.broadcasted_iota(jnp.int32, (1, 2 * HD), 1)
    scale = 1.0 / math.sqrt(HD)
    sums = {}

    def add(name, value):
        sums[name] = sums[name] + value if name in sums else value

    for part in range(2):
        here = slice(part * half, (part + 1) * half)
        seen = (part + 1) * half
        grad = gmix[here, :].astype(F32) * linv[here, :]
        product = grad * mixed[here, :].astype(F32)
        queries = []
        for head in range(2):
            mine = (lane >= head * HD) & (lane < (head + 1) * HD)
            query = jnp.where(mine, q[here, :], jnp.zeros((), BF16))
            grad_low = jnp.where(mine, grad, 0.0).astype(BF16)
            dot = jnp.sum(jnp.where(mine, product, 0.0), axis=-1, keepdims=True)
            near_e, far_e = e[head, here, 0:seen], e[head, here, rows:]
            near = (near_e.astype(F32) * (mt(grad_low, v[0:seen, :]) - dot)).astype(BF16)
            far = (far_e.astype(F32) * (mt(grad_low, vm[...]) - dot)).astype(BF16)
            queries.append(mm(near, k[0:seen, :]) + mm(far, km[...]))
            dk_near, dv_near = tm(near, query), tm(near_e, grad_low)
            for block in range(part + 1):
                where = slice(block * half, (block + 1) * half)
                add(("k", block), dk_near[where])
                add(("v", block), dv_near[where])
            add("km", tm(far, query))
            add("vm", tm(far_e, grad_low))
        dq[here, :] = (jnp.where(lane < HD, queries[0], queries[1]) * scale).astype(BF16)
    for block in range(2):
        where = slice(block * half, (block + 1) * half)
        dk[where, :] = sums["k", block].astype(BF16)
        dv[where, :] = sums["v", block].astype(BF16)
    dkm[...] = sums["km"].astype(BF16)
    dvm[...] = sums["vm"].astype(BF16)


def recall_back_kernel(info, dkm, dvm, wk, wv, fit, arrived, grad_memory, vecs):
    grad_recalled = (mt(dkm[...], wk[...]) + mt(dvm[...], wv[...])).astype(BF16)
    handed = tm(fit[...], grad_recalled).astype(BF16)
    grad_memory[...] = handed
    xhat, _ = normalized(arrived[...].astype(F32))
    n = jnp.where(scalar(info, "first") > 0, 0.0, handed.astype(F32))
    vecs[...] = jnp.concatenate([column_sum(n * xhat), column_sum(n), jnp.zeros((6, n.shape[1]), F32)], axis=0)


def weight_grads_kernel(info, normed, recalled, dq, dk, dv, dkm, dvm, gwo, send, keep_a, keep_b, keep_c, whole):
    low, rec = normed[...], recalled[...]
    half = whole.shape[0] // 2
    third = keep_a.shape[0]
    core = scalar(info, "core")
    grads = (
        lambda: tm(low, dq[...]),
        lambda: tm(low, dk[...]) + tm(rec, dkm[...]),
        lambda: tm(low, dv[...]) + tm(rec, dvm[...]),
        None,
    )
    parts = (keep_a, keep_b, keep_c)
    for which, grad in enumerate(grads):
        source = gwo
        if grad is not None:
            whole[...] = grad().astype(BF16)
            source = whole
        send[which * half : (which + 1) * half, :] = source[at_half(1 - core, half), :]
        start = 0
        while start < half:
            part, offset = divmod(which * half + start, third)
            count = min(third - offset, half - start)
            at = pl.ds(pl.multiple_of(core * half + start, 16), count)
            parts[part][offset : offset + count, :] = source[at, :]
            start += count


def project_back_kernel(info, hidden, dq, dk, dv, dvm, wq, wk, wv, vecs_mid, vecs_rec, gb_own, gb_far, gn, vecs):
    width = hidden.shape[1]
    n = mt(dq[...], wq[...]) + mt(dk[...], wk[...]) + mt(dv[...], wv[...])
    gn[...] = n
    xhat, _ = normalized(hidden[...].astype(F32))
    shard = lax.broadcasted_iota(jnp.int32, (4, 1), 0)
    bias_rows = jnp.where(shard == scalar(info, "me"), gb_own[...], 0.0) + jnp.where(shard == scalar(info, "far"), gb_far[...], 0.0)
    vecs[...] = jnp.concatenate(
        [
            column_sum(n * xhat) + vecs_rec[0:1, :],
            column_sum(n) + vecs_rec[1:2, :],
            column_sum(dq[...].astype(F32)),
            column_sum(dv[...].astype(F32)) + column_sum(dvm[...].astype(F32)),
            vecs_mid[0:4, :],
            bias_rows,
            jnp.zeros((4, width), F32),
        ],
        axis=0,
    ).astype(BF16)


def last_kernel(hidden, gain, gn, handed, grad_resid, resid, out0, out1, b_out, output, grad_hidden):
    xhat, inverse = normalized(hidden[...].astype(F32))
    n = gn[...] + handed[...].astype(F32)
    grad_hidden[...] = grad_resid[...] + norm_back(xhat, inverse, n, gain[...])
    total = resid[...] + out0[...].astype(F32) + out1[...].astype(F32) + b_out[...]
    output[...] = total.astype(BF16)


def added(left, right):
    return (left.astype(F32) + right.astype(F32)).astype(BF16)


def fold_kernel(plan, info, *refs):
    count = len(plan)
    sources, targets = refs[: 2 * count], list(refs[2 * count :])
    for which, (kind, start, link) in enumerate(plan):
        kept, came = sources[2 * which], sources[2 * which + 1]
        if start is not None:
            came = came.at[pl.ds(start, kept.shape[0]), :]
        keep = targets.pop(0)
        if kind is None:
            keep[...] = added(kept[...], came[...])
            continue
        send = targets.pop(0)
        if kind == "groups":
            keep[...] = added(kept[0], came[0])
            send[...] = added(kept[1], came[1])
            continue
        half = kept.shape[-2] // 2
        mine = scalar(info, link)
        for ref, bit in ((keep, mine), (send, 1 - mine)):
            at = at_half(bit, half)
            if len(kept.shape) == 3:
                for group in range(kept.shape[0]):
                    ref[group] = added(kept[group, at, :], came[group, at, :])
            else:
                ref[...] = added(kept[at, :], came[at, :])


def join_kernel(plan, info, *refs):
    count = len(plan)
    sources, targets = refs[: 2 * count], list(refs[2 * count :])
    for which, (link, segments, vectors, apart) in enumerate(plan):
        own, came = sources[2 * which], sources[2 * which + 1]
        bit = scalar(info, link)
        pieces = len(segments) + (1 if vectors else 0)
        outs = [targets.pop(0) for _ in range(pieces)] if apart else [targets.pop(0)] * pieces
        read = write = 0
        for segment, out in zip(segments, outs):
            out[pl.ds(pl.multiple_of(write + bit * segment, 16), segment), :] = own[read : read + segment, :]
            out[pl.ds(pl.multiple_of(write + (1 - bit) * segment, 16), segment), :] = came[read : read + segment, :]
            read += segment
            write = 0 if apart else write + 2 * segment
        if vectors:
            outs[-1][write : write + 16, :] = added(own[read:, :], came[read:, :])


AXES = {"core": ("mp", 1), "y": ("mp", 2), "x": ("dp", 1), "z1": ("dp", 2), "z2": ("dp", 4)}


def swap(value, link):
    axis, mask = AXES[link]
    return lax.ppermute(value, axis, [(i, i ^ mask) for i in range(lax.axis_size(axis))])


def bit_of(link):
    axis, mask = AXES[link]
    return (lax.axis_index(axis) // mask) % 2


SCALAR = {"core": 0, "y": 1, "x": 2, "z1": 3, "z2": 4, "me": 5, "far": 6, "first": 7, "reset": 8, "cut_in": 9, "cut_out": 10}


def scalar_array(reset):
    bit = {link: bit_of(link) for link in AXES}
    me = lax.axis_index("mp")
    values = dict(
        bit, me=me, far=me ^ 2, first=me == 0, reset=reset, cut_in=2 * bit["z1"] + bit["x"], cut_out=2 * bit["x"] + bit["z1"]
    )
    row = lax.broadcasted_iota(jnp.int32, (1, 16), 1)
    packed = jnp.zeros((1, 16), jnp.int32)
    for name, value in values.items():
        packed = jnp.where(row == SCALAR[name], jnp.asarray(value, jnp.int32), packed)
    return packed


def scalar(info, name):
    return info[0, SCALAR[name]]


def halving(line, info, name, parts):
    came = {}
    for keep, send, links, _ in parts:
        if id(send) not in came:
            came[id(send)] = swap(send, links[0])
    plan, operands, outs = [], [], []
    for keep, send, links, start in parts:
        kind = None
        if len(links) > 1:
            kind = "groups" if links[1] == "y" and keep.ndim == 3 else "rows"
        plan.append((kind, start, links[1] if kind else None))
        operands += [keep, came[id(send)]]
        if kind is None:
            outs.append((keep.shape, BF16))
        elif kind == "groups":
            outs += [(keep.shape[1:], BF16)] * 2
        else:
            outs += [(keep.shape[:-2] + (keep.shape[-2] // 2, keep.shape[-1]), BF16)] * 2
    results = list(
        line.call(lambda *refs: fold_kernel(plan, *refs), outs, f"fold_{name}", (info, *operands), small=1)
    )
    after = []
    for (kind, _, _), (_, _, links, _) in zip(plan, parts):
        if kind is None:
            after.append(results.pop(0))
        else:
            after.append((results.pop(0), results.pop(0), links[1:], None))
    return after


def doubling(line, info, name, parts):
    plan, operands, outs, counts = [], [], [], []
    for array, link, segments, vectors, apart in parts:
        width = array.shape[1]
        operands += [array, swap(array, link)]
        plan.append((link, segments, vectors, apart))
        shapes = [(2 * segment, width) for segment in segments] + ([(16, width)] if vectors else [])
        if not apart:
            shapes = [(sum(rows for rows, _ in shapes), width)]
        outs += [(shape, BF16) for shape in shapes]
        counts.append(len(shapes))
    results = list(
        line.call(lambda *refs: join_kernel(plan, *refs), outs, f"join_{name}", (info, *operands), small=1)
    )
    split = []
    for count, (_, _, _, _, apart) in zip(counts, parts):
        piece, results = results[:count], results[count:]
        split.append(piece if apart else piece[0])
    return split


def beyond(value):
    others = lax.axis_size("dp") // 8
    if others == 1:
        return value
    groups = [[low + 8 * high for high in range(others)] for low in range(8)]
    return lax.psum(value.astype(F32), "dp", axis_index_groups=groups).astype(BF16)


def squares_kernel(info, a0, a1, b0, b1, c0, c1, *outs):
    *outs, vecs = outs
    third = b0.shape[0]
    half = outs[0].shape[0] // 2
    vecs[...] = added(a0[third:, :], a1[third:, :]).astype(F32)
    for core, parts in ((scalar(info, "core"), (a0, b0, c0)), (1 - scalar(info, "core"), (a1, b1, c1))):
        for which, out in enumerate(outs):
            start = 0
            while start < half:
                part, offset = divmod(which * half + start, third)
                count = min(third - offset, half - start)
                at = pl.ds(pl.multiple_of(core * half + start, 16), count)
                out[at, :] = parts[part][offset : offset + count, :].astype(F32)
                start += count


def mlp_grads_kernel(info, a, b0, b1, c0, c1, gw_in, gw_out):
    half = b0.shape[0]
    cut = gw_in.shape[0] - 2 * half
    gw_in[0 : 2 * half, :] = a[...].astype(F32)
    first = scalar(info, "x") == 0
    gw_in[2 * half :, :] = jnp.where(first, b0[...], b1[...])[:cut].astype(F32)
    gw_out[0 : 2 * half - cut, :] = jnp.where(first, b1[...], b0[...])[: 2 * half - cut].astype(F32)
    base = 2 * half - cut
    for own, bit in ((c0, scalar(info, "z1")), (c1, 1 - scalar(info, "z1"))):
        gw_out[pl.ds(pl.multiple_of(base + bit * half, half), half), :] = own[...].astype(F32)


def from_behind(value, axis, steps):
    count = lax.axis_size(axis)
    leading, last = (max(0, -steps), min(count, count - steps))
    return lax.ppermute(value, axis, [(source, source + steps) for source in range(leading, last)])


def local(
    hidden,
    past_states,
    reset_flags,
    sample_positions,
    norm1_gain,
    norm1_shift,
    w_query,
    bias_query,
    w_key,
    w_value,
    bias_value,
    w_attn_out,
    bias_attn_out,
    norm2_gain,
    norm2_shift,
    w_mlp_in,
    bias_mlp_in,
    w_mlp_out,
    bias_mlp_out,
    cotangent,
):
    rows, width = hidden.shape[1], hidden.shape[2]
    size = past_states.shape[1]
    units = w_mlp_in.shape[1]
    assert rows == size and sample_positions.shape[2] == size
    pairs = width // (2 * HD)
    arr, cot = hidden[0], cotangent[0]
    gain1, shift1, gain2, shift2 = norm1_gain, norm1_shift, norm2_gain, norm2_shift
    b_q, b_v, b_o, b_in, b_out = bias_query, bias_value, bias_attn_out, bias_mlp_in, bias_mlp_out
    row_bf, row_f = ((rows, width), BF16), ((rows, width), F32)
    square_f, square_bf, vec_f = ((width, width), F32), ((width, width), BF16), ((8, width), F32)

    line = Line()
    info = scalar_array(reset_flags[0])
    half_w, third = width // 2, 2 * width // 3
    quarter = ((width // 4, width), BF16)

    arrived = from_behind(arr, "mp", 1)
    cot_sib = swap(cot, "core")
    normed, q, k, v = line.call(
        front_kernel, [row_bf] * 4, "front", (arr, gain1, shift1, w_query, b_q, w_key, w_value, b_v),
        stream=(0, 3, 5, 6),
    )
    fit, cut_in, cut_out = line.call(
        lambda *refs: fit_kernel(size, *refs), [((size, size), BF16), quarter, quarter], "fit",
        (info, w_mlp_in, w_mlp_out), small=1, direct=(1, 2), far=(1, 2), scratch=[pltpu.SemaphoreType.DMA((2,))],
    )
    far_in, far_out, b_far = swap(cut_in, "y"), swap(cut_out, "y"), swap(b_in, "y")
    recalled, km, vm, often = line.call(
        memory_kernel, [row_bf] * 3 + [((8, size), F32)], "memory",
        (info, arrived, past_states[0], sample_positions[0], gain1, shift1, fit, w_key, w_value, b_v), small=1,
        stream=(2, 3, 7, 8),
    )

    whole = lambda shape: pl.BlockSpec(shape, lambda i: (0,) * len(shape))
    blocks = [
        pl.BlockSpec((rows, 2 * HD), lambda i: (0, i)),
        pl.BlockSpec((rows, 2 * HD), lambda i: (0, i + pairs // 2)),
    ]
    e_blocks = [
        pl.BlockSpec((2, rows, rows + size), lambda i: (i, 0, 0)),
        pl.BlockSpec((2, rows, rows + size), lambda i: (i + pairs // 2, 0, 0)),
    ]
    e_all = ((2 * pairs, rows, rows + size), BF16)
    grid = (pairs // 2,)
    vec1, often_spec = whole((width,)), whole((8, size))
    token = ((8, 128), F32)
    e, mixed, linv, done = line.blocks(
        attend_kernel, [e_all, row_bf, row_f, token], "attend", (q, k, v, km, vm, often), grid,
        [blocks[0]] * 5 + [often_spec], [e_blocks[0]] + [blocks[0]] * 2 + [whole((8, 128))], far=(0,), limit=24,
    )
    far_in, far_out = hold(far_in, done), hold(far_out, done)
    more_in, more_out = swap(far_in, "x"), swap(far_out, "z1")
    e, mixed, linv, resid, normed2 = line.blocks(
        attend_more_kernel, [e_all, row_bf, row_f, row_f, row_bf], "attend_more",
        (q, k, v, km, vm, often, e, mixed, linv, w_attn_out, b_o, arr, gain2, shift2), grid,
        [blocks[1]] * 5 + [often_spec, ANY, whole((rows, half_w)), ANY]
        + [whole((width, width)), vec1, whole((rows, width)), vec1, vec1],
        [e_blocks[1]] + [blocks[1]] * 2 + [whole((rows, width))] * 2,
        scratch=[pltpu.VMEM((rows, width), BF16)], aliases={6: 0, 7: 1, 8: 2}, far=(0,), limit=28, there=(6,),
    )
    normed2_sib = swap(normed2, "core")
    far_in, far_out = line.call(
        lambda *refs: join_kernel([("x", (width // 4,), False, False), ("z1", (width // 4,), False, False)], *refs),
        [((half_w, width), BF16)] * 2, "join_weights", (info, far_in, more_in, far_out, more_out), small=1,
    )
    more_in, more_out = swap(far_in, "z1"), swap(far_out, "x")

    part, both = ((third, width), BF16), ((2, rows, width), BF16)
    bias_f = ((1, units), F32)
    out_own, gx_own, g_a, g_b, g_c, gb_own = line.call(
        mlp_own_kernel, [both, both, part, part, part, bias_f], "mlp_own",
        (normed2, normed2_sib, cot, cot_sib, w_mlp_in, b_in, w_mlp_out), stream=(4, 2, 6), limit=32,
        scratch=[pltpu.VMEM((2 * rows, units), BF16)] * 2,
    )
    w_in_far, w_out_far = line.call(
        lambda *refs: join_kernel([("z1", (half_w,), False, False), ("x", (half_w,), False, False)], *refs),
        [((width, units), BF16), ((units, width), BF16)], "far_weights", (info, far_in, more_in, far_out, more_out), small=1,
    )
    gx_keep, gx_send, out_keep, out_send, r_a, r_b, r_c, gb_far = line.call(
        mlp_far_kernel, [row_bf] * 4 + [part] * 3 + [bias_f], "mlp_far",
        (normed2, normed2_sib, cot, cot_sib, w_in_far, b_far, w_out_far, out_own, gx_own), stream=(2,), limit=32,
        scratch=[pltpu.VMEM((2 * rows, units), BF16)] * 2,
    )
    halves = ((2, third // 2, width), BF16)
    keep_b, send_b, keep_c, send_c = line.call(
        part_kernel, [halves] * 4, "part", (info, g_b, g_c, r_b, r_c), small=1
    )
    gx_came = swap(gx_send, "core")
    out_came = swap(out_send, "core")
    mlp_parts = [
        (g_a, r_a, ("y", "x", "z1", "z2"), None),
        (keep_b, send_b, ("x", "z1", "z2", "y"), None),
        (keep_c, send_c, ("z1", "z2", "y", "x"), None),
    ]

    grad_mixed, grad_resid, gwo, vecs_mid = line.call(
        middle_kernel, [row_bf, row_f, square_bf, vec_f], "middle",
        (gx_keep, gx_came, resid, cot, gain2, mixed, w_attn_out), stream=(3, 6),
    )
    grads = ()
    for which in range(2):
        grads = line.blocks(
            attend_back_kernel, [row_bf] * 5, f"attend_back_{which}", (q, k, v, km, vm, e, linv, mixed, grad_mixed) + tuple(grads),
            grid, [blocks[which]] * 5 + [e_blocks[which]] + [blocks[which]] * 3 + [ANY] * len(grads),
            [blocks[which]] * 5, there=(5,), aliases={9 + i: i for i in range(len(grads))},
        )
    dq, dk, dv, dkm, dvm = grads
    mlp_parts = halving(line, info, "mlp_1", mlp_parts)
    send, keep_a, keep_b, keep_c = line.call(
        weight_grads_kernel, [((2 * width, width), BF16), part, part, part], "weight_grads",
        (info, normed, recalled, dq, dk, dv, dkm, dvm, gwo), small=1, scratch=[pltpu.VMEM((width, width), BF16)],
    )
    parts = [
        (keep_a, send, ("core", "y", "x", "z1", "z2"), 0),
        (keep_b, send, ("core", "x", "z1", "z2", "y"), third),
        (keep_c, send, ("core", "z1", "z2", "y", "x"), 2 * third),
    ]
    grad_memory, vecs_rec = line.call(
        recall_back_kernel, [row_bf, vec_f], "recall_back", (info, dkm, dvm, w_key, w_value, fit, arrived), small=1, stream=(3, 4),
    )
    handed = from_behind(grad_memory, "mp", -1)
    parts = halving(line, info, "core", parts)
    gn, vecs = line.call(
        project_back_kernel, [row_f, ((16, width), BF16)], "project_back",
        (info, arr, dq, dk, dv, dvm, w_query, w_key, w_value, vecs_mid, vecs_rec, gb_own, gb_far), small=1,
        stream=(6, 7, 8, 1),
    )
    output, grad_hidden = line.call(
        last_kernel, [row_bf, row_f], "last", (arr, gain1, gn, handed, grad_resid, resid, out_keep, out_came, b_out),
        stream=(0,), far=(0, 1),
    )
    mlp_parts = halving(line, info, "mlp_2", mlp_parts)
    parts = halving(line, info, "1", parts)
    mlp_parts = halving(line, info, "mlp_3", mlp_parts)
    parts = halving(line, info, "2", parts)
    mlp_a, mlp_b, mlp_c = halving(line, info, "mlp_4", mlp_parts)
    parts = halving(line, info, "3", parts)
    block_a, block_b, block_c = halving(line, info, "4", parts)

    small = block_a.shape[0]
    mlp_small = mlp_a.shape[0]
    pack = jnp.concatenate([block_a, mlp_a, vecs], axis=0)
    pack, block_b, mlp_b, mlp_c = beyond(pack), beyond(block_b), beyond(mlp_b), beyond(mlp_c)
    block_c = beyond(block_c)
    pack, block_b, mlp_b, block_c, mlp_c = doubling(line, info, "1", [
        (pack, "z2", (small, mlp_small), True, False),
        (block_b, "y", (small,), False, False), (mlp_b, "z2", (mlp_small,), False, False),
        (block_c, "x", (small,), False, False), (mlp_c, "x", (mlp_small,), False, False),
    ])
    small, mlp_small = 2 * small, 2 * mlp_small
    pack, block_b, mlp_b, block_c, mlp_c = doubling(line, info, "2", [
        (pack, "z1", (small, mlp_small), True, False),
        (block_b, "z2", (small,), False, False), (mlp_b, "z1", (mlp_small,), False, False),
        (block_c, "y", (small,), False, False), (mlp_c, "z2", (mlp_small,), False, False),
    ])
    small, mlp_small = 2 * small, 2 * mlp_small
    mlp_b0, mlp_c0 = mlp_b, mlp_c
    mlp_b1, mlp_c1 = swap(mlp_b, "x"), swap(mlp_c, "z1")
    (block_a, mlp_a, vecs), block_b, block_c = doubling(line, info, "3", [
        (pack, "x", (small, mlp_small), True, True),
        (block_b, "z1", (small,), False, False),
        (block_c, "z2", (small,), False, False),
    ])
    gw_in, gw_out = line.call(
        mlp_grads_kernel, [((width, units), F32), ((units, width), F32)], "mlp_grads",
        (info, mlp_a, mlp_b0, mlp_b1, mlp_c0, mlp_c1), small=1, far=(0, 1),
    )
    small = 2 * small
    pack = jnp.concatenate([block_a, vecs], axis=0)
    pack, block_b, block_c = doubling(line, info, "4", [
        (pack, "y", (small,), True, False), (block_b, "x", (small,), False, False), (block_c, "z1", (small,), False, False),
    ])
    gwq, gwk, gwv, gwo, vecs = line.call(
        squares_kernel, [square_f] * 4 + [((16, width), F32)], "squares",
        (info, pack, swap(pack, "core"), block_b, swap(block_b, "core"), block_c, swap(block_c, "core")),
        small=1, far=(0, 1, 2, 3),
    )
    return (
        output[None],
        grad_hidden[None],
        vecs[0],
        vecs[1],
        gwq,
        vecs[2],
        gwk,
        gwv,
        vecs[3],
        gwo,
        vecs[4],
        vecs[5],
        vecs[6],
        gw_in,
        lax.dynamic_index_in_dim(vecs, 8 + lax.axis_index("mp"), 0, keepdims=False),
        gw_out,
        vecs[7],
    )


def solution(mesh):
    rows = P("dp", "mp", None)
    placed = (rows, P("dp", None, None), P("dp"), rows) + (P(),) * 11
    placed += (P(None, "mp"), P("mp"), P("mp", None), P(), rows)
    return jax.shard_map(
        local,
        mesh=mesh,
        in_specs=placed,
        out_specs=(rows, rows) + (P(),) * 11 + (P(None, "mp"), P("mp"), P("mp", None), P()),
        check_vma=False,
    )
```

```python
import math

import jax
import jax.numpy as jnp
from jax import lax
from jax.experimental import pallas as pl
from jax.experimental.pallas import tpu as pltpu
from jax.sharding import PartitionSpec as P

HD = 64
NORM_EPSILON = 1e-05
RIDGE_WEIGHT = 0.1
NOTHING = -1e30
GELU_SLOPE = math.sqrt(2.0 / math.pi)
GELU_CUBE = 0.044715
F32 = jnp.float32
BF16 = jnp.bfloat16
MEBI = 1 << 20


def mm(left, right):
    return jnp.dot(left, right, preferred_element_type=F32)


def mt(left, right):
    return lax.dot_general(left, right, (((1,), (1,)), ((), ())), preferred_element_type=F32)


def tm(left, right):
    return lax.dot_general(left, right, (((0,), (0,)), ((), ())), preferred_element_type=F32)


def column_sum(values):
    return jnp.sum(values, axis=0, keepdims=True)


def normalized(values):
    row_mean = jnp.mean(values, axis=-1, keepdims=True)
    centered = values - row_mean
    row_var = jnp.mean(centered * centered, axis=-1, keepdims=True)
    inverse = lax.rsqrt(row_var + NORM_EPSILON)
    return centered * inverse, inverse


def norm_back(xhat, inverse, incoming, gain):
    g = incoming * gain
    mean_g = jnp.mean(g, axis=-1, keepdims=True)
    mean_gx = jnp.mean(g * xhat, axis=-1, keepdims=True)
    return inverse * (g - mean_g - xhat * mean_gx)


SMALL = pl.BlockSpec(memory_space=pltpu.SMEM)
VMEM = pl.BlockSpec(memory_space=pltpu.VMEM)
ANY = pl.BlockSpec(memory_space=pl.ANY)
HBM = pl.BlockSpec(memory_space=pltpu.HBM)


class Arriving:
    def __init__(self, source, held, sem):
        self.held, self.copy = held, pltpu.make_async_copy(source, held, sem)
        self.shape, self.dtype = held.shape, held.dtype
        self.here = False
        self.copy.start()

    def wait(self):
        if not self.here:
            self.copy.wait()
            self.here = True
        return self.held

    @property
    def at(self):
        return self.wait().at

    def __getitem__(self, index):
        return self.wait()[index]


class Leaving:
    def __init__(self, target, held, sem):
        self.held, self.copy = held, pltpu.make_async_copy(held, target, sem)
        self.shape, self.dtype = held.shape, held.dtype
        self.gone = False

    def leave(self):
        if not self.gone:
            self.copy.start()
            self.gone = True

    def __getitem__(self, index):
        return self.held[index]

    def __setitem__(self, index, value):
        self.held[index] = value
        if index is Ellipsis:
            self.leave()


class Line:
    def __init__(self):
        self.last = None

    def start(self, body, outs, name, operands, grid, in_specs, out_specs, scratch, after=(), aliases=None, far=(), limit=32, there=()):
        waits = list(after) + ([] if self.last is None else [self.last])
        operands = [pltpu.with_memory_space_constraint(o, pltpu.HBM) if i in there else o for i, o in enumerate(operands)]
        known, gone = len(operands), len(operands) + len(waits)
        results = pl.pallas_call(
            lambda *refs: body(*refs[:known], *refs[gone : gone + len(outs)], *refs[gone + len(outs) + 1 :]),
            out_shape=[(pltpu.HBM if i in far else pltpu.VMEM)(shape, dtype) for i, (shape, dtype) in enumerate(outs)]
            + [pltpu.VMEM((8, 128), F32)],
            grid=grid,
            in_specs=list(in_specs) + [ANY] * len(waits),
            out_specs=list(out_specs) + [VMEM],
            scratch_shapes=list(scratch),
            input_output_aliases=aliases or {},
            compiler_params=pltpu.CompilerParams(vmem_limit_bytes=limit * MEBI),
            cost_estimate=pl.CostEstimate(flops=0, bytes_accessed=0, transcendentals=0),
            name=name,
        )(*operands, *waits)
        *results, self.last = results
        return results

    def blocks(self, body, outs, name, operands, grid, in_specs, out_specs, scratch=(), **more):
        return self.start(body, outs, name, operands, grid, in_specs, out_specs, scratch, **more)

    def call(self, body, outs, name, operands, small=0, load=(), far=(), scratch=(), after=(), limit=16):
        outs = list(outs) + [(operands[i].shape, operands[i].dtype) for i in load]
        own, kept = len(scratch), len(outs) - len(load)
        in_specs = [SMALL if i < small else HBM if i in load else VMEM for i in range(len(operands))]
        out_specs = [HBM if i in far else VMEM for i in range(len(outs))]
        held = [pltpu.VMEM(*outs[i]) for i in far]
        sems = [pltpu.SemaphoreType.DMA((len(far) + len(load),))] if far or load else []

        def run(*refs):
            ins, targets, rest = refs[: len(operands)], refs[len(operands) : len(operands) + len(outs)], refs[len(operands) + len(outs) :]
            mine, buffers, sem = rest[:own], rest[own:], rest[-1] if sems else None
            ins, targets = list(ins), list(targets)
            for slot, i in enumerate(load):
                ins[i] = Arriving(ins[i], targets[kept + slot], sem.at[len(far) + slot])
            for slot, i in enumerate(far):
                targets[i] = Leaving(targets[i], buffers[slot], sem.at[slot])
            body(*ins, *targets[:kept], *mine)
            for i in load:
                ins[i].wait()
            for i in far:
                targets[i].leave()
            for i in far:
                targets[i].copy.wait()

        return self.start(
            run, outs, name, operands, (1,), in_specs, out_specs, list(scratch) + held + sems, after, far=far, limit=limit,
            there=tuple(load),
        )


def hold(value, *until):
    return lax.optimization_barrier((value,) + until)[0]


def at_half(bit, count):
    return pl.ds(pl.multiple_of(bit * count, count), count)


def fit_at_positions(size, fit_ref):
    half = size // 2
    spread = 1.0 / size
    row = lax.broadcasted_iota(jnp.int32, (half, half), 0)
    col = lax.broadcasted_iota(jnp.int32, (half, half), 1)
    eye = jnp.where(row == col, 1.0, 0.0).astype(F32)
    flip = jnp.where(row + col == half - 1, 1.0, 0.0).astype(BF16)

    def design(columns):
        apart = (row.astype(F32) + 0.5) / size - (columns.astype(F32) + 0.5) / size
        return jnp.exp(-(apart * apart) / (2.0 * spread * spread))

    def pieces(value):
        high = value.astype(BF16)
        return high, (value - high.astype(F32)).astype(BF16)

    def exact(left, right):
        (left_high, left_low), (right_high, right_low) = pieces(left), pieces(right)
        return mm(left_high, right_high) + (mm(left_high, right_low) + mm(left_low, right_high))

    def full(left, right):
        return jnp.dot(left, right, precision=lax.Precision.HIGHEST, preferred_element_type=F32)

    direct, mirrored = design(col), design(size - 1 - col)
    brackets, guesses = [], []
    for part in (direct + mirrored, direct - mirrored):
        bracket = full(part, part) + RIDGE_WEIGHT * eye
        low = bracket.astype(BF16)
        brackets.append(bracket)
        guesses.append(2.39060839 * eye - 0.96134588 * bracket + 0.09859958 * mm(low, low))
    for step in range(6):
        for which in range(2):
            bracket, guess = brackets[which], guesses[which]
            if step < 4:
                low = guess.astype(BF16)
                left = 2.0 * eye - mm(bracket.astype(BF16), low)
                guesses[which] = mm(low, left.astype(BF16))
            else:
                guesses[which] = exact(guess, 2.0 * eye - exact(bracket, guess))
    even, odd = (eye - RIDGE_WEIGHT * guess for guess in guesses)
    inner = (0.5 * (even + odd)).astype(BF16)
    outer = (0.5 * (even - odd)).astype(BF16)
    fit_ref[0:half, 0:half] = inner
    fit_ref[0:half, half:size] = mm(outer, flip).astype(BF16)
    fit_ref[half:size, 0:half] = mm(flip, outer).astype(BF16)
    fit_ref[half:size, half:size] = mm(flip, mm(inner, flip).astype(BF16)).astype(BF16)


VECTORS = ("gain1", "shift1", "b_q", "b_v", "b_o", "gain2", "shift2", "b_in", "b_out")


def vector(table, name):
    at = VECTORS.index(name)
    return table[at : at + 1, :]


def start_kernel(info, w_in, w_out, *refs):
    vectors, (fit, table, cut_in, cut_out) = refs[: len(VECTORS)], refs[-4:]
    fit_at_positions(fit.shape[0], fit)
    table[...] = jnp.zeros_like(table)
    for at, value in enumerate(vectors):
        table[at, :] = value[...]
    count = cut_out.shape[0]
    cut_in[0:count, :] = w_in[at_half(scalar(info, "x"), count), :]
    bias, pieces = vector(table, "b_in"), []
    for _ in range(3):
        pieces.append(bias.astype(BF16))
        bias = bias - pieces[-1].astype(F32)
    cut_in[count:, :] = jnp.concatenate(pieces + [jnp.zeros((13, table.shape[1]), BF16)], axis=0)
    cut_in.leave()
    cut_out[...] = w_out[at_half(scalar(info, "z1"), count), :]


def front_kernel(hidden, table, wq, wk, wv, normed, q, k, v):
    xhat, _ = normalized(hidden[...].astype(F32))
    low = (xhat * vector(table, "gain1") + vector(table, "shift1")).astype(BF16)
    normed[...] = low
    scale = 1.0 / math.sqrt(HD)
    q[...] = (mm(low, wq[...]) + vector(table, "b_q")).astype(BF16) * jnp.asarray(scale, BF16)
    k[...] = mm(low, wk[...]).astype(BF16)
    v[...] = (mm(low, wv[...]) + vector(table, "b_v")).astype(BF16)


def memory_kernel(info, arrived, past, positions, table, fit, wk, wv, recalled, km, vm, often):
    size = fit.shape[0]
    xhat, _ = normalized(arrived[...].astype(F32))
    before = xhat * vector(table, "gain1") + vector(table, "shift1")
    kept = past[...].astype(F32) * (1 - scalar(info, "reset")).astype(F32)
    earlier = jnp.where(scalar(info, "first") > 0, kept, before).astype(BF16)
    low = mm(fit[...], earlier).astype(BF16)
    recalled[...] = low
    km[...] = mm(low, wk[...]).astype(BF16)
    vm[...] = (mm(low, wv[...]) + vector(table, "b_v")).astype(BF16)
    place = lax.broadcasted_iota(jnp.int32, (size, positions.shape[1]), 0)
    hit = jnp.where(place == positions[...], 1.0, 0.0).astype(BF16)
    count = mt(jnp.ones((8, positions.shape[1]), BF16), hit)
    often[...] = jnp.where(count > 0.5, jnp.log(jnp.maximum(count, 1.0)), NOTHING)


def attend_pair(q, k, v, km, vm, often, e, mixed, linv):
    rows = q.shape[0]
    half = rows // 2
    lane = lax.broadcasted_iota(jnp.int32, (1, 2 * HD), 1)
    row = lax.broadcasted_iota(jnp.int32, (half, half), 0)
    col = lax.broadcasted_iota(jnp.int32, (half, half), 1)
    log_count = often[0:1, :]
    for part in range(2):
        here = slice(part * half, (part + 1) * half)
        seen = (part + 1) * half
        results = []
        for head in range(2):
            mine = (lane >= head * HD) & (lane < (head + 1) * HD)
            query = jnp.where(mine, q[here, :], jnp.zeros((), BF16))
            near = mt(query, k[0:seen, :])
            edge = jnp.where(col > row, NOTHING, near[:, part * half :])
            far = mt(query, km[...]) + log_count
            top = jnp.maximum(jnp.max(edge, axis=-1, keepdims=True), jnp.max(far, axis=-1, keepdims=True))
            if part:
                top = jnp.maximum(top, jnp.max(near[:, : part * half], axis=-1, keepdims=True))
            edge = jnp.exp(edge - top)
            far = jnp.exp(far - top)
            total = jnp.sum(edge, axis=-1, keepdims=True) + jnp.sum(far, axis=-1, keepdims=True)
            edge_low, far_low = edge.astype(BF16), far.astype(BF16)
            e[head, here, part * half : seen] = edge_low
            e[head, here, rows:] = far_low
            out = mm(edge_low, v[part * half : seen, :]) + mm(far_low, vm[...])
            if part:
                start = jnp.exp(near[:, : part * half] - top)
                total = total + jnp.sum(start, axis=-1, keepdims=True)
                start_low = start.astype(BF16)
                e[head, here, 0 : part * half] = start_low
                out = out + mm(start_low, v[0 : part * half, :])
            inverse = 1.0 / total
            results.append((out * inverse, inverse))
        first = lane < HD
        mixed[here, :] = jnp.where(first, results[0][0], results[1][0]).astype(BF16)
        linv[here, :] = jnp.where(first, results[0][1], results[1][1])


def attend_kernel(q, k, v, km, vm, often, *refs):
    e, mixed, linv = refs[-3:]
    attend_pair(q, k, v, km, vm, often, e, mixed, linv)


def attend_more_kernel(
    q, k, v, km, vm, often, e_done, mixed_done, linv_done, wo, table, hidden,
    e, mixed, linv, resid, normed2_a, normed2_b, every,
):
    step, rows = pl.program_id(0), q.shape[0]
    attend_pair(q, k, v, km, vm, often, e, mixed, linv)
    done, block = mixed_done.shape[1], mixed.shape[1]
    every[:, pl.ds(pl.multiple_of(done + step * block, block), block)] = mixed[...]

    @pl.when(step == pl.num_programs(0) - 1)
    def _():
        every[:, 0:done] = mixed_done[...]
        total = hidden[...].astype(F32) + mm(every[...], wo[...]) + vector(table, "b_o")
        resid[...] = total
        xhat, _ = normalized(total)
        normed2 = (xhat * vector(table, "gain2") + vector(table, "shift2")).astype(BF16)
        normed2_a[...] = normed2[: rows // 2]
        normed2_b[...] = normed2[rows // 2 :]


def mlp_block(x, cot, w_in, b_in, w_out):
    pre = mm(x, w_in) + b_in
    square = pre * pre
    bend = jnp.tanh(GELU_SLOPE * pre * (1.0 + GELU_CUBE * square))
    act = (0.5 * pre * (1.0 + bend)).astype(BF16)
    slope = 0.5 * (1.0 + bend) + (0.5 * GELU_SLOPE) * pre * (1.0 - bend * bend) * (1.0 + 3.0 * GELU_CUBE * square)
    gpre = (mt(cot, w_out) * slope).astype(BF16)
    return mm(act, w_out), mt(gpre, w_in), act, gpre


def mlp_kernel(xa, xb, xc, xd, cot0, cot1, w_in, b_in, w_out, out, gx, grads, g_bias, acts, gpres):
    block, width, units = xa.shape[0], xa.shape[1], acts.shape[1]
    bias = b_in[...] if b_in.shape[0] == 1 else vector(b_in, "b_in")
    parts = []
    for which, x in enumerate((xa, xb, xc, xd)):
        here, there = slice(which % 2 * block, (which % 2 + 1) * block), slice(which * block, (which + 1) * block)
        cot = (cot0, cot1)[which // 2]
        o, g, act, gpre = mlp_block(x[...], cot[here, :], w_in[...], bias, w_out[...])
        out[which // 2, here, :], gx[which // 2, here, :] = o.astype(BF16), g.astype(BF16)
        acts[there, :] = act
        gpres[there, :] = gpre
        parts.append((x, there))
    total = tm(xa[...], gpres[0:block, :])
    for x, there in parts[1:]:
        total = total + tm(x[...], gpres[there, :])
    grads[0:width, :] = total.astype(BF16)
    half = 2 * block
    grads[width : width + units, :] = (tm(acts[:half, :], cot0[...]) + tm(acts[half:, :], cot1[...])).astype(BF16)
    g_bias[...] = column_sum(gpres[...].astype(F32))


def merge_kernel(gx, gx_far, keep_gx, send_gx):
    keep_gx[...] = added(gx[0], gx_far[0])
    send_gx[...] = added(gx[1], gx_far[1])


def middle_kernel(
    gx, gx_more, resid, cot, table, mixed, wo, out_own, out_far, grad_mixed, grad_resid, gwo, vecs,
    send_a, send_b
):
    half = send_a.shape[0]
    send_a[...] = added(out_own[1, 0:half, :], out_far[1, 0:half, :])
    send_b[...] = added(out_own[1, half:, :], out_far[1, half:, :])
    xhat, inverse = normalized(resid[...])
    n = gx[...].astype(F32) + gx_more[...].astype(F32)
    cot_full = cot[...].astype(F32)
    total = cot_full + norm_back(xhat, inverse, n, vector(table, "gain2"))
    grad_resid[...] = total
    low = total.astype(BF16)
    grad_mixed[...] = mt(low, wo[...]).astype(BF16)
    gwo[...] = tm(mixed[...], low).astype(BF16)
    vecs[...] = jnp.concatenate(
        [
            column_sum(low.astype(F32)),
            column_sum(n * xhat),
            column_sum(n),
            column_sum(cot_full),
            jnp.zeros((4, n.shape[1]), F32),
        ],
        axis=0,
    )


def attend_back_kernel(q, k, v, km, vm, e, linv, mixed, gmix, *refs):
    dq, dk, dv, dkm, dvm = refs[-5:]
    rows = q.shape[0]
    half = rows // 2
    lane = lax.broadcasted_iota(jnp.int32, (1, 2 * HD), 1)
    scale = 1.0 / math.sqrt(HD)
    sums = {}

    def add(name, value):
        sums[name] = sums[name] + value if name in sums else value

    for part in range(2):
        here = slice(part * half, (part + 1) * half)
        seen = (part + 1) * half
        grad = gmix[here, :].astype(F32) * linv[here, :]
        product = grad * mixed[here, :].astype(F32)
        queries = []
        for head in range(2):
            mine = (lane >= head * HD) & (lane < (head + 1) * HD)
            query = jnp.where(mine, q[here, :], jnp.zeros((), BF16))
            grad_low = jnp.where(mine, grad, 0.0).astype(BF16)
            dot = jnp.sum(jnp.where(mine, product, 0.0), axis=-1, keepdims=True)
            near_e, far_e = e[head, here, 0:seen], e[head, here, rows:]
            near = (near_e.astype(F32) * (mt(grad_low, v[0:seen, :]) - dot)).astype(BF16)
            far = (far_e.astype(F32) * (mt(grad_low, vm[...]) - dot)).astype(BF16)
            queries.append(mm(near, k[0:seen, :]) + mm(far, km[...]))
            dk_near, dv_near = tm(query, near), tm(grad_low, near_e)
            for block in range(part + 1):
                where = slice(block * half, (block + 1) * half)
                add(("k", block), dk_near[:, where])
                add(("v", block), dv_near[:, where])
            add("km", tm(query, far))
            add("vm", tm(grad_low, far_e))
        dq[here, :] = (jnp.where(lane < HD, queries[0], queries[1]) * scale).astype(BF16)
    for block in range(2):
        where = slice(block * half, (block + 1) * half)
        dk[where, :] = sums["k", block].T.astype(BF16)
        dv[where, :] = sums["v", block].T.astype(BF16)
    dkm[...] = sums["km"].T.astype(BF16)
    dvm[...] = sums["vm"].T.astype(BF16)


def recall_back_kernel(info, dkm, dvm, wk, wv, fit, arrived, grad_memory, vecs):
    grad_recalled = (mt(dkm[...], wk[...]) + mt(dvm[...], wv[...])).astype(BF16)
    handed = tm(fit[...], grad_recalled).astype(BF16)
    grad_memory[...] = handed
    xhat, _ = normalized(arrived[...].astype(F32))
    n = jnp.where(scalar(info, "first") > 0, 0.0, handed.astype(F32))
    vecs[...] = jnp.concatenate([column_sum(n * xhat), column_sum(n), jnp.zeros((6, n.shape[1]), F32)], axis=0)


def weight_grads_kernel(info, normed, recalled, dq, dk, dv, dkm, dvm, gwo, send, keep_a, keep_b, keep_c, whole):
    low, rec = normed[...], recalled[...]
    half = whole.shape[0] // 2
    third = keep_a.shape[0]
    core = scalar(info, "core")
    grads = (
        lambda: tm(low, dq[...]),
        lambda: tm(low, dk[...]) + tm(rec, dkm[...]),
        lambda: tm(low, dv[...]) + tm(rec, dvm[...]),
        None,
    )
    parts = (keep_a, keep_b, keep_c)
    for which, grad in enumerate(grads):
        source = gwo
        if grad is not None:
            whole[...] = grad().astype(BF16)
            source = whole
        send[which * half : (which + 1) * half, :] = source[at_half(1 - core, half), :]
        start = 0
        while start < half:
            part, offset = divmod(which * half + start, third)
            count = min(third - offset, half - start)
            at = pl.ds(pl.multiple_of(core * half + start, 16), count)
            parts[part][offset : offset + count, :] = source[at, :]
            start += count


def project_back_kernel(info, hidden, dq, dk, dv, dvm, wq, wk, wv, vecs_mid, vecs_rec, gb_own, gb_far, gn, vecs):
    width = hidden.shape[1]
    n = mt(dq[...], wq[...]) + mt(dk[...], wk[...]) + mt(dv[...], wv[...])
    gn[...] = n
    xhat, _ = normalized(hidden[...].astype(F32))
    shard = lax.broadcasted_iota(jnp.int32, (4, 1), 0)
    bias_rows = jnp.where(shard == scalar(info, "me"), gb_own[...], 0.0) + jnp.where(shard == scalar(info, "far"), gb_far[...], 0.0)
    vecs[...] = jnp.concatenate(
        [
            column_sum(n * xhat) + vecs_rec[0:1, :],
            column_sum(n) + vecs_rec[1:2, :],
            column_sum(dq[...].astype(F32)),
            column_sum(dv[...].astype(F32)) + column_sum(dvm[...].astype(F32)),
            vecs_mid[0:4, :],
            bias_rows,
            jnp.zeros((4, width), F32),
        ],
        axis=0,
    ).astype(BF16)


def last_kernel(hidden, table, gn, handed, grad_resid, grad_hidden):
    xhat, inverse = normalized(hidden[...].astype(F32))
    n = gn[...] + handed[...].astype(F32)
    grad_hidden[...] = grad_resid[...] + norm_back(xhat, inverse, n, vector(table, "gain1"))


def added(left, right):
    return (left.astype(F32) + right.astype(F32)).astype(BF16)


def join_kernel(plan, info, *refs):
    for which, link in enumerate(plan):
        own, came, out = refs[2 * which], refs[2 * which + 1], refs[2 * len(plan) + which]
        count = out.shape[0] // 2
        out[at_half(scalar(info, link), count), :] = own[0:count, :]
        out[at_half(1 - scalar(info, link), count), :] = came[0:count, :]


def far_weights_kernel(info, in_own, in_came, out_own, out_came, w_in, w_out, b_in):
    join_kernel(("x", "z1"), info, in_own, in_came, out_own, out_came, w_in, w_out)
    pieces = in_own[in_own.shape[0] - 16 :, :].astype(F32)
    b_in[...] = pieces[0:1] + pieces[1:2] + pieces[2:3]


MLP_PARTS = (
    (("y", "x", "z2", "z1"), 384), (("y", "z1", "x", "z2"), 128), (("x", "y", "z2", "z1"), 128),
    (("x", "z1", "y", "z2"), 384), (("z1", "y", "x", "z2"), 384), (("z1", "x", "y", "z2"), 128),
)
ATTN_ORDERS = (("y", "z1", "x", "z2"), ("x", "y", "z1", "z2"), ("z1", "x", "y", "z2"))
AXES = {"core": ("mp", 1), "y": ("mp", 2), "x": ("dp", 1), "z1": ("dp", 2), "z2": ("dp", 4)}


def swap(value, link):
    axis, mask = AXES[link] if link in AXES else ("dp", int(link))
    return lax.ppermute(value, axis, [(i, i ^ mask) for i in range(lax.axis_size(axis))])


def bit_of(link):
    axis, mask = AXES[link]
    return (lax.axis_index(axis) // mask) % 2


SCALAR = {"core": 0, "y": 1, "x": 2, "z1": 3, "z2": 4, "me": 5, "far": 6, "first": 7, "reset": 8}


def scalar_array(reset):
    bit = {link: bit_of(link) for link in AXES}
    me = lax.axis_index("mp")
    values = dict(bit, me=me, far=me ^ 2, first=me == 0, reset=reset)
    row = lax.broadcasted_iota(jnp.int32, (1, 16), 1)
    packed = jnp.zeros((1, 16), jnp.int32)
    for name, value in values.items():
        packed = jnp.where(row == SCALAR[name], jnp.asarray(value, jnp.int32), packed)
    return packed


def scalar(info, name):
    return info[0, SCALAR[name]]


class Item:
    def __init__(self, steps, *kept, now=None, came=None):
        self.steps, self.kept, self.now, self.came = list(steps), list(kept), now, came


class Rounds:
    def __init__(self, line, info):
        self.line, self.info = line, info

    def go(self, name, items):
        arrays, sends, outs, jobs = [], {}, [], []

        def slot(array):
            for which, known in enumerate(arrays):
                if known is array:
                    return which
            arrays.append(array)
            return len(arrays) - 1

        for item in items:
            kind, link = item.now or ("start", None)
            came, at = (slot(item.came[0]), item.came[1]) if link else (None, 0)
            sources = []
            for array, first, rows in item.kept:
                sources.append((slot(array), first, came, at, rows, kind, link))
                at += rows
            rows = item.kept[0][2] * (2 if kind == "double" else 1)
            step = item.steps.pop(0) if item.steps else None
            sent = sends.setdefault(step[1], [0]) if step else None
            if step is None:
                jobs.append((sources[0], "all", None, len(outs), 0, rows))
                item.kept = [("out", len(outs), rows)]
                outs.append(rows)
            elif step[0] in ("swap", "double"):
                jobs.append((sources[0], "all", None, step[1], sent[0], rows))
                item.came, item.kept = (None, sent[0]), [(step[1], sent[0], rows)]
                sent[0] += rows
            elif step[0] == "pair":
                jobs.append((sources[0], "all", None, len(outs), 0, rows))
                jobs.append((sources[1], "all", None, step[1], sent[0], rows))
                item.came, item.kept = (None, sent[0]), [("out", len(outs), rows)]
                sent[0] += rows
                outs.append(rows)
            else:
                half, kept = rows // 2, []
                item.came = (None, sent[0])
                for source in sources:
                    jobs.append((source, "mine", step[1], len(outs), 0, half))
                    jobs.append((source, "other", step[1], step[1], sent[0], half))
                    kept.append(("out", len(outs), half))
                    sent[0] += half
                    outs.append(half)
                item.kept = kept
            item.now = step
        links = list(sends)
        width = arrays[0].shape[1]
        shapes = [((rows, width), BF16) for rows in outs] + [((sends[link][0], width), BF16) for link in links]

        def body(info, *refs):
            ins, results = refs[: len(arrays)], refs[len(arrays) :]
            for (kept, first, came, at, rows, kind, over), what, link, target, base, count in jobs:
                out = results[len(outs) + links.index(target) if isinstance(target, str) else target]
                if kind == "double":
                    for bit, ref, start in ((scalar(info, over), kept, first), (1 - scalar(info, over), came, at)):
                        out[pl.ds(pl.multiple_of(base + bit * rows, 16), rows), :] = ins[ref][start : start + rows, :]
                    continue
                start = 0
                if what != "all":
                    bit = scalar(info, link)
                    start = (bit if what == "mine" else 1 - bit) * count

                def here(base):
                    if what == "all":
                        return slice(base, base + count)
                    return pl.ds(pl.multiple_of(base + start, 16), count)

                value = ins[kept][here(first), :]
                if kind != "start":
                    value = added(value, ins[came][here(at), :])
                out[base : base + count, :] = value

        results = self.line.call(body, shapes, f"round_{name}", (self.info, *arrays), small=1)
        sent = dict(zip(links, results[len(outs) :]))
        arrived = {link: swap(array, link) for link, array in sent.items()}
        for item in items:
            if item.now:
                item.came = (arrived[item.now[1]], item.came[1])
            item.kept = [
                (results[first], 0, rows) if where == "out" else (sent[where], first, rows) for where, first, rows in item.kept
            ]


def more_links():
    return [str(8 << bit) for bit in range((lax.axis_size("dp") // 8).bit_length() - 1)]


def steps_of(order, paired):
    first = [("pair" if link == "y" and paired else "half", link) for link in order[:3]]
    back = [("double", link) for link in order[2::-1] if not (link == "y" and paired)]
    return first + [("swap", link) for link in [order[3]] + more_links()] + back


def squares_kernel(mine, info, source, *refs):
    if mine:
        outs, rest = refs[:4], refs[4:]
        bit = scalar(info, "core")
    else:
        (own, *_), outs, vecs, rest = refs[:5], refs[5:9], refs[9:18], refs[18:]
        bit = 1 - scalar(info, "core")
    held, sems = rest[:4], rest[4]
    half = held[0].shape[0]
    copies = []
    for which, (out, buffer) in enumerate(zip(outs, held)):
        buffer[...] = source[which * half : (which + 1) * half, :].astype(F32)
        copies.append(pltpu.make_async_copy(buffer, out.at[at_half(bit, half), :], sems.at[which]))
        copies[-1].start()
    if not mine:
        total = added(own[4 * half :, :], source[4 * half :, :]).astype(F32)
        for at in range(8):
            rest[5 + at][...] = total[at, :]
        far = scalar(info, "me")
        row = total[8:9, :]
        for at in range(1, 4):
            row = jnp.where(far == at, total[8 + at : 9 + at, :], row)
        rest[13][...] = row[0, :]
        for at, vec in enumerate(vecs):
            copies.append(pltpu.make_async_copy(rest[5 + at], vec, sems.at[4 + at]))
            copies[-1].start()
    for copy in copies:
        copy.wait()


def mlp_grads_kernel(plan, info, *refs):
    ins, (gw_in, gw_out, whole) = refs[: 2 * len(plan)], refs[2 * len(plan) :]
    for which, (link, rows, own_at, came_at, base) in enumerate(plan):
        for bit, ref, at in ((scalar(info, link), ins[2 * which], own_at), (1 - scalar(info, link), ins[2 * which + 1], came_at)):
            whole[pl.ds(pl.multiple_of(base + bit * rows, 16), rows), :] = ref[at : at + rows, :]
    count = gw_in.shape[0]
    gw_in[...] = whole[:count, :].astype(F32)
    gw_out[...] = whole[count:, :].astype(F32)


def emit_kernel(resid, out_own, out_far, came_a, came_b, table, output):
    came = jnp.concatenate([came_a[...], came_b[...]], axis=0).astype(F32)
    total = resid[...] + added(out_own[0], out_far[0]).astype(F32) + came + vector(table, "b_out")
    output[...] = total.astype(BF16)


def from_behind(value, axis, steps):
    count = lax.axis_size(axis)
    leading, last = (max(0, -steps), min(count, count - steps))
    return lax.ppermute(value, axis, [(source, source + steps) for source in range(leading, last)])


def local(
    hidden,
    past_states,
    reset_flags,
    sample_positions,
    norm1_gain,
    norm1_shift,
    w_query,
    bias_query,
    w_key,
    w_value,
    bias_value,
    w_attn_out,
    bias_attn_out,
    norm2_gain,
    norm2_shift,
    w_mlp_in,
    bias_mlp_in,
    w_mlp_out,
    bias_mlp_out,
    cotangent,
):
    rows, width = hidden.shape[1], hidden.shape[2]
    size = past_states.shape[1]
    units = w_mlp_in.shape[1]
    assert rows == size and sample_positions.shape[2] == size
    pairs = width // (2 * HD)
    arr, cot = hidden[0], cotangent[0]
    half_bf = ((rows // 2, width), BF16)
    row_bf, row_f = ((rows, width), BF16), ((rows, width), F32)
    square_f, square_bf, vec_f = ((width, width), F32), ((width, width), BF16), ((8, width), F32)

    line = Line()
    info = scalar_array(reset_flags[0])
    half_w, third = width // 2, 2 * width // 3

    arrived = from_behind(arr, "mp", 1)
    (
        fit, table, cut_in, cut_out,
        w_mlp_in, w_mlp_out, arr, w_query, w_key, w_value, past, positions, w_attn_out, cot, *_
    ) = line.call(
        start_kernel,
        [((size, size), BF16), ((16, width), F32), ((half_w + 16, width), BF16), ((half_w, width), BF16)], "start",
        (
            info, w_mlp_in, w_mlp_out, norm1_gain, norm1_shift, bias_query, bias_value, bias_attn_out, norm2_gain,
            norm2_shift, bias_mlp_in, bias_mlp_out, arr, w_query, w_key, w_value, past_states[0], sample_positions[0],
            w_attn_out, cot,
        ),
        small=1, load=(1, 2, 12, 13, 14, 15, 16, 17, 18, 19) + tuple(range(3, 12)), far=(2, 3),
    )
    far_cut, far_out = swap(cut_in, "y"), swap(cut_out, "y")
    normed, q, k, v = line.call(front_kernel, [row_bf] * 4, "front", (arr, table, w_query, w_key, w_value))
    recalled, km, vm, often = line.call(
        memory_kernel, [row_bf] * 3 + [((8, size), F32)], "memory",
        (info, arrived, past, positions, table, fit, w_key, w_value), small=1,
    )

    calls = 3 if pairs % 3 == 0 else 1
    per = pairs // calls
    blocks = [pl.BlockSpec((rows, 2 * HD), lambda i, c=c: (0, i + c * per)) for c in range(calls)]
    e_blocks = [pl.BlockSpec((2, rows, rows + size), lambda i, c=c: (i + c * per, 0, 0)) for c in range(calls)]
    grid = (per,)
    shared = (q, k, v, km, vm, often)
    results = [((2 * pairs, rows, rows + size), BF16), row_bf, row_f]
    begun = ()
    for call in range(calls - 1):
        e, mixed, linv = line.blocks(
            attend_kernel, results, f"attend_{call}", shared + begun, grid,
            [blocks[call]] * 5 + [VMEM] + [ANY] * len(begun), [e_blocks[call]] + [blocks[call]] * 2,
            far=(0,), limit=20, aliases={6 + i: i for i in range(len(begun))}, there=(6,) if begun else (),
        )
        begun = (e, mixed, linv)
    e, mixed, linv, resid, *normed2 = line.blocks(
        attend_more_kernel, results + [row_f, half_bf, half_bf], "attend_more",
        shared + begun + (w_attn_out, table, arr), grid,
        [blocks[-1]] * 5 + [VMEM, ANY, pl.BlockSpec((rows, (calls - 1) * per * 2 * HD), lambda i: (0, 0)), ANY] + [VMEM] * 3,
        [e_blocks[-1]] + [blocks[-1]] * 2 + [VMEM] * 3,
        scratch=[pltpu.VMEM((rows, width), BF16)], aliases={6: 0, 7: 1, 8: 2}, far=(0,), limit=24, there=(6,),
    )
    normed2 += [swap(half, "core") for half in normed2]
    cot_sib = swap(cot, "core")
    far_in, far_out = hold(far_cut, line.last), hold(far_out, line.last)
    more_in, more_out = swap(far_in, "x"), swap(far_out, "z1")
    part, both = ((third, width), BF16), ((2, rows, width), BF16)
    bias_f, stacked = ((1, units), F32), ((width + units, width), BF16)
    out_own, gx_own, g_own, gb_own = line.call(
        mlp_kernel, [both, both, stacked, bias_f], "mlp_own",
        (*normed2, cot, cot_sib, w_mlp_in, table, w_mlp_out), limit=24,
        scratch=[pltpu.VMEM((2 * rows, units), BF16)] * 2,
    )
    w_in_far, w_out_far, b_far = line.call(
        far_weights_kernel, [((width, units), BF16), ((units, width), BF16), ((1, units), F32)], "far_weights",
        (info, far_in, more_in, far_out, more_out), small=1,
    )
    out_far, gx_far, g_far, gb_far = line.call(
        mlp_kernel, [both, both, stacked, bias_f], "mlp_far",
        (*normed2, cot, cot_sib, w_in_far, b_far, w_out_far), limit=20,
        scratch=[pltpu.VMEM((2 * rows, units), BF16)] * 2,
    )
    gx_keep, gx_send = line.call(merge_kernel, [row_bf] * 2, "merge", (gx_own, gx_far))
    gx_came = swap(gx_send, "core")
    rounds = Rounds(line, info)
    mlp_items, at = [], 0
    for order, count in MLP_PARTS:
        mlp_items.append(Item(steps_of(order, True), (g_own, at, count), (g_far, at, count)))
        at += count
    rounds.go("a", mlp_items)

    grad_mixed, grad_resid, gwo, vecs_mid, *out_send = line.call(
        middle_kernel, [row_bf, row_f, square_bf, vec_f, half_bf, half_bf], "middle",
        (gx_keep, gx_came, resid, cot, table, mixed, w_attn_out, out_own, out_far),
    )
    out_came = [swap(half, "core") for half in out_send]
    grads = ()
    back = 2 if pairs % 2 == 0 else 1
    per = pairs // back
    blocks = [pl.BlockSpec((rows, 2 * HD), lambda i, c=c: (0, i + c * per)) for c in range(back)]
    e_blocks = [pl.BlockSpec((2, rows, rows + size), lambda i, c=c: (i + c * per, 0, 0)) for c in range(back)]
    grid = (per,)
    for which in range(back):
        grads = line.blocks(
            attend_back_kernel, [row_bf] * 5, f"attend_back_{which}", (q, k, v, km, vm, e, linv, mixed, grad_mixed) + tuple(grads),
            grid, [blocks[which]] * 5 + [e_blocks[which]] + [blocks[which]] * 3 + [ANY] * len(grads),
            [blocks[which]] * 5, there=(5,), aliases={9 + i: i for i in range(len(grads))},
        )
        if which == 0:
            (output,) = line.call(emit_kernel, [row_bf], "emit", (resid, out_own, out_far, *out_came, table), far=(0,))
    dq, dk, dv, dkm, dvm = grads
    rounds.go("b", mlp_items)
    send, keep_a, keep_b, keep_c = line.call(
        weight_grads_kernel, [((2 * width, width), BF16), part, part, part], "weight_grads",
        (info, normed, recalled, dq, dk, dv, dkm, dvm, gwo), small=1, scratch=[pltpu.VMEM((width, width), BF16)],
    )
    core_came = swap(send, "core")
    attn_items = [
        Item(steps_of(order, False) + [("double", "core")], (kept, 0, third), now=("half", "core"), came=(core_came, which * third))
        for which, (order, kept) in enumerate(zip(ATTN_ORDERS, (keep_a, keep_b, keep_c)))
    ]
    grad_memory, vecs_rec = line.call(
        recall_back_kernel, [row_bf, vec_f], "recall_back", (info, dkm, dvm, w_key, w_value, fit, arrived), small=1,
    )
    handed = from_behind(grad_memory, "mp", -1)
    gn, vecs = line.call(
        project_back_kernel, [row_f, ((16, width), BF16)], "project_back",
        (info, arr, dq, dk, dv, dvm, w_query, w_key, w_value, vecs_mid, vecs_rec, gb_own, gb_far), small=1,
    )
    rounds.go("c", mlp_items + attn_items)
    (grad_hidden,) = line.call(
        last_kernel, [row_f], "last", (arr, table, gn, handed, grad_resid), far=(0,)
    )
    vec_item = Item([("swap", link) for link in ["z2"] + more_links() + ["x", "z1", "y", "core"]], (vecs, 0, 16))
    rounds.go("d", mlp_items + attn_items)
    for link in more_links():
        rounds.go("d" + link, mlp_items)
    rounds.go("e", mlp_items + attn_items)
    rounds.go("f", mlp_items + attn_items + [vec_item])
    for link in more_links():
        rounds.go("f" + link, attn_items + [vec_item])
    mlp_now = [(*item.kept[0], *item.came, item.now[1]) for item in mlp_items]
    rounds.go("g", attn_items + [vec_item])
    plan, operands, at = [], [], 0
    for own, first, count, came, came_at, link in mlp_now:
        plan.append((link, count, first, came_at, at))
        operands += [own, came]
        at += 2 * count
    gw_in, gw_out = line.call(
        lambda *refs: mlp_grads_kernel(plan, *refs), [((width, units), F32), ((units, width), F32)], "mlp_grads",
        (info, *operands), small=1, far=(0, 1), scratch=[pltpu.VMEM((width + units, width), BF16)], limit=24,
    )
    rounds.go("h", attn_items + [vec_item])
    rounds.go("i", attn_items + [vec_item])
    rounds.go("k", attn_items + [vec_item])
    last_own, (last_came, _) = vec_item.kept[0][0], vec_item.came
    buffers = [pltpu.VMEM((half_w, width), F32)] * 4 + [pltpu.SemaphoreType.DMA((13,))]
    squares = line.start(
        lambda *refs: squares_kernel(True, *refs), [square_f] * 4, "squares_own", (info, last_own), (1,), [SMALL, VMEM],
        [HBM] * 4, buffers, far=(0, 1, 2, 3), limit=16,
    )
    gwq, gwk, gwv, gwo, *vecs = line.start(
        lambda *refs: squares_kernel(False, *refs), [square_f] * 4 + [((width,), F32)] * 9, "squares_came",
        (info, last_came, last_own, *squares), (1,), [SMALL, VMEM, VMEM] + [HBM] * 4, [HBM] * 13,
        buffers + [pltpu.VMEM((width,), F32)] * 9, far=tuple(range(13)), limit=16, there=(3, 4, 5, 6), aliases={3 + i: i for i in range(4)},
    )
    return (
        output[None],
        grad_hidden[None],
        vecs[0],
        vecs[1],
        gwq,
        vecs[2],
        gwk,
        gwv,
        vecs[3],
        gwo,
        vecs[4],
        vecs[5],
        vecs[6],
        gw_in,
        vecs[8],
        gw_out,
        vecs[7],
    )


def solution(mesh):
    rows = P("dp", "mp", None)
    placed = (rows, P("dp", None, None), P("dp"), rows) + (P(),) * 11
    placed += (P(None, "mp"), P("mp"), P("mp", None), P(), rows)
    return jax.shard_map(
        local,
        mesh=mesh,
        in_specs=placed,
        out_specs=(rows, rows) + (P(),) * 11 + (P(None, "mp"), P("mp"), P("mp", None), P()),
        check_vma=False,
    )
```

```python
import math

import jax
import jax.numpy as jnp
from jax import lax
from jax.experimental import pallas as pl
from jax.experimental.pallas import tpu as pltpu
from jax.sharding import PartitionSpec as P

HD = 64
NORM_EPSILON = 1e-05
RIDGE_WEIGHT = 0.1
NOTHING = -1e30
GELU_SLOPE = math.sqrt(2.0 / math.pi)
GELU_CUBE = 0.044715
F32 = jnp.float32
BF16 = jnp.bfloat16
MEBI = 1 << 20


def mm(left, right):
    return jnp.dot(left, right, preferred_element_type=F32)


def mt(left, right):
    return lax.dot_general(left, right, (((1,), (1,)), ((), ())), preferred_element_type=F32)


def tm(left, right):
    return lax.dot_general(left, right, (((0,), (0,)), ((), ())), preferred_element_type=F32)


def column_sum(values):
    return jnp.sum(values, axis=0, keepdims=True)


def normalized(values):
    row_mean = jnp.mean(values, axis=-1, keepdims=True)
    centered = values - row_mean
    row_var = jnp.mean(centered * centered, axis=-1, keepdims=True)
    inverse = lax.rsqrt(row_var + NORM_EPSILON)
    return centered * inverse, inverse


def norm_back(xhat, inverse, incoming, gain):
    g = incoming * gain
    mean_g = jnp.mean(g, axis=-1, keepdims=True)
    mean_gx = jnp.mean(g * xhat, axis=-1, keepdims=True)
    return inverse * (g - mean_g - xhat * mean_gx)


SMALL = pl.BlockSpec(memory_space=pltpu.SMEM)
VMEM = pl.BlockSpec(memory_space=pltpu.VMEM)
ANY = pl.BlockSpec(memory_space=pl.ANY)
HBM = pl.BlockSpec(memory_space=pltpu.HBM)


class Arriving:
    def __init__(self, source, held, sem):
        self.held, self.copy = held, pltpu.make_async_copy(source, held, sem)
        self.shape, self.dtype = held.shape, held.dtype
        self.here = False
        self.copy.start()

    def wait(self):
        if not self.here:
            self.copy.wait()
            self.here = True
        return self.held

    @property
    def at(self):
        return self.wait().at

    def __getitem__(self, index):
        return self.wait()[index]


class Leaving:
    def __init__(self, target, held, sem):
        self.held, self.copy = held, pltpu.make_async_copy(held, target, sem)
        self.shape, self.dtype = held.shape, held.dtype
        self.gone = False

    def leave(self):
        if not self.gone:
            self.copy.start()
            self.gone = True

    def __getitem__(self, index):
        return self.held[index]

    def __setitem__(self, index, value):
        self.held[index] = value
        if index is Ellipsis:
            self.leave()


class Line:
    def __init__(self):
        self.last = None

    def start(self, body, outs, name, operands, grid, in_specs, out_specs, scratch, after=(), aliases=None, far=(), limit=32, there=()):
        waits = list(after) + ([] if self.last is None else [self.last])
        operands = [pltpu.with_memory_space_constraint(o, pltpu.HBM) if i in there else o for i, o in enumerate(operands)]
        known, gone = len(operands), len(operands) + len(waits)
        results = pl.pallas_call(
            lambda *refs: body(*refs[:known], *refs[gone : gone + len(outs)], *refs[gone + len(outs) + 1 :]),
            out_shape=[(pltpu.HBM if i in far else pltpu.VMEM)(shape, dtype) for i, (shape, dtype) in enumerate(outs)]
            + [pltpu.VMEM((8, 128), F32)],
            grid=grid,
            in_specs=list(in_specs) + [ANY] * len(waits),
            out_specs=list(out_specs) + [VMEM],
            scratch_shapes=list(scratch),
            input_output_aliases=aliases or {},
            compiler_params=pltpu.CompilerParams(vmem_limit_bytes=limit * MEBI),
            cost_estimate=pl.CostEstimate(flops=0, bytes_accessed=0, transcendentals=0),
            name=name,
        )(*operands, *waits)
        *results, self.last = results
        return results

    def blocks(self, body, outs, name, operands, grid, in_specs, out_specs, scratch=(), **more):
        return self.start(body, outs, name, operands, grid, in_specs, out_specs, scratch, **more)

    def call(self, body, outs, name, operands, small=0, load=(), far=(), scratch=(), after=(), limit=16):
        outs = list(outs) + [(operands[i].shape, operands[i].dtype) for i in load]
        own, kept = len(scratch), len(outs) - len(load)
        in_specs = [SMALL if i < small else HBM if i in load else VMEM for i in range(len(operands))]
        out_specs = [HBM if i in far else VMEM for i in range(len(outs))]
        held = [pltpu.VMEM(*outs[i]) for i in far]
        sems = [pltpu.SemaphoreType.DMA((len(far) + len(load),))] if far or load else []

        def run(*refs):
            ins, targets, rest = refs[: len(operands)], refs[len(operands) : len(operands) + len(outs)], refs[len(operands) + len(outs) :]
            mine, buffers, sem = rest[:own], rest[own:], rest[-1] if sems else None
            ins, targets = list(ins), list(targets)
            for slot, i in enumerate(load):
                ins[i] = Arriving(ins[i], targets[kept + slot], sem.at[len(far) + slot])
            for slot, i in enumerate(far):
                targets[i] = Leaving(targets[i], buffers[slot], sem.at[slot])
            body(*ins, *targets[:kept], *mine)
            for i in load:
                ins[i].wait()
            for i in far:
                targets[i].leave()
            for i in far:
                targets[i].copy.wait()

        return self.start(
            run, outs, name, operands, (1,), in_specs, out_specs, list(scratch) + held + sems, after, far=far, limit=limit,
            there=tuple(load),
        )


def hold(value, *until):
    return lax.optimization_barrier((value,) + until)[0]


def at_half(bit, count):
    return pl.ds(pl.multiple_of(bit * count, count), count)


def fit_at_positions(size, fit_ref):
    half = size // 2
    spread = 1.0 / size
    row = lax.broadcasted_iota(jnp.int32, (half, half), 0)
    col = lax.broadcasted_iota(jnp.int32, (half, half), 1)
    eye = jnp.where(row == col, 1.0, 0.0).astype(F32)
    flip = jnp.where(row + col == half - 1, 1.0, 0.0).astype(BF16)

    def design(columns):
        apart = (row.astype(F32) + 0.5) / size - (columns.astype(F32) + 0.5) / size
        return jnp.exp(-(apart * apart) / (2.0 * spread * spread))

    def pieces(value):
        high = value.astype(BF16)
        return high, (value - high.astype(F32)).astype(BF16)

    def exact(left, right):
        (left_high, left_low), (right_high, right_low) = pieces(left), pieces(right)
        return mm(left_high, right_high) + (mm(left_high, right_low) + mm(left_low, right_high))

    def full(left, right):
        return jnp.dot(left, right, precision=lax.Precision.HIGHEST, preferred_element_type=F32)

    direct, mirrored = design(col), design(size - 1 - col)
    brackets, guesses = [], []
    for part in (direct + mirrored, direct - mirrored):
        bracket = full(part, part) + RIDGE_WEIGHT * eye
        low = bracket.astype(BF16)
        brackets.append(bracket)
        guesses.append(2.39060839 * eye - 0.96134588 * bracket + 0.09859958 * mm(low, low))
    for step in range(6):
        for which in range(2):
            bracket, guess = brackets[which], guesses[which]
            if step < 4:
                low = guess.astype(BF16)
                left = 2.0 * eye - mm(bracket.astype(BF16), low)
                guesses[which] = mm(low, left.astype(BF16))
            else:
                guesses[which] = exact(guess, 2.0 * eye - exact(bracket, guess))
    even, odd = (eye - RIDGE_WEIGHT * guess for guess in guesses)
    inner = (0.5 * (even + odd)).astype(BF16)
    outer = (0.5 * (even - odd)).astype(BF16)
    fit_ref[0:half, 0:half] = inner
    fit_ref[0:half, half:size] = mm(outer, flip).astype(BF16)
    fit_ref[half:size, 0:half] = mm(flip, outer).astype(BF16)
    fit_ref[half:size, half:size] = mm(flip, mm(inner, flip).astype(BF16)).astype(BF16)


VECTORS = ("gain1", "shift1", "b_q", "b_v", "b_o", "gain2", "shift2", "b_in", "b_out")


def vector(table, name):
    at = VECTORS.index(name)
    return table[at : at + 1, :]


def start_kernel(info, w_in, w_out, *refs):
    vectors, (fit, table, cut_in, cut_out) = refs[: len(VECTORS)], refs[-4:]
    fit_at_positions(fit.shape[0], fit)
    table[...] = jnp.zeros_like(table)
    for at, value in enumerate(vectors):
        table[at, :] = value[...]
    count = cut_out.shape[0]
    cut_in[0:count, :] = w_in[at_half(scalar(info, "x"), count), :]
    bias, pieces = vector(table, "b_in"), []
    for _ in range(3):
        pieces.append(bias.astype(BF16))
        bias = bias - pieces[-1].astype(F32)
    cut_in[count:, :] = jnp.concatenate(pieces + [jnp.zeros((13, table.shape[1]), BF16)], axis=0)
    cut_in.leave()
    cut_out[...] = w_out[at_half(scalar(info, "z1"), count), :]


def front_kernel(hidden, table, wq, wk, wv, normed, q, k, v):
    xhat, _ = normalized(hidden[...].astype(F32))
    low = (xhat * vector(table, "gain1") + vector(table, "shift1")).astype(BF16)
    normed[...] = low
    scale = 1.0 / math.sqrt(HD)
    q[...] = (mm(low, wq[...]) + vector(table, "b_q")).astype(BF16) * jnp.asarray(scale, BF16)
    k[...] = mm(low, wk[...]).astype(BF16)
    v[...] = (mm(low, wv[...]) + vector(table, "b_v")).astype(BF16)


def memory_kernel(info, arrived, past, positions, table, fit, wk, wv, recalled, km, vm, often):
    size = fit.shape[0]
    xhat, _ = normalized(arrived[...].astype(F32))
    before = xhat * vector(table, "gain1") + vector(table, "shift1")
    kept = past[...].astype(F32) * (1 - scalar(info, "reset")).astype(F32)
    earlier = jnp.where(scalar(info, "first") > 0, kept, before).astype(BF16)
    low = mm(fit[...], earlier).astype(BF16)
    recalled[...] = low
    km[...] = mm(low, wk[...]).astype(BF16)
    vm[...] = (mm(low, wv[...]) + vector(table, "b_v")).astype(BF16)
    place = lax.broadcasted_iota(jnp.int32, (size, positions.shape[1]), 0)
    hit = jnp.where(place == positions[...], 1.0, 0.0).astype(BF16)
    count = mt(jnp.ones((8, positions.shape[1]), BF16), hit)
    often[...] = jnp.where(count > 0.5, jnp.log(jnp.maximum(count, 1.0)), NOTHING)


def attend_pair(q, k, v, km, vm, often, e, mixed, linv):
    rows = q.shape[0]
    half = rows // 2
    lane = lax.broadcasted_iota(jnp.int32, (1, 2 * HD), 1)
    row = lax.broadcasted_iota(jnp.int32, (half, half), 0)
    col = lax.broadcasted_iota(jnp.int32, (half, half), 1)
    log_count = often[0:1, :]
    units = [(part, head) for part in range(2) for head in range(2)]
    scores = {}
    for part, head in units:
        here = slice(part * half, (part + 1) * half)
        mine = (lane >= head * HD) & (lane < (head + 1) * HD)
        query = jnp.where(mine, q[here, :], jnp.zeros((), BF16))
        near = mt(query, k[0 : (part + 1) * half, :])
        far = mt(query, km[...]) + log_count
        edge = jnp.where(col > row, NOTHING, near[:, part * half :])
        top = jnp.maximum(jnp.max(edge, axis=-1, keepdims=True), jnp.max(far, axis=-1, keepdims=True))
        if part:
            top = jnp.maximum(top, jnp.max(near[:, : part * half], axis=-1, keepdims=True))
        scores[part, head] = (near, edge, far, top)
    for part in range(2):
        here = slice(part * half, (part + 1) * half)
        seen = (part + 1) * half
        results = []
        for head in range(2):
            near, edge, far, top = scores[part, head]
            edge = jnp.exp(edge - top)
            far = jnp.exp(far - top)
            total = jnp.sum(edge, axis=-1, keepdims=True) + jnp.sum(far, axis=-1, keepdims=True)
            edge_low, far_low = edge.astype(BF16), far.astype(BF16)
            e[head, here, part * half : seen] = edge_low
            e[head, here, rows:] = far_low
            out = mm(edge_low, v[part * half : seen, :]) + mm(far_low, vm[...])
            if part:
                start = jnp.exp(near[:, : part * half] - top)
                total = total + jnp.sum(start, axis=-1, keepdims=True)
                start_low = start.astype(BF16)
                e[head, here, 0 : part * half] = start_low
                out = out + mm(start_low, v[0 : part * half, :])
            inverse = 1.0 / total
            results.append((out * inverse, inverse))
        first = lane < HD
        mixed[here, :] = jnp.where(first, results[0][0], results[1][0]).astype(BF16)
        linv[here, :] = jnp.where(first, results[0][1], results[1][1])


def attend_kernel(q, k, v, km, vm, often, *refs):
    e, mixed, linv = refs[-3:]
    attend_pair(q, k, v, km, vm, often, e, mixed, linv)


def attend_more_kernel(
    q, k, v, km, vm, often, e_done, mixed_done, linv_done, wo, table, hidden,
    e, mixed, linv, resid, normed2_a, normed2_b, every,
):
    step, rows = pl.program_id(0), q.shape[0]
    attend_pair(q, k, v, km, vm, often, e, mixed, linv)
    done, block = mixed_done.shape[1], mixed.shape[1]
    every[:, pl.ds(pl.multiple_of(done + step * block, block), block)] = mixed[...]

    @pl.when(step == pl.num_programs(0) - 1)
    def _():
        every[:, 0:done] = mixed_done[...]
        total = hidden[...].astype(F32) + mm(every[...], wo[...]) + vector(table, "b_o")
        resid[...] = total
        xhat, _ = normalized(total)
        normed2 = (xhat * vector(table, "gain2") + vector(table, "shift2")).astype(BF16)
        normed2_a[...] = normed2[: rows // 2]
        normed2_b[...] = normed2[rows // 2 :]


def mlp_block(x, cot, w_in, b_in, w_out):
    pre = mm(x, w_in) + b_in
    square = pre * pre
    bend = jnp.tanh(GELU_SLOPE * pre * (1.0 + GELU_CUBE * square))
    act = (0.5 * pre * (1.0 + bend)).astype(BF16)
    slope = 0.5 * (1.0 + bend) + (0.5 * GELU_SLOPE) * pre * (1.0 - bend * bend) * (1.0 + 3.0 * GELU_CUBE * square)
    gpre = (mt(cot, w_out) * slope).astype(BF16)
    return mm(act, w_out), mt(gpre, w_in), act, gpre


def mlp_kernel(xa, xb, xc, xd, cot0, cot1, w_in, b_in, w_out, out, gx, grads, g_bias, acts, gpres):
    block, width, units = xa.shape[0], xa.shape[1], acts.shape[1]
    bias = b_in[...] if b_in.shape[0] == 1 else vector(b_in, "b_in")
    parts = []
    for which, x in enumerate((xa, xb, xc, xd)):
        here, there = slice(which % 2 * block, (which % 2 + 1) * block), slice(which * block, (which + 1) * block)
        cot = (cot0, cot1)[which // 2]
        o, g, act, gpre = mlp_block(x[...], cot[here, :], w_in[...], bias, w_out[...])
        out[which // 2, here, :], gx[which // 2, here, :] = o.astype(BF16), g.astype(BF16)
        acts[there, :] = act
        gpres[there, :] = gpre
        parts.append((x, there))
    total = tm(xa[...], gpres[0:block, :])
    for x, there in parts[1:]:
        total = total + tm(x[...], gpres[there, :])
    grads[0:width, :] = total.astype(BF16)
    half = 2 * block
    grads[width : width + units, :] = (tm(acts[:half, :], cot0[...]) + tm(acts[half:, :], cot1[...])).astype(BF16)
    g_bias[...] = column_sum(gpres[...].astype(F32))


def merge_kernel(gx, gx_far, keep_gx, send_gx):
    keep_gx[...] = added(gx[0], gx_far[0])
    send_gx[...] = added(gx[1], gx_far[1])


def middle_kernel(
    gx, gx_more, resid, cot, table, mixed, wo, out_own, out_far, grad_mixed, grad_resid, gwo, vecs,
    send_a, send_b
):
    half = send_a.shape[0]
    send_a[...] = added(out_own[1, 0:half, :], out_far[1, 0:half, :])
    send_b[...] = added(out_own[1, half:, :], out_far[1, half:, :])
    xhat, inverse = normalized(resid[...])
    n = gx[...].astype(F32) + gx_more[...].astype(F32)
    cot_full = cot[...].astype(F32)
    total = cot_full + norm_back(xhat, inverse, n, vector(table, "gain2"))
    grad_resid[...] = total
    low = total.astype(BF16)
    grad_mixed[...] = mt(low, wo[...]).astype(BF16)
    gwo[...] = tm(mixed[...], low).astype(BF16)
    vecs[...] = jnp.concatenate(
        [
            column_sum(low.astype(F32)),
            column_sum(n * xhat),
            column_sum(n),
            column_sum(cot_full),
            jnp.zeros((4, n.shape[1]), F32),
        ],
        axis=0,
    )


def attend_back_kernel(q, k, v, km, vm, e, linv, mixed, gmix, *refs):
    dq, dk, dv, dkm, dvm = refs[-5:]
    rows = q.shape[0]
    half = rows // 2
    lane = lax.broadcasted_iota(jnp.int32, (1, 2 * HD), 1)
    scale = 1.0 / math.sqrt(HD)
    sums = {}

    def add(name, value):
        sums[name] = sums[name] + value if name in sums else value

    for part in range(2):
        here = slice(part * half, (part + 1) * half)
        seen = (part + 1) * half
        grad = gmix[here, :].astype(F32) * linv[here, :]
        product = grad * mixed[here, :].astype(F32)
        queries = []
        for head in range(2):
            mine = (lane >= head * HD) & (lane < (head + 1) * HD)
            query = jnp.where(mine, q[here, :], jnp.zeros((), BF16))
            grad_low = jnp.where(mine, grad, 0.0).astype(BF16)
            dot = jnp.sum(jnp.where(mine, product, 0.0), axis=-1, keepdims=True)
            near_e, far_e = e[head, here, 0:seen], e[head, here, rows:]
            near = (near_e.astype(F32) * (mt(grad_low, v[0:seen, :]) - dot)).astype(BF16)
            far = (far_e.astype(F32) * (mt(grad_low, vm[...]) - dot)).astype(BF16)
            queries.append(mm(near, k[0:seen, :]) + mm(far, km[...]))
            dk_near, dv_near = tm(query, near), tm(grad_low, near_e)
            for block in range(part + 1):
                where = slice(block * half, (block + 1) * half)
                add(("k", block), dk_near[:, where])
                add(("v", block), dv_near[:, where])
            add("km", tm(query, far))
            add("vm", tm(grad_low, far_e))
        dq[here, :] = (jnp.where(lane < HD, queries[0], queries[1]) * scale).astype(BF16)
    for block in range(2):
        where = slice(block * half, (block + 1) * half)
        dk[where, :] = sums["k", block].T.astype(BF16)
        dv[where, :] = sums["v", block].T.astype(BF16)
    dkm[...] = sums["km"].T.astype(BF16)
    dvm[...] = sums["vm"].T.astype(BF16)


def recall_back_kernel(info, dkm, dvm, wk, wv, fit, arrived, grad_memory, vecs):
    grad_recalled = (mt(dkm[...], wk[...]) + mt(dvm[...], wv[...])).astype(BF16)
    handed = tm(fit[...], grad_recalled).astype(BF16)
    grad_memory[...] = handed
    xhat, _ = normalized(arrived[...].astype(F32))
    n = jnp.where(scalar(info, "first") > 0, 0.0, handed.astype(F32))
    vecs[...] = jnp.concatenate([column_sum(n * xhat), column_sum(n), jnp.zeros((6, n.shape[1]), F32)], axis=0)


def weight_grads_kernel(info, normed, recalled, dq, dk, dv, dkm, dvm, gwo, send, *refs):
    low, rec = normed[...], recalled[...]
    *parts, whole = refs
    half = whole.shape[0] // 2
    core = scalar(info, "core")
    grads = (
        lambda: tm(low, dq[...]),
        lambda: tm(low, dk[...]) + tm(rec, dkm[...]),
        lambda: tm(low, dv[...]) + tm(rec, dvm[...]),
        None,
    )
    for which, grad in enumerate(grads):
        source = gwo
        if grad is not None:
            whole[...] = grad().astype(BF16)
            source = whole
        start = begin = 0
        for part in parts:
            piece = part.shape[0] // 8
            for first in range(2):
                at = (4 * first + which) * piece
                send[begin + at : begin + at + piece, :] = source[
                    pl.ds(pl.multiple_of((1 - core) * half + start, 16), piece), :
                ]
                part[at : at + piece, :] = source[pl.ds(pl.multiple_of(core * half + start, 16), piece), :]
                start += piece
            begin += part.shape[0]


def project_back_kernel(info, hidden, dq, dk, dv, dvm, wq, wk, wv, vecs_mid, vecs_rec, gb_own, gb_far, gn, vecs):
    width = hidden.shape[1]
    n = mt(dq[...], wq[...]) + mt(dk[...], wk[...]) + mt(dv[...], wv[...])
    gn[...] = n
    xhat, _ = normalized(hidden[...].astype(F32))
    shard = lax.broadcasted_iota(jnp.int32, (4, 1), 0)
    bias_rows = jnp.where(shard == scalar(info, "me"), gb_own[...], 0.0) + jnp.where(shard == scalar(info, "far"), gb_far[...], 0.0)
    vecs[...] = jnp.concatenate(
        [
            column_sum(n * xhat) + vecs_rec[0:1, :],
            column_sum(n) + vecs_rec[1:2, :],
            column_sum(dq[...].astype(F32)),
            column_sum(dv[...].astype(F32)) + column_sum(dvm[...].astype(F32)),
            vecs_mid[0:4, :],
            bias_rows,
            jnp.zeros((4, width), F32),
        ],
        axis=0,
    ).astype(BF16)


def last_kernel(hidden, table, gn, handed, grad_resid, grad_hidden):
    xhat, inverse = normalized(hidden[...].astype(F32))
    n = gn[...] + handed[...].astype(F32)
    grad_hidden[...] = grad_resid[...] + norm_back(xhat, inverse, n, vector(table, "gain1"))


def added(left, right):
    return (left.astype(F32) + right.astype(F32)).astype(BF16)


def join_kernel(plan, info, *refs):
    for which, link in enumerate(plan):
        own, came, out = refs[2 * which], refs[2 * which + 1], refs[2 * len(plan) + which]
        count = out.shape[0] // 2
        out[at_half(scalar(info, link), count), :] = own[0:count, :]
        out[at_half(1 - scalar(info, link), count), :] = came[0:count, :]


def far_weights_kernel(info, in_own, in_came, out_own, out_came, w_in, w_out, b_in):
    join_kernel(("x", "z1"), info, in_own, in_came, out_own, out_came, w_in, w_out)
    pieces = in_own[in_own.shape[0] - 16 :, :].astype(F32)
    b_in[...] = pieces[0:1] + pieces[1:2] + pieces[2:3]


MLP_PARTS = (
    (("y", "x", "z2", "z1"), 384), (("y", "z1", "x", "z2"), 128), (("x", "y", "z2", "z1"), 128),
    (("x", "z1", "y", "z2"), 384), (("z1", "y", "x", "z2"), 384), (("z1", "x", "y", "z2"), 128),
)
ATTN_PARTS = ((("y", "z1", "x", "z2"), 512), (("x", "y", "z1", "z2"), 512), (("z1", "x", "y", "z2"), 512))
AXES = {"core": ("mp", 1), "y": ("mp", 2), "x": ("dp", 1), "z1": ("dp", 2), "z2": ("dp", 4)}


def swap(value, link):
    axis, mask = AXES[link] if link in AXES else ("dp", int(link))
    return lax.ppermute(value, axis, [(i, i ^ mask) for i in range(lax.axis_size(axis))])


def bit_of(link):
    axis, mask = AXES[link]
    return (lax.axis_index(axis) // mask) % 2


SCALAR = {"core": 0, "y": 1, "x": 2, "z1": 3, "z2": 4, "me": 5, "far": 6, "first": 7, "reset": 8}


def scalar_array(reset):
    bit = {link: bit_of(link) for link in AXES}
    me = lax.axis_index("mp")
    values = dict(bit, me=me, far=me ^ 2, first=me == 0, reset=reset)
    row = lax.broadcasted_iota(jnp.int32, (1, 16), 1)
    packed = jnp.zeros((1, 16), jnp.int32)
    for name, value in values.items():
        packed = jnp.where(row == SCALAR[name], jnp.asarray(value, jnp.int32), packed)
    return packed


def scalar(info, name):
    return info[0, SCALAR[name]]


class Item:
    def __init__(self, steps, *kept, now=None, came=None):
        self.steps, self.kept, self.now, self.came = list(steps), list(kept), now, came


class Rounds:
    def __init__(self, line, info):
        self.line, self.info = line, info

    def go(self, name, items, mirror=False):
        arrays, sends, outs, jobs = [], {}, [], []

        def slot(array):
            for which, known in enumerate(arrays):
                if known is array:
                    return which
            arrays.append(array)
            return len(arrays) - 1

        for item in items:
            kind, link = item.now or ("start", None)
            came, at = (slot(item.came[0]), item.came[1]) if link else (None, 0)
            sources = []
            for array, first, rows in item.kept:
                sources.append((slot(array), first, came, at, rows, kind, link))
                at += rows
            rows = item.kept[0][2] * (2 if kind == "double" else 1)
            step = item.steps.pop(0) if item.steps else None
            sent = sends.setdefault(step[1], [0]) if step else None
            if step is None:
                jobs.append((sources[0], "all", None, len(outs), 0, rows))
                item.kept = [("out", len(outs), rows)]
                outs.append(rows)
            elif step[0] in ("swap", "double"):
                jobs.append((sources[0], "all", None, step[1], sent[0], rows))
                item.came, item.kept = (None, sent[0]), [(step[1], sent[0], rows)]
                sent[0] += rows
                if mirror:
                    again = sends.setdefault("core", [0])
                    jobs.append((sources[0], "all", None, "core", again[0], rows))
                    again[0] += rows
            elif step[0] == "pair":
                jobs.append((sources[0], "all", None, len(outs), 0, rows))
                jobs.append((sources[1], "all", None, step[1], sent[0], rows))
                item.came, item.kept = (None, sent[0]), [("out", len(outs), rows)]
                sent[0] += rows
                outs.append(rows)
            else:
                half, kept = rows // 2, []
                item.came = (None, sent[0])
                for source in sources:
                    jobs.append((source, "mine", step[1], len(outs), 0, half))
                    jobs.append((source, "other", step[1], step[1], sent[0], half))
                    kept.append(("out", len(outs), half))
                    sent[0] += half
                    outs.append(half)
                item.kept = kept
            item.now = step
        links = list(sends)
        width = arrays[0].shape[1]
        shapes = [((rows, width), BF16) for rows in outs] + [((sends[link][0], width), BF16) for link in links]

        def body(info, *refs):
            ins, results = refs[: len(arrays)], refs[len(arrays) :]
            for (kept, first, came, at, rows, kind, over), what, link, target, base, count in jobs:
                out = results[len(outs) + links.index(target) if isinstance(target, str) else target]
                if kind == "double":
                    for bit, ref, start in ((scalar(info, over), kept, first), (1 - scalar(info, over), came, at)):
                        out[pl.ds(pl.multiple_of(base + bit * rows, 16), rows), :] = ins[ref][start : start + rows, :]
                    continue
                start = 0
                if what != "all":
                    bit = scalar(info, link)
                    start = (bit if what == "mine" else 1 - bit) * count

                def here(base):
                    if what == "all":
                        return slice(base, base + count)
                    return pl.ds(pl.multiple_of(base + start, 16), count)

                value = ins[kept][here(first), :]
                if kind != "start":
                    value = added(value, ins[came][here(at), :])
                out[base : base + count, :] = value

        results = self.line.call(body, shapes, f"round_{name}", (self.info, *arrays), small=1)
        sent = dict(zip(links, results[len(outs) :]))
        arrived = {link: swap(array, link) for link, array in sent.items()}
        self.mirror = arrived.get("core")
        for item in items:
            if item.now:
                item.came = (arrived[item.now[1]], item.came[1])
            item.kept = [
                (results[first], 0, rows) if where == "out" else (sent[where], first, rows) for where, first, rows in item.kept
            ]


def more_links():
    return [str(8 << bit) for bit in range((lax.axis_size("dp") // 8).bit_length() - 1)]


def steps_of(order, paired):
    first = [("pair" if link == "y" and paired else "half", link) for link in order[:3]]
    back = [("double", link) for link in order[2::-1] if not (link == "y" and paired)]
    return first + [("swap", link) for link in [order[3]] + more_links()] + back


def squares_kernel(plan, count, skip, vectors, info, *refs):
    ins, rest = refs[:count], refs[count + skip :]
    outs, rest = rest[:4], rest[4:]
    vecs, rest = (rest[:9], rest[9:]) if vectors else ((), rest)
    buffers, sems = rest[: 4 * len(plan)], rest[4 * len(plan)]
    copies = []

    def leave(buffer, target):
        copies.append(pltpu.make_async_copy(buffer, target, sems.at[len(copies)]))
        copies[-1].start()

    half = outs[0].shape[0] // 2
    for block, (part, this_core, this_half, array, first, start, piece) in enumerate(plan):
        core, bit = scalar(info, "core"), scalar(info, ATTN_PARTS[part][0][0])
        core, bit = core if this_core else 1 - core, bit if this_half else 1 - bit
        at = pl.ds(pl.multiple_of(core * half + start + bit * piece, 16), piece)
        for which, out in enumerate(outs):
            buffer = buffers[4 * block + which]
            buffer[...] = ins[array][first + which * piece : first + (which + 1) * piece, :].astype(F32)
            leave(buffer, out.at[at, :])
    if vectors:
        rows = [ins[array][first : first + 16, :].astype(F32) for array, first in vectors]
        total = (rows[0] + rows[1]) + (rows[2] + rows[3])
        me, row = scalar(info, "me"), total[8:9, :]
        for at in range(1, 4):
            row = jnp.where(me == at, total[8 + at : 9 + at, :], row)
        held = rest[4 * len(plan) + 1 :]
        for at, (buffer, out) in enumerate(zip(held, vecs)):
            buffer[...] = total[at, :] if at < 8 else row[0, :]
            leave(buffer, out)
    for copy in copies:
        copy.wait()


def mlp_grads_kernel(plan, info, *refs):
    ins, (gw_in, gw_out, whole) = refs[: 2 * len(plan)], refs[2 * len(plan) :]
    for which, (link, rows, own_at, came_at, base) in enumerate(plan):
        for bit, ref, at in ((scalar(info, link), ins[2 * which], own_at), (1 - scalar(info, link), ins[2 * which + 1], came_at)):
            whole[pl.ds(pl.multiple_of(base + bit * rows, 16), rows), :] = ref[at : at + rows, :]
    count = gw_in.shape[0]
    gw_in[...] = whole[:count, :].astype(F32)
    gw_out[...] = whole[count:, :].astype(F32)


def emit_kernel(resid, out_own, out_far, came_a, came_b, table, output):
    came = jnp.concatenate([came_a[...], came_b[...]], axis=0).astype(F32)
    total = resid[...] + added(out_own[0], out_far[0]).astype(F32) + came + vector(table, "b_out")
    output[...] = total.astype(BF16)


def from_behind(value, axis, steps):
    count = lax.axis_size(axis)
    leading, last = (max(0, -steps), min(count, count - steps))
    return lax.ppermute(value, axis, [(source, source + steps) for source in range(leading, last)])


def local(
    hidden,
    past_states,
    reset_flags,
    sample_positions,
    norm1_gain,
    norm1_shift,
    w_query,
    bias_query,
    w_key,
    w_value,
    bias_value,
    w_attn_out,
    bias_attn_out,
    norm2_gain,
    norm2_shift,
    w_mlp_in,
    bias_mlp_in,
    w_mlp_out,
    bias_mlp_out,
    cotangent,
):
    rows, width = hidden.shape[1], hidden.shape[2]
    size = past_states.shape[1]
    units = w_mlp_in.shape[1]
    assert rows == size and sample_positions.shape[2] == size
    pairs = width // (2 * HD)
    arr, cot = hidden[0], cotangent[0]
    half_bf = ((rows // 2, width), BF16)
    row_bf, row_f = ((rows, width), BF16), ((rows, width), F32)
    square_f, square_bf, vec_f = ((width, width), F32), ((width, width), BF16), ((8, width), F32)

    line = Line()
    info = scalar_array(reset_flags[0])
    half_w, third = width // 2, 2 * width // 3

    arrived = from_behind(arr, "mp", 1)
    (
        fit, table, cut_in, cut_out,
        w_mlp_in, w_mlp_out, arr, w_query, w_key, w_value, past, positions, w_attn_out, cot, *_
    ) = line.call(
        start_kernel,
        [((size, size), BF16), ((16, width), F32), ((half_w + 16, width), BF16), ((half_w, width), BF16)], "start",
        (
            info, w_mlp_in, w_mlp_out, norm1_gain, norm1_shift, bias_query, bias_value, bias_attn_out, norm2_gain,
            norm2_shift, bias_mlp_in, bias_mlp_out, arr, w_query, w_key, w_value, past_states[0], sample_positions[0],
            w_attn_out, cot,
        ),
        small=1, load=(1, 2, 12, 13, 14, 15, 16, 17, 18, 19) + tuple(range(3, 12)), far=(2, 3),
    )
    far_cut, far_out = swap(cut_in, "y"), swap(cut_out, "y")
    normed, q, k, v = line.call(front_kernel, [row_bf] * 4, "front", (arr, table, w_query, w_key, w_value))
    recalled, km, vm, often = line.call(
        memory_kernel, [row_bf] * 3 + [((8, size), F32)], "memory",
        (info, arrived, past, positions, table, fit, w_key, w_value), small=1,
    )

    calls = 3 if pairs % 3 == 0 else 1
    per = pairs // calls
    blocks = [pl.BlockSpec((rows, 2 * HD), lambda i, c=c: (0, i + c * per)) for c in range(calls)]
    e_blocks = [pl.BlockSpec((2, rows, rows + size), lambda i, c=c: (i + c * per, 0, 0)) for c in range(calls)]
    grid = (per,)
    shared = (q, k, v, km, vm, often)
    results = [((2 * pairs, rows, rows + size), BF16), row_bf, row_f]
    begun = ()
    for call in range(calls - 1):
        e, mixed, linv = line.blocks(
            attend_kernel, results, f"attend_{call}", shared + begun, grid,
            [blocks[call]] * 5 + [VMEM] + [ANY] * len(begun), [e_blocks[call]] + [blocks[call]] * 2,
            far=(0,), limit=20, aliases={6 + i: i for i in range(len(begun))}, there=(6,) if begun else (),
        )
        begun = (e, mixed, linv)
    e, mixed, linv, resid, *normed2 = line.blocks(
        attend_more_kernel, results + [row_f, half_bf, half_bf], "attend_more",
        shared + begun + (w_attn_out, table, arr), grid,
        [blocks[-1]] * 5 + [VMEM, ANY, pl.BlockSpec((rows, (calls - 1) * per * 2 * HD), lambda i: (0, 0)), ANY] + [VMEM] * 3,
        [e_blocks[-1]] + [blocks[-1]] * 2 + [VMEM] * 3,
        scratch=[pltpu.VMEM((rows, width), BF16)], aliases={6: 0, 7: 1, 8: 2}, far=(0,), limit=24, there=(6,),
    )
    normed2 += [swap(half, "core") for half in normed2]
    cot_sib = swap(cot, "core")
    far_in, far_out = hold(far_cut, line.last), hold(far_out, line.last)
    more_in, more_out = swap(far_in, "x"), swap(far_out, "z1")
    part, both = ((third, width), BF16), ((2, rows, width), BF16)
    bias_f, stacked = ((1, units), F32), ((width + units, width), BF16)
    out_own, gx_own, g_own, gb_own = line.call(
        mlp_kernel, [both, both, stacked, bias_f], "mlp_own",
        (*normed2, cot, cot_sib, w_mlp_in, table, w_mlp_out), limit=24,
        scratch=[pltpu.VMEM((2 * rows, units), BF16)] * 2,
    )
    w_in_far, w_out_far, b_far = line.call(
        far_weights_kernel, [((width, units), BF16), ((units, width), BF16), ((1, units), F32)], "far_weights",
        (info, far_in, more_in, far_out, more_out), small=1,
    )
    out_far, gx_far, g_far, gb_far = line.call(
        mlp_kernel, [both, both, stacked, bias_f], "mlp_far",
        (*normed2, cot, cot_sib, w_in_far, b_far, w_out_far), limit=20,
        scratch=[pltpu.VMEM((2 * rows, units), BF16)] * 2,
    )
    gx_keep, gx_send = line.call(merge_kernel, [row_bf] * 2, "merge", (gx_own, gx_far))
    gx_came = swap(gx_send, "core")
    rounds = Rounds(line, info)
    mlp_items, at = [], 0
    for order, count in MLP_PARTS:
        mlp_items.append(Item(steps_of(order, True), (g_own, at, count), (g_far, at, count)))
        at += count
    rounds.go("a", mlp_items)

    grad_mixed, grad_resid, gwo, vecs_mid, *out_send = line.call(
        middle_kernel, [row_bf, row_f, square_bf, vec_f, half_bf, half_bf], "middle",
        (gx_keep, gx_came, resid, cot, table, mixed, w_attn_out, out_own, out_far),
    )
    out_came = [swap(half, "core") for half in out_send]
    grads = ()
    back = 2 if pairs % 2 == 0 else 1
    per = pairs // back
    blocks = [pl.BlockSpec((rows, 2 * HD), lambda i, c=c: (0, i + c * per)) for c in range(back)]
    e_blocks = [pl.BlockSpec((2, rows, rows + size), lambda i, c=c: (i + c * per, 0, 0)) for c in range(back)]
    grid = (per,)
    for which in range(back):
        grads = line.blocks(
            attend_back_kernel, [row_bf] * 5, f"attend_back_{which}", (q, k, v, km, vm, e, linv, mixed, grad_mixed) + tuple(grads),
            grid, [blocks[which]] * 5 + [e_blocks[which]] + [blocks[which]] * 3 + [ANY] * len(grads),
            [blocks[which]] * 5, there=(5,), aliases={9 + i: i for i in range(len(grads))},
        )
        if which == 0:
            (output,) = line.call(emit_kernel, [row_bf], "emit", (resid, out_own, out_far, *out_came, table), far=(0,))
    dq, dk, dv, dkm, dvm = grads
    rounds.go("b", mlp_items)
    send, *keeps = line.call(
        weight_grads_kernel, [((2 * width, width), BF16)] + [((count, width), BF16) for _, count in ATTN_PARTS], "weight_grads",
        (info, normed, recalled, dq, dk, dv, dkm, dvm, gwo), small=1, scratch=[pltpu.VMEM((width, width), BF16)],
    )
    core_came = swap(send, "core")
    attn_items, at = [], 0
    for (order, count), kept in zip(ATTN_PARTS, keeps):
        attn_items.append(Item(steps_of(order, False), (kept, 0, count), now=("half", "core"), came=(core_came, at)))
        at += count
    grad_memory, vecs_rec = line.call(
        recall_back_kernel, [row_bf, vec_f], "recall_back", (info, dkm, dvm, w_key, w_value, fit, arrived), small=1,
    )
    handed = from_behind(grad_memory, "mp", -1)
    gn, vecs = line.call(
        project_back_kernel, [row_f, ((16, width), BF16)], "project_back",
        (info, arr, dq, dk, dv, dvm, w_query, w_key, w_value, vecs_mid, vecs_rec, gb_own, gb_far), small=1,
    )
    rounds.go("c", mlp_items + attn_items)
    (grad_hidden,) = line.call(
        last_kernel, [row_f], "last", (arr, table, gn, handed, grad_resid), far=(0,)
    )
    vec_item = Item([("swap", link) for link in ["z2"] + more_links() + ["x", "z1", "y"]], (vecs, 0, 16))
    rounds.go("d", mlp_items + attn_items)
    for link in more_links():
        rounds.go("d" + link, mlp_items)
    rounds.go("e", mlp_items + attn_items)
    rounds.go("f", mlp_items + attn_items + [vec_item])
    for link in more_links():
        rounds.go("f" + link, attn_items + [vec_item])
    mlp_now = [(*item.kept[0], *item.came, item.now[1]) for item in mlp_items]
    rounds.go("g", attn_items + [vec_item])
    plan, operands, at = [], [], 0
    for own, first, count, came, came_at, link in mlp_now:
        plan.append((link, count, first, came_at, at))
        operands += [own, came]
        at += 2 * count
    gw_in, gw_out = line.call(
        lambda *refs: mlp_grads_kernel(plan, *refs), [((width, units), F32), ((units, width), F32)], "mlp_grads",
        (info, *operands), small=1, far=(0, 1), scratch=[pltpu.VMEM((width + units, width), BF16)], limit=24,
    )
    rounds.go("h", attn_items + [vec_item])
    rounds.go("i", attn_items + [vec_item], mirror=True)
    mirror = rounds.mirror

    def squares(name, arrays, plan, begun=(), vectors=()):
        starts, at = [], 0
        for _, rows_of in ATTN_PARTS:
            starts.append((at, rows_of // 8))
            at += rows_of // 4
        plan = [block + starts[block[0]] for block in plan]
        count, more = len(arrays), 9 if vectors else 0
        scratch = [pltpu.VMEM((block[-1], width), F32) for block in plan for _ in range(4)] + [pltpu.SemaphoreType.DMA((4 * len(plan) + more,))]
        return line.start(
            lambda *refs: squares_kernel(plan, count, len(begun), vectors, *refs), [square_f] * 4 + [((width,), F32)] * more, name,
            (info, *arrays, *begun), (1,), [SMALL] + [VMEM] * count + [HBM] * len(begun), [HBM] * (4 + more),
            scratch + [pltpu.VMEM((width,), F32)] * more, far=tuple(range(4 + more)), limit=16,
            there=tuple(range(1 + count, 1 + count + len(begun))), aliases={1 + count + i: i for i in range(len(begun))},
        )

    own = [item.kept[0] for item in attn_items]
    parts = range(len(ATTN_PARTS))
    plan = [(part, True, True, part, own[part][1]) for part in parts]
    at = 0
    for part, item in enumerate(attn_items):
        plan.append((part, False, True, len(parts), at))
        at += item.kept[0][2]
    begun = squares("squares_1", [array for array, _, _ in own] + [mirror], plan)
    came = [(hold(item.came[0], line.last), item.came[1]) for item in attn_items]
    passed = [swap(array, "core") for array, _ in came]
    begun = squares(
        "squares_2", [array for array, _ in came], [(part, True, False, part, came[part][1]) for part in parts], begun
    )
    vec_part = [item.now[1] for item in attn_items].index(vec_item.now[1])
    vec_own, vec_came = vec_item.kept[0], vec_item.came
    gwq, gwk, gwv, gwo, *vecs = squares(
        "squares_3", passed + [vec_own[0], vec_came[0], mirror],
        [(part, False, False, part, came[part][1]) for part in parts], begun,
        (
            (len(parts), vec_own[1]), (len(parts) + 1, vec_came[1]), (len(parts) + 2, at), (vec_part, vec_came[1])
        ),
    )
    return (
        output[None],
        grad_hidden[None],
        vecs[0],
        vecs[1],
        gwq,
        vecs[2],
        gwk,
        gwv,
        vecs[3],
        gwo,
        vecs[4],
        vecs[5],
        vecs[6],
        gw_in,
        vecs[8],
        gw_out,
        vecs[7],
    )


def solution(mesh):
    rows = P("dp", "mp", None)
    placed = (rows, P("dp", None, None), P("dp"), rows) + (P(),) * 11
    placed += (P(None, "mp"), P("mp"), P("mp", None), P(), rows)
    return jax.shard_map(
        local,
        mesh=mesh,
        in_specs=placed,
        out_specs=(rows, rows) + (P(),) * 11 + (P(None, "mp"), P("mp"), P("mp", None), P()),
        check_vma=False,
    )
```

```python
import math

import jax
import jax.numpy as jnp
from jax import lax
from jax.experimental import pallas as pl
from jax.experimental.pallas import tpu as pltpu
from jax.sharding import PartitionSpec as P

HD = 64
NORM_EPSILON = 1e-05
RIDGE_WEIGHT = 0.1
NOTHING = -1e30
GELU_SLOPE = math.sqrt(2.0 / math.pi)
GELU_CUBE = 0.044715
F32 = jnp.float32
BF16 = jnp.bfloat16
MEBI = 1 << 20


def mm(left, right):
    return jnp.dot(left, right, preferred_element_type=F32)


def mt(left, right):
    return lax.dot_general(left, right, (((1,), (1,)), ((), ())), preferred_element_type=F32)


def tm(left, right):
    return lax.dot_general(left, right, (((0,), (0,)), ((), ())), preferred_element_type=F32)


def summed(first, *others):
    total = first.astype(F32)
    for other in others:
        total = total + other.astype(F32)
    return total.astype(BF16)


def column_sum(values):
    return jnp.sum(values, axis=0, keepdims=True)


def normalized(values):
    row_mean = jnp.mean(values, axis=-1, keepdims=True)
    centered = values - row_mean
    row_var = jnp.mean(centered * centered, axis=-1, keepdims=True)
    inverse = lax.rsqrt(row_var + NORM_EPSILON)
    return centered * inverse, inverse


def norm_back(xhat, inverse, incoming, gain):
    g = incoming * gain
    mean_g = jnp.mean(g, axis=-1, keepdims=True)
    mean_gx = jnp.mean(g * xhat, axis=-1, keepdims=True)
    return inverse * (g - mean_g - xhat * mean_gx)


SMALL = pl.BlockSpec(memory_space=pltpu.SMEM)
VMEM = pl.BlockSpec(memory_space=pltpu.VMEM)
ANY = pl.BlockSpec(memory_space=pl.ANY)
HBM = pl.BlockSpec(memory_space=pltpu.HBM)


class Arriving:
    def __init__(self, source, held, sem):
        self.held, self.copy = held, pltpu.make_async_copy(source, held, sem)
        self.shape, self.dtype = held.shape, held.dtype
        self.here = False
        self.copy.start()

    def wait(self):
        if not self.here:
            self.copy.wait()
            self.here = True
        return self.held

    @property
    def at(self):
        return self.wait().at

    def __getitem__(self, index):
        return self.wait()[index]


class Leaving:
    def __init__(self, target, held, sem):
        self.held, self.copy = held, pltpu.make_async_copy(held, target, sem)
        self.shape, self.dtype = held.shape, held.dtype
        self.gone = False

    def leave(self):
        if not self.gone:
            self.copy.start()
            self.gone = True

    def __getitem__(self, index):
        return self.held[index]

    def __setitem__(self, index, value):
        self.held[index] = value
        if index is Ellipsis:
            self.leave()


class Line:
    def __init__(self):
        self.last = None

    def start(self, body, outs, name, operands, grid, in_specs, out_specs, scratch, after=(), aliases=None, far=(), limit=32, there=()):
        waits = list(after) + ([] if self.last is None else [self.last])
        operands = [pltpu.with_memory_space_constraint(o, pltpu.HBM) if i in there else o for i, o in enumerate(operands)]
        known, gone = len(operands), len(operands) + len(waits)
        results = pl.pallas_call(
            lambda *refs: body(*refs[:known], *refs[gone : gone + len(outs)], *refs[gone + len(outs) + 1 :]),
            out_shape=[(pltpu.HBM if i in far else pltpu.VMEM)(shape, dtype) for i, (shape, dtype) in enumerate(outs)]
            + [pltpu.VMEM((8, 128), F32)],
            grid=grid,
            in_specs=list(in_specs) + [ANY] * len(waits),
            out_specs=list(out_specs) + [VMEM],
            scratch_shapes=list(scratch),
            input_output_aliases=aliases or {},
            compiler_params=pltpu.CompilerParams(vmem_limit_bytes=limit * MEBI),
            cost_estimate=pl.CostEstimate(flops=0, bytes_accessed=0, transcendentals=0),
            name=name,
        )(*operands, *waits)
        *results, self.last = results
        return results

    def blocks(self, body, outs, name, operands, grid, in_specs, out_specs, scratch=(), **more):
        return self.start(body, outs, name, operands, grid, in_specs, out_specs, scratch, **more)

    def call(self, body, outs, name, operands, small=0, load=(), far=(), scratch=(), after=(), limit=16):
        outs = list(outs) + [(operands[i].shape, operands[i].dtype) for i in load]
        own, kept = len(scratch), len(outs) - len(load)
        in_specs = [SMALL if i < small else HBM if i in load else VMEM for i in range(len(operands))]
        out_specs = [HBM if i in far else VMEM for i in range(len(outs))]
        held = [pltpu.VMEM(*outs[i]) for i in far]
        sems = [pltpu.SemaphoreType.DMA((len(far) + len(load),))] if far or load else []

        def run(*refs):
            ins, targets, rest = refs[: len(operands)], refs[len(operands) : len(operands) + len(outs)], refs[len(operands) + len(outs) :]
            mine, buffers, sem = rest[:own], rest[own:], rest[-1] if sems else None
            ins, targets = list(ins), list(targets)
            for slot, i in enumerate(load):
                ins[i] = Arriving(ins[i], targets[kept + slot], sem.at[len(far) + slot])
            for slot, i in enumerate(far):
                targets[i] = Leaving(targets[i], buffers[slot], sem.at[slot])
            body(*ins, *targets[:kept], *mine)
            for i in load:
                ins[i].wait()
            for i in far:
                targets[i].leave()
            for i in far:
                targets[i].copy.wait()

        return self.start(
            run, outs, name, operands, (1,), in_specs, out_specs, list(scratch) + held + sems, after, far=far, limit=limit,
            there=tuple(load),
        )


def hold(value, *until):
    return lax.optimization_barrier((value,) + until)[0]


def at_half(bit, count):
    return pl.ds(pl.multiple_of(bit * count, count), count)


def fit_at_positions(size, fit_ref):
    half = size // 2
    spread = 1.0 / size
    row = lax.broadcasted_iota(jnp.int32, (half, half), 0)
    col = lax.broadcasted_iota(jnp.int32, (half, half), 1)
    eye = jnp.where(row == col, 1.0, 0.0).astype(F32)
    flip = jnp.where(row + col == half - 1, 1.0, 0.0).astype(BF16)

    def design(columns):
        apart = (row.astype(F32) + 0.5) / size - (columns.astype(F32) + 0.5) / size
        return jnp.exp(-(apart * apart) / (2.0 * spread * spread))

    def pieces(value):
        high = value.astype(BF16)
        return high, (value - high.astype(F32)).astype(BF16)

    def exact(left, right):
        (left_high, left_low), (right_high, right_low) = pieces(left), pieces(right)
        return mm(left_high, right_high) + (mm(left_high, right_low) + mm(left_low, right_high))

    def full(left, right):
        return jnp.dot(left, right, precision=lax.Precision.HIGHEST, preferred_element_type=F32)

    direct, mirrored = design(col), design(size - 1 - col)
    brackets, guesses = [], []
    for part in (direct + mirrored, direct - mirrored):
        bracket = full(part, part) + RIDGE_WEIGHT * eye
        low = bracket.astype(BF16)
        brackets.append(bracket)
        guesses.append(2.39060839 * eye - 0.96134588 * bracket + 0.09859958 * mm(low, low))
    for step in range(6):
        for which in range(2):
            bracket, guess = brackets[which], guesses[which]
            if step < 4:
                low = guess.astype(BF16)
                left = 2.0 * eye - mm(bracket.astype(BF16), low)
                guesses[which] = mm(low, left.astype(BF16))
            else:
                guesses[which] = exact(guess, 2.0 * eye - exact(bracket, guess))
    even, odd = (eye - RIDGE_WEIGHT * guess for guess in guesses)
    inner = (0.5 * (even + odd)).astype(BF16)
    outer = (0.5 * (even - odd)).astype(BF16)
    fit_ref[0:half, 0:half] = inner
    fit_ref[0:half, half:size] = mm(outer, flip).astype(BF16)
    fit_ref[half:size, 0:half] = mm(flip, outer).astype(BF16)
    fit_ref[half:size, half:size] = mm(flip, mm(inner, flip).astype(BF16)).astype(BF16)


VECTORS = ("gain1", "shift1", "b_q", "b_v", "b_o", "gain2", "shift2", "b_in", "b_out")


def vector(table, name):
    at = VECTORS.index(name)
    return table[at : at + 1, :]


def start_kernel(info, w_in, w_out, *refs):
    vectors, (fit, table, cut_in, cut_out) = refs[: len(VECTORS)], refs[-4:]
    fit_at_positions(fit.shape[0], fit)
    table[...] = jnp.zeros_like(table)
    for at, value in enumerate(vectors):
        table[at, :] = value[...]
    count = cut_in.shape[1]
    mine = at_half(scalar(info, "half"), count)
    cut_in[...] = w_in[:, mine]
    bias, pieces = vector(table, "b_in"), []
    for _ in range(3):
        pieces.append(bias.astype(BF16))
        bias = bias - pieces[-1].astype(F32)
    cut_out[0:count, :] = w_out[mine, :]
    cut_out[count:, :] = jnp.concatenate(pieces + [jnp.zeros((13, table.shape[1]), BF16)], axis=0)


def front_kernel(hidden, table, wq, wk, wv, normed, q, k, v):
    xhat, _ = normalized(hidden[...].astype(F32))
    low = (xhat * vector(table, "gain1") + vector(table, "shift1")).astype(BF16)
    normed[...] = low
    scale = 1.0 / math.sqrt(HD)
    q[...] = (mm(low, wq[...]) + vector(table, "b_q")).astype(BF16) * jnp.asarray(scale, BF16)
    k[...] = mm(low, wk[...]).astype(BF16)
    v[...] = (mm(low, wv[...]) + vector(table, "b_v")).astype(BF16)


def memory_kernel(info, arrived, past, positions, table, fit, wk, wv, recalled, km, vm, often):
    size = fit.shape[0]
    xhat, _ = normalized(arrived[...].astype(F32))
    before = xhat * vector(table, "gain1") + vector(table, "shift1")
    kept = past[...].astype(F32) * (1 - scalar(info, "reset")).astype(F32)
    earlier = jnp.where(scalar(info, "first") > 0, kept, before).astype(BF16)
    low = mm(fit[...], earlier).astype(BF16)
    recalled[...] = low
    km[...] = mm(low, wk[...]).astype(BF16)
    vm[...] = (mm(low, wv[...]) + vector(table, "b_v")).astype(BF16)
    place = lax.broadcasted_iota(jnp.int32, (size, positions.shape[1]), 0)
    hit = jnp.where(place == positions[...], 1.0, 0.0).astype(BF16)
    count = mt(jnp.ones((8, positions.shape[1]), BF16), hit)
    often[...] = jnp.where(count > 0.5, jnp.log(jnp.maximum(count, 1.0)), NOTHING)


def attend_pair(q, k, v, km, vm, often, e, mixed, linv):
    rows = q.shape[0]
    half = rows // 2
    lane = lax.broadcasted_iota(jnp.int32, (1, 2 * HD), 1)
    row = lax.broadcasted_iota(jnp.int32, (half, half), 0)
    col = lax.broadcasted_iota(jnp.int32, (half, half), 1)
    log_count = often[0:1, :]
    units = [(part, head) for part in range(2) for head in range(2)]
    scores = {}
    for part, head in units:
        here = slice(part * half, (part + 1) * half)
        mine = (lane >= head * HD) & (lane < (head + 1) * HD)
        query = jnp.where(mine, q[here, :], jnp.zeros((), BF16))
        near = mt(query, k[0 : (part + 1) * half, :])
        far = mt(query, km[...]) + log_count
        edge = jnp.where(col > row, NOTHING, near[:, part * half :])
        top = jnp.maximum(jnp.max(edge, axis=-1, keepdims=True), jnp.max(far, axis=-1, keepdims=True))
        if part:
            top = jnp.maximum(top, jnp.max(near[:, : part * half], axis=-1, keepdims=True))
        scores[part, head] = (near, edge, far, top)
    for part in range(2):
        here = slice(part * half, (part + 1) * half)
        seen = (part + 1) * half
        results = []
        for head in range(2):
            near, edge, far, top = scores[part, head]
            edge = jnp.exp(edge - top)
            far = jnp.exp(far - top)
            total = jnp.sum(edge, axis=-1, keepdims=True) + jnp.sum(far, axis=-1, keepdims=True)
            edge_low, far_low = edge.astype(BF16), far.astype(BF16)
            e[head, here, part * half : seen] = edge_low
            e[head, here, rows:] = far_low
            out = mm(edge_low, v[part * half : seen, :]) + mm(far_low, vm[...])
            if part:
                start = jnp.exp(near[:, : part * half] - top)
                total = total + jnp.sum(start, axis=-1, keepdims=True)
                start_low = start.astype(BF16)
                e[head, here, 0 : part * half] = start_low
                out = out + mm(start_low, v[0 : part * half, :])
            inverse = 1.0 / total
            results.append((out * inverse, inverse))
        first = lane < HD
        mixed[here, :] = jnp.where(first, results[0][0], results[1][0]).astype(BF16)
        linv[here, :] = jnp.where(first, results[0][1], results[1][1])


def attend_kernel(q, k, v, km, vm, often, *refs):
    e, mixed, linv = refs[-3:]
    attend_pair(q, k, v, km, vm, often, e, mixed, linv)


def attend_more_kernel(
    q, k, v, km, vm, often, e_done, mixed_done, linv_done, wo, table, hidden,
    e, mixed, linv, resid, normed2_a, normed2_b, every,
):
    step, rows = pl.program_id(0), q.shape[0]
    attend_pair(q, k, v, km, vm, often, e, mixed, linv)
    done, block = mixed_done.shape[1], mixed.shape[1]
    every[:, pl.ds(pl.multiple_of(done + step * block, block), block)] = mixed[...]

    @pl.when(step == pl.num_programs(0) - 1)
    def _():
        every[:, 0:done] = mixed_done[...]
        total = hidden[...].astype(F32) + mm(every[...], wo[...]) + vector(table, "b_o")
        resid[...] = total
        xhat, _ = normalized(total)
        normed2 = (xhat * vector(table, "gain2") + vector(table, "shift2")).astype(BF16)
        normed2_a[...] = normed2[: rows // 2]
        normed2_b[...] = normed2[rows // 2 :]


def mlp_block(x, cot, w_in, b_in, w_out):
    pre = mm(x, w_in) + b_in
    square = pre * pre
    bend = jnp.tanh(GELU_SLOPE * pre * (1.0 + GELU_CUBE * square))
    act = (0.5 * pre * (1.0 + bend)).astype(BF16)
    slope = 0.5 * (1.0 + bend) + (0.5 * GELU_SLOPE) * pre * (1.0 - bend * bend) * (1.0 + 3.0 * GELU_CUBE * square)
    gpre = (mt(cot, w_out) * slope).astype(BF16)
    return mm(act, w_out), mt(gpre, w_in), act, gpre


def mlp_kernel(xa, xb, xc, xd, cot0, cot1, w_in, b_in, w_out, out, gx, grads, g_bias, acts, gpres):
    block, width, units = xa.shape[0], xa.shape[1], acts.shape[1]
    bias = b_in[...] if b_in.shape[0] == 1 else vector(b_in, "b_in")
    parts = []
    for which, x in enumerate((xa, xb, xc, xd)):
        here, there = slice(which % 2 * block, (which % 2 + 1) * block), slice(which * block, (which + 1) * block)
        cot = (cot0, cot1)[which // 2]
        o, g, act, gpre = mlp_block(x[...], cot[here, :], w_in[...], bias, w_out[...])
        out[which // 2, here, :], gx[which // 2, here, :] = o.astype(BF16), g.astype(BF16)
        acts[there, :] = act
        gpres[there, :] = gpre
        parts.append((x, there))
    total = tm(xa[...], gpres[0:block, :])
    for x, there in parts[1:]:
        total = total + tm(x[...], gpres[there, :])
    grads[0:width, :] = total.astype(BF16)
    half = 2 * block
    grads[width : width + units, :] = (tm(acts[:half, :], cot0[...]) + tm(acts[half:, :], cot1[...])).astype(BF16)
    g_bias[...] = column_sum(gpres[...].astype(F32))


def mlp_far_kernel(other, info, xa, xb, xc, xd, cot0, cot1, w_in, w_out, *refs):
    out, gx, grads, g_bias, acts, gpres = refs[-6:]
    block, width, units = xa.shape[0], xa.shape[1], w_in.shape[1]
    half = scalar(info, "half")
    half = 1 - half if other else half
    mine = at_half(half, units)
    pieces = w_out[units : units + 16, mine].astype(F32)
    bias = pieces[0:1] + pieces[1:2] + pieces[2:3]
    parts = []
    for which, x in enumerate((xa, xb, xc, xd)):
        here, there = slice(which % 2 * block, (which % 2 + 1) * block), slice(which * block, (which + 1) * block)
        cot = (cot0, cot1)[which // 2]
        o, g, act, gpre = mlp_block(x[...], cot[here, :], w_in[...], bias, w_out[0:units, :])
        out[which // 2, here, :], gx[which // 2, here, :] = o.astype(BF16), g.astype(BF16)
        acts[there, :] = act
        gpres[there, :] = gpre
        parts.append((x, there))
    total = tm(xa[...], gpres[0:block, :])
    for x, there in parts[1:]:
        total = total + tm(x[...], gpres[there, :])
    grads[0:width, mine] = total.astype(BF16)
    total = tm(acts[: 2 * block, :], cot0[...]) + tm(acts[2 * block :, :], cot1[...])
    grads[pl.ds(pl.multiple_of(width + half * units, 128), units), :] = total.astype(BF16)
    g_bias[...] = column_sum(gpres[...].astype(F32))


def merge_kernel(gx, gx_far, gx_other, keep_gx, send_gx):
    keep_gx[...] = summed(gx[0], gx_far[0], gx_other[0])
    send_gx[...] = summed(gx[1], gx_far[1], gx_other[1])


def middle_kernel(
    gx, gx_more, resid, cot, table, mixed, wo, out_own, out_far, out_other, grad_mixed, grad_resid, gwo, vecs,
    send_a, send_b
):
    half = send_a.shape[0]
    send_a[...] = summed(out_own[1, 0:half, :], out_far[1, 0:half, :], out_other[1, 0:half, :])
    send_b[...] = summed(out_own[1, half:, :], out_far[1, half:, :], out_other[1, half:, :])
    xhat, inverse = normalized(resid[...])
    n = gx[...].astype(F32) + gx_more[...].astype(F32)
    cot_full = cot[...].astype(F32)
    total = cot_full + norm_back(xhat, inverse, n, vector(table, "gain2"))
    grad_resid[...] = total
    low = total.astype(BF16)
    grad_mixed[...] = mt(low, wo[...]).astype(BF16)
    gwo[...] = tm(mixed[...], low).astype(BF16)
    vecs[...] = jnp.concatenate(
        [
            column_sum(low.astype(F32)),
            column_sum(n * xhat),
            column_sum(n),
            column_sum(cot_full),
            jnp.zeros((4, n.shape[1]), F32),
        ],
        axis=0,
    )


def attend_back_kernel(q, k, v, km, vm, e, linv, mixed, gmix, *refs):
    dq, dk, dv, dkm, dvm, ds, queries, grads = refs[-8:]
    rows = q.shape[0]
    half = rows // 2
    lane = lax.broadcasted_iota(jnp.int32, (1, 2 * HD), 1)
    scale = 1.0 / math.sqrt(HD)
    grad = gmix[...].astype(F32) * linv[...]
    product = grad * mixed[...].astype(F32)
    for head in range(2):
        mine = (lane >= head * HD) & (lane < (head + 1) * HD)
        all_rows = slice(head * rows, (head + 1) * rows)
        queries[all_rows, :] = jnp.where(mine, q[...], jnp.zeros((), BF16))
        grads[all_rows, :] = jnp.where(mine, grad, 0.0).astype(BF16)
    for head in range(2):
        mine = (lane >= head * HD) & (lane < (head + 1) * HD)
        dots = jnp.sum(jnp.where(mine, product, 0.0), axis=-1, keepdims=True)
        for part in range(2):
            here = slice(part * half, (part + 1) * half)
            there = slice(head * rows + part * half, head * rows + (part + 1) * half)
            seen = (part + 1) * half
            dot, grad_low = dots[here], grads[there, :]
            near = e[head, here, 0:seen].astype(F32) * (mt(grad_low, v[0:seen, :]) - dot)
            far = e[head, here, rows:].astype(F32) * (mt(grad_low, vm[...]) - dot)
            ds[there, 0:seen] = near.astype(BF16)
            ds[there, rows:] = far.astype(BF16)
    for part in range(2):
        here = slice(part * half, (part + 1) * half)
        seen = (part + 1) * half
        parts = []
        for head in range(2):
            there = slice(head * rows + part * half, head * rows + (part + 1) * half)
            parts.append(mm(ds[there, 0:seen], k[0:seen, :]) + mm(ds[there, rows:], km[...]))
        dq[here, :] = (jnp.where(lane < HD, parts[0], parts[1]) * scale).astype(BF16)
    late = [slice(head * rows + half, (head + 1) * rows) for head in range(2)]

    def both(left, right):
        first = tm(left[...], right(slice(0, half)))
        second = sum(tm(left[at, :], right(slice(half, rows), head)) for head, at in enumerate(late))
        return first, second, tm(left[...], right(slice(rows, None)))

    def scores(columns, head=None):
        return ds[:, columns] if head is None else ds[late[head], columns]

    def weights(columns, head=None):
        if head is None:
            return e[:, :, columns].reshape(2 * rows, -1)
        return e[head, half:, columns]

    for left, right, near, far in ((queries, scores, dk, dkm), (grads, weights, dv, dvm)):
        first, second, rest = both(left, right)
        near[0:half, :] = first.T.astype(BF16)
        near[half:, :] = second.T.astype(BF16)
        far[...] = rest.T.astype(BF16)


def recall_back_kernel(info, dkm, dvm, wk, wv, fit, arrived, grad_memory, vecs):
    grad_recalled = (mt(dkm[...], wk[...]) + mt(dvm[...], wv[...])).astype(BF16)
    handed = tm(fit[...], grad_recalled).astype(BF16)
    grad_memory[...] = handed
    xhat, _ = normalized(arrived[...].astype(F32))
    n = jnp.where(scalar(info, "first") > 0, 0.0, handed.astype(F32))
    vecs[...] = jnp.concatenate([column_sum(n * xhat), column_sum(n), jnp.zeros((6, n.shape[1]), F32)], axis=0)


def weight_grads_kernel(info, normed, recalled, dq, dk, dv, dkm, dvm, gwo, send, *refs):
    low, rec = normed[...], recalled[...]
    *parts, whole = refs
    half = whole.shape[0] // 2
    core = scalar(info, "core")
    grads = (
        lambda: tm(low, dq[...]),
        lambda: tm(low, dk[...]) + tm(rec, dkm[...]),
        lambda: tm(low, dv[...]) + tm(rec, dvm[...]),
        None,
    )
    for which, grad in enumerate(grads):
        source = gwo
        if grad is not None:
            whole[...] = grad().astype(BF16)
            source = whole
        start = begin = 0
        for part in parts:
            piece = part.shape[0] // 8
            for first in range(2):
                at = (4 * first + which) * piece
                send[begin + at : begin + at + piece, :] = source[
                    pl.ds(pl.multiple_of((1 - core) * half + start, 16), piece), :
                ]
                part[at : at + piece, :] = source[pl.ds(pl.multiple_of(core * half + start, 16), piece), :]
                start += piece
            begin += part.shape[0]


def project_back_kernel(info, hidden, dq, dk, dv, dvm, wq, wk, wv, vecs_mid, vecs_rec, gb_own, gb_far, gb_other, gn, vecs):
    width = hidden.shape[1]
    n = mt(dq[...], wq[...]) + mt(dk[...], wk[...]) + mt(dv[...], wv[...])
    gn[...] = n
    xhat, _ = normalized(hidden[...].astype(F32))
    shard = lax.broadcasted_iota(jnp.int32, (4, 1), 0)
    halves = [gb_far[...], gb_other[...]]
    far = jnp.where(scalar(info, "half") == 0, jnp.concatenate(halves, axis=1), jnp.concatenate(halves[::-1], axis=1))
    bias_rows = jnp.where(shard == scalar(info, "me"), gb_own[...], 0.0) + jnp.where(shard == scalar(info, "far"), far, 0.0)
    vecs[...] = jnp.concatenate(
        [
            column_sum(n * xhat) + vecs_rec[0:1, :],
            column_sum(n) + vecs_rec[1:2, :],
            column_sum(dq[...].astype(F32)),
            column_sum(dv[...].astype(F32)) + column_sum(dvm[...].astype(F32)),
            vecs_mid[0:4, :],
            bias_rows,
            jnp.zeros((4, width), F32),
        ],
        axis=0,
    ).astype(BF16)


def last_kernel(hidden, table, gn, handed, grad_resid, grad_hidden):
    xhat, inverse = normalized(hidden[...].astype(F32))
    n = gn[...] + handed[...].astype(F32)
    grad_hidden[...] = grad_resid[...] + norm_back(xhat, inverse, n, vector(table, "gain1"))


def added(left, right):
    return (left.astype(F32) + right.astype(F32)).astype(BF16)


MLP_PARTS = (
    (("y", "x", "z2", "z1"), 384), (("y", "z1", "x", "z2"), 128), (("x", "y", "z2", "z1"), 128),
    (("x", "z1", "y", "z2"), 384), (("z1", "y", "x", "z2"), 384), (("z1", "x", "y", "z2"), 128),
)
ATTN_PARTS = ((("y", "z1", "x", "z2"), 512), (("x", "y", "z1", "z2"), 512), (("z1", "x", "y", "z2"), 512))
AXES = {"core": ("mp", 1), "y": ("mp", 2), "x": ("dp", 1), "z1": ("dp", 2), "z2": ("dp", 4)}


def swap(value, link):
    axis, mask = AXES[link] if link in AXES else ("dp", int(link))
    return lax.ppermute(value, axis, [(i, i ^ mask) for i in range(lax.axis_size(axis))])


def bit_of(link):
    axis, mask = AXES[link]
    return (lax.axis_index(axis) // mask) % 2


SCALAR = {"core": 0, "y": 1, "x": 2, "z1": 3, "z2": 4, "me": 5, "far": 6, "first": 7, "reset": 8, "half": 9}


def scalar_array(reset):
    bit = {link: bit_of(link) for link in AXES}
    me = lax.axis_index("mp")
    values = dict(bit, me=me, far=me ^ 2, first=me == 0, reset=reset, half=bit["x"] ^ bit["z1"])
    row = lax.broadcasted_iota(jnp.int32, (1, 16), 1)
    packed = jnp.zeros((1, 16), jnp.int32)
    for name, value in values.items():
        packed = jnp.where(row == SCALAR[name], jnp.asarray(value, jnp.int32), packed)
    return packed


def scalar(info, name):
    return info[0, SCALAR[name]]


class Item:
    def __init__(self, steps, *kept, now=None, came=None):
        self.steps, self.kept, self.now, self.came = list(steps), list(kept), now, came


class Rounds:
    def __init__(self, line, info):
        self.line, self.info = line, info

    def go(self, name, items, mirror=False):
        arrays, sends, outs, jobs = [], {}, [], []

        def slot(array):
            for which, known in enumerate(arrays):
                if known is array:
                    return which
            arrays.append(array)
            return len(arrays) - 1

        for item in items:
            kind, link = item.now or ("start", None)
            came, at = (slot(item.came[0]), item.came[1]) if link else (None, 0)
            sources = []
            for array, first, rows in item.kept:
                sources.append((slot(array), first, came, at, rows, kind, link))
                at += rows
            rows = item.kept[0][2] * (2 if kind == "double" else 1)
            step = item.steps.pop(0) if item.steps else None
            sent = sends.setdefault(step[1], [0]) if step else None
            if step is None:
                jobs.append((sources[0], "all", None, len(outs), 0, rows))
                item.kept = [("out", len(outs), rows)]
                outs.append(rows)
            elif step[0] in ("swap", "double"):
                jobs.append((sources[0], "all", None, step[1], sent[0], rows))
                item.came, item.kept = (None, sent[0]), [(step[1], sent[0], rows)]
                sent[0] += rows
                if mirror:
                    again = sends.setdefault("core", [0])
                    jobs.append((sources[0], "all", None, "core", again[0], rows))
                    again[0] += rows
            elif step[0] == "pair":
                jobs.append((sources[0], "all", None, len(outs), 0, rows))
                jobs.append((sources[1], "all", None, step[1], sent[0], rows))
                item.came, item.kept = (None, sent[0]), [("out", len(outs), rows)]
                sent[0] += rows
                outs.append(rows)
            else:
                half, kept = rows // 2, []
                item.came = (None, sent[0])
                for source in sources:
                    jobs.append((source, "mine", step[1], len(outs), 0, half))
                    jobs.append((source, "other", step[1], step[1], sent[0], half))
                    kept.append(("out", len(outs), half))
                    sent[0] += half
                    outs.append(half)
                item.kept = kept
            item.now = step
        links = list(sends)
        width = arrays[0].shape[1]
        shapes = [((rows, width), BF16) for rows in outs] + [((sends[link][0], width), BF16) for link in links]

        def body(info, *refs):
            ins, results = refs[: len(arrays)], refs[len(arrays) :]
            for (kept, first, came, at, rows, kind, over), what, link, target, base, count in jobs:
                out = results[len(outs) + links.index(target) if isinstance(target, str) else target]
                if kind == "double":
                    for bit, ref, start in ((scalar(info, over), kept, first), (1 - scalar(info, over), came, at)):
                        out[pl.ds(pl.multiple_of(base + bit * rows, 16), rows), :] = ins[ref][start : start + rows, :]
                    continue
                start = 0
                if what != "all":
                    bit = scalar(info, link)
                    start = (bit if what == "mine" else 1 - bit) * count

                def here(base):
                    if what == "all":
                        return slice(base, base + count)
                    return pl.ds(pl.multiple_of(base + start, 16), count)

                value = ins[kept][here(first), :]
                if kind != "start":
                    value = added(value, ins[came][here(at), :])
                out[base : base + count, :] = value

        results = self.line.call(body, shapes, f"round_{name}", (self.info, *arrays), small=1, limit=4)
        sent = dict(zip(links, results[len(outs) :]))
        arrived = {link: swap(array, link) for link, array in sent.items()}
        self.mirror = arrived.get("core")
        for item in items:
            if item.now:
                item.came = (arrived[item.now[1]], item.came[1])
            item.kept = [
                (results[first], 0, rows) if where == "out" else (sent[where], first, rows) for where, first, rows in item.kept
            ]


def more_links():
    return [str(8 << bit) for bit in range((lax.axis_size("dp") // 8).bit_length() - 1)]


def steps_of(order, paired):
    first = [("pair" if link == "y" and paired else "half", link) for link in order[:3]]
    back = [("double", link) for link in order[2::-1] if not (link == "y" and paired)]
    return first + [("swap", link) for link in [order[3]] + more_links()] + back


def squares_kernel(plan, count, skip, vectors, info, *refs):
    ins, rest = refs[:count], refs[count + skip :]
    outs, rest = rest[:4], rest[4:]
    vecs, rest = (rest[:9], rest[9:]) if vectors else ((), rest)
    buffers, sems = rest[: 4 * len(plan)], rest[4 * len(plan)]
    copies = []

    def leave(buffer, target):
        copies.append(pltpu.make_async_copy(buffer, target, sems.at[len(copies)]))
        copies[-1].start()

    half = outs[0].shape[0] // 2
    for block, (part, this_core, this_half, array, first, start, piece) in enumerate(plan):
        core, bit = scalar(info, "core"), scalar(info, ATTN_PARTS[part][0][0])
        core, bit = core if this_core else 1 - core, bit if this_half else 1 - bit
        at = pl.ds(pl.multiple_of(core * half + start + bit * piece, 16), piece)
        for which, out in enumerate(outs):
            buffer = buffers[4 * block + which]
            buffer[...] = ins[array][first + which * piece : first + (which + 1) * piece, :].astype(F32)
            leave(buffer, out.at[at, :])
    if vectors:
        rows = [ins[array][first : first + 16, :].astype(F32) for array, first in vectors]
        total = (rows[0] + rows[1]) + (rows[2] + rows[3])
        me, row = scalar(info, "me"), total[8:9, :]
        for at in range(1, 4):
            row = jnp.where(me == at, total[8 + at : 9 + at, :], row)
        held = rest[4 * len(plan) + 1 :]
        for at, (buffer, out) in enumerate(zip(held, vecs)):
            buffer[...] = total[at, :] if at < 8 else row[0, :]
            leave(buffer, out)
    for copy in copies:
        copy.wait()


def mlp_grads_kernel(plan, info, *refs):
    ins, (gw_in, gw_out, whole) = refs[: 2 * len(plan)], refs[2 * len(plan) :]
    for which, (link, rows, own_at, came_at, base) in enumerate(plan):
        for bit, ref, at in ((scalar(info, link), ins[2 * which], own_at), (1 - scalar(info, link), ins[2 * which + 1], came_at)):
            whole[pl.ds(pl.multiple_of(base + bit * rows, 16), rows), :] = ref[at : at + rows, :]
    count = gw_in.shape[0]
    gw_in[...] = whole[:count, :].astype(F32)
    gw_out[...] = whole[count:, :].astype(F32)


def emit_kernel(resid, out_own, out_far, out_other, came_a, came_b, table, output):
    came = jnp.concatenate([came_a[...], came_b[...]], axis=0).astype(F32)
    total = resid[...] + summed(out_own[0], out_far[0], out_other[0]).astype(F32) + came + vector(table, "b_out")
    output[...] = total.astype(BF16)


def from_behind(value, axis, steps):
    count = lax.axis_size(axis)
    leading, last = (max(0, -steps), min(count, count - steps))
    return lax.ppermute(value, axis, [(source, source + steps) for source in range(leading, last)])


def local(
    hidden,
    past_states,
    reset_flags,
    sample_positions,
    norm1_gain,
    norm1_shift,
    w_query,
    bias_query,
    w_key,
    w_value,
    bias_value,
    w_attn_out,
    bias_attn_out,
    norm2_gain,
    norm2_shift,
    w_mlp_in,
    bias_mlp_in,
    w_mlp_out,
    bias_mlp_out,
    cotangent,
):
    rows, width = hidden.shape[1], hidden.shape[2]
    size = past_states.shape[1]
    units = w_mlp_in.shape[1]
    assert rows == size and sample_positions.shape[2] == size
    pairs = width // (2 * HD)
    arr, cot = hidden[0], cotangent[0]
    half_bf = ((rows // 2, width), BF16)
    row_bf, row_f = ((rows, width), BF16), ((rows, width), F32)
    square_f, square_bf, vec_f = ((width, width), F32), ((width, width), BF16), ((8, width), F32)

    line = Line()
    info = scalar_array(reset_flags[0])
    half_w, third = width // 2, 2 * width // 3

    arrived = from_behind(arr, "mp", 1)
    (
        fit, table, cut_in, cut_out,
        w_mlp_in, w_mlp_out, arr, w_query, w_key, w_value, past, positions, w_attn_out, cot, *_
    ) = line.call(
        start_kernel,
        [((size, size), BF16), ((16, width), F32), ((width, units // 2), BF16), ((units // 2 + 16, width), BF16)], "start",
        (
            info, w_mlp_in, w_mlp_out, norm1_gain, norm1_shift, bias_query, bias_value, bias_attn_out, norm2_gain,
            norm2_shift, bias_mlp_in, bias_mlp_out, arr, w_query, w_key, w_value, past_states[0], sample_positions[0],
            w_attn_out, cot,
        ),
        small=1, load=(1, 2, 12, 13, 14, 15, 16, 17, 18, 19) + tuple(range(3, 12)), far=(2, 3),
    )
    far_cut, far_out = swap(cut_in, "y"), swap(cut_out, "y")
    normed, q, k, v = line.call(front_kernel, [row_bf] * 4, "front", (arr, table, w_query, w_key, w_value))
    recalled, km, vm, often = line.call(
        memory_kernel, [row_bf] * 3 + [((8, size), F32)], "memory",
        (info, arrived, past, positions, table, fit, w_key, w_value), small=1,
    )

    calls = 3 if pairs % 3 == 0 else 1
    per = pairs // calls
    blocks = [pl.BlockSpec((rows, 2 * HD), lambda i, c=c: (0, i + c * per)) for c in range(calls)]
    e_blocks = [pl.BlockSpec((2, rows, rows + size), lambda i, c=c: (i + c * per, 0, 0)) for c in range(calls)]
    grid = (per,)
    shared = (q, k, v, km, vm, often)
    results = [((2 * pairs, rows, rows + size), BF16), row_bf, row_f]
    begun = ()
    for call in range(calls - 1):
        e, mixed, linv = line.blocks(
            attend_kernel, results, f"attend_{call}", shared + begun, grid,
            [blocks[call]] * 5 + [VMEM] + [ANY] * len(begun), [e_blocks[call]] + [blocks[call]] * 2,
            far=(0,), limit=20, aliases={6 + i: i for i in range(len(begun))}, there=(6,) if begun else (),
        )
        begun = (e, mixed, linv)
    cot_sib = swap(cot, "core")
    e, mixed, linv, resid, *normed2 = line.blocks(
        attend_more_kernel, results + [row_f, half_bf, half_bf], "attend_more",
        shared + begun + (w_attn_out, table, arr), grid,
        [blocks[-1]] * 5 + [VMEM, ANY, pl.BlockSpec((rows, (calls - 1) * per * 2 * HD), lambda i: (0, 0)), ANY] + [VMEM] * 3,
        [e_blocks[-1]] + [blocks[-1]] * 2 + [VMEM] * 3,
        scratch=[pltpu.VMEM((rows, width), BF16)], aliases={6: 0, 7: 1, 8: 2}, far=(0,), limit=24, there=(6,),
        after=(cot_sib,),
    )
    normed2 += [swap(half, "core") for half in normed2]
    far_in, far_out = hold(far_cut, *normed2[2:]), hold(far_out, *normed2[2:])
    more_in, more_out = swap(far_in, "x"), swap(far_out, "z1")
    part, both = ((third, width), BF16), ((2, rows, width), BF16)
    bias_f, stacked = ((1, units), F32), ((width + units, width), BF16)
    out_own, gx_own, g_own, gb_own = line.call(
        mlp_kernel, [both, both, stacked, bias_f], "mlp_own",
        (*normed2, cot, cot_sib, w_mlp_in, table, w_mlp_out), limit=18,
        scratch=[pltpu.VMEM((2 * rows, units), BF16)] * 2,
    )
    half_bias, rows_of = ((1, units // 2), F32), (*normed2, cot, cot_sib)
    scratch = [pltpu.VMEM((2 * rows, units // 2), BF16)] * 2
    out_far, gx_far, g_far, gb_far = line.call(
        lambda *refs: mlp_far_kernel(False, *refs), [both, both, stacked, half_bias], "mlp_far",
        (info, *rows_of, far_in, far_out), small=1, limit=14, scratch=scratch,
    )
    out_other, gx_other, g_far, gb_other = line.start(
        lambda *refs: mlp_far_kernel(True, *refs), [both, both, stacked, half_bias], "mlp_other",
        (info, *rows_of, more_in, more_out, g_far), (1,), [SMALL] + [VMEM] * 9, [VMEM] * 4, scratch, limit=14, aliases={9: 2},
    )
    gx_keep, gx_send = line.call(merge_kernel, [row_bf] * 2, "merge", (gx_own, gx_far, gx_other))
    gx_came = swap(gx_send, "core")
    rounds = Rounds(line, info)
    mlp_items, at = [], 0
    for order, count in MLP_PARTS:
        mlp_items.append(Item(steps_of(order, True), (g_own, at, count), (g_far, at, count)))
        at += count
    rounds.go("a", mlp_items)

    grad_mixed, grad_resid, gwo, vecs_mid, *out_send = line.call(
        middle_kernel, [row_bf, row_f, square_bf, vec_f, half_bf, half_bf], "middle",
        (gx_keep, gx_came, resid, cot, table, mixed, w_attn_out, out_own, out_far, out_other),
    )
    out_came = [swap(half, "core") for half in out_send]
    grads = ()
    back = 2 if pairs % 2 == 0 else 1
    per = pairs // back
    blocks = [pl.BlockSpec((rows, 2 * HD), lambda i, c=c: (0, i + c * per)) for c in range(back)]
    e_blocks = [pl.BlockSpec((2, rows, rows + size), lambda i, c=c: (i + c * per, 0, 0)) for c in range(back)]
    grid = (per,)
    for which in range(back):
        grads = line.blocks(
            attend_back_kernel, [row_bf] * 5, f"attend_back_{which}", (q, k, v, km, vm, e, linv, mixed, grad_mixed) + tuple(grads),
            grid, [blocks[which]] * 5 + [e_blocks[which]] + [blocks[which]] * 3 + [ANY] * len(grads),
            [blocks[which]] * 5, there=(5,), limit=20,
            scratch=[pltpu.VMEM((2 * rows, rows + size), BF16)] + [pltpu.VMEM((2 * rows, 2 * HD), BF16)] * 2, aliases={9 + i: i for i in range(len(grads))},
        )
        if which == 0:
            (output,) = line.call(emit_kernel, [row_bf], "emit", (resid, out_own, out_far, out_other, *out_came, table), far=(0,))
    dq, dk, dv, dkm, dvm = grads
    rounds.go("b", mlp_items)
    send, *keeps = line.call(
        weight_grads_kernel, [((2 * width, width), BF16)] + [((count, width), BF16) for _, count in ATTN_PARTS], "weight_grads",
        (info, normed, recalled, dq, dk, dv, dkm, dvm, gwo), small=1, scratch=[pltpu.VMEM((width, width), BF16)],
    )
    core_came = swap(send, "core")
    attn_items, at = [], 0
    for (order, count), kept in zip(ATTN_PARTS, keeps):
        attn_items.append(Item(steps_of(order, False), (kept, 0, count), now=("half", "core"), came=(core_came, at)))
        at += count
    grad_memory, vecs_rec = line.call(
        recall_back_kernel, [row_bf, vec_f], "recall_back", (info, dkm, dvm, w_key, w_value, fit, arrived), small=1,
    )
    handed = from_behind(grad_memory, "mp", -1)
    gn, vecs = line.call(
        project_back_kernel, [row_f, ((16, width), BF16)], "project_back",
        (info, arr, dq, dk, dv, dvm, w_query, w_key, w_value, vecs_mid, vecs_rec, gb_own, gb_far, gb_other), small=1,
    )
    rounds.go("c", mlp_items + attn_items)
    (grad_hidden,) = line.call(
        last_kernel, [row_f], "last", (arr, table, gn, handed, grad_resid), far=(0,)
    )
    vec_item = Item([("swap", link) for link in ["z2"] + more_links() + ["x", "z1", "y"]], (vecs, 0, 16))
    rounds.go("d", mlp_items + attn_items)
    for link in more_links():
        rounds.go("d" + link, mlp_items)
    rounds.go("e", mlp_items + attn_items)
    rounds.go("f", mlp_items + attn_items + [vec_item])
    for link in more_links():
        rounds.go("f" + link, attn_items + [vec_item])
    mlp_now = [(*item.kept[0], *item.came, item.now[1]) for item in mlp_items]
    rounds.go("g", attn_items + [vec_item])
    plan, operands, at = [], [], 0
    for own, first, count, came, came_at, link in mlp_now:
        plan.append((link, count, first, came_at, at))
        operands += [own, came]
        at += 2 * count
    gw_in, gw_out = line.call(
        lambda *refs: mlp_grads_kernel(plan, *refs), [((width, units), F32), ((units, width), F32)], "mlp_grads",
        (info, *operands), small=1, far=(0, 1), scratch=[pltpu.VMEM((width + units, width), BF16)], limit=24,
    )
    rounds.go("h", attn_items + [vec_item])
    rounds.go("i", attn_items + [vec_item], mirror=True)
    mirror = rounds.mirror

    def squares(name, arrays, plan, begun=(), vectors=()):
        starts, at = [], 0
        for _, rows_of in ATTN_PARTS:
            starts.append((at, rows_of // 8))
            at += rows_of // 4
        plan = [block + starts[block[0]] for block in plan]
        count, more = len(arrays), 9 if vectors else 0
        scratch = [pltpu.VMEM((block[-1], width), F32) for block in plan for _ in range(4)] + [pltpu.SemaphoreType.DMA((4 * len(plan) + more,))]
        return line.start(
            lambda *refs: squares_kernel(plan, count, len(begun), vectors, *refs), [square_f] * 4 + [((width,), F32)] * more, name,
            (info, *arrays, *begun), (1,), [SMALL] + [VMEM] * count + [HBM] * len(begun), [HBM] * (4 + more),
            scratch + [pltpu.VMEM((width,), F32)] * more, far=tuple(range(4 + more)), limit=16,
            there=tuple(range(1 + count, 1 + count + len(begun))), aliases={1 + count + i: i for i in range(len(begun))},
        )

    own = [item.kept[0] for item in attn_items]
    parts = range(len(ATTN_PARTS))
    plan = [(part, True, True, part, own[part][1]) for part in parts]
    at = 0
    for part, item in enumerate(attn_items):
        plan.append((part, False, True, len(parts), at))
        at += item.kept[0][2]
    begun = squares("squares_1", [array for array, _, _ in own] + [mirror], plan)
    came = [(hold(item.came[0], line.last), item.came[1]) for item in attn_items]
    passed = [swap(array, "core") for array, _ in came]
    begun = squares(
        "squares_2", [array for array, _ in came], [(part, True, False, part, came[part][1]) for part in parts], begun
    )
    vec_part = [item.now[1] for item in attn_items].index(vec_item.now[1])
    vec_own, vec_came = vec_item.kept[0], vec_item.came
    gwq, gwk, gwv, gwo, *vecs = squares(
        "squares_3", passed + [vec_own[0], vec_came[0], mirror],
        [(part, False, False, part, came[part][1]) for part in parts], begun,
        (
            (len(parts), vec_own[1]), (len(parts) + 1, vec_came[1]), (len(parts) + 2, at), (vec_part, vec_came[1])
        ),
    )
    return (
        output[None],
        grad_hidden[None],
        vecs[0],
        vecs[1],
        gwq,
        vecs[2],
        gwk,
        gwv,
        vecs[3],
        gwo,
        vecs[4],
        vecs[5],
        vecs[6],
        gw_in,
        vecs[8],
        gw_out,
        vecs[7],
    )


def solution(mesh):
    rows = P("dp", "mp", None)
    placed = (rows, P("dp", None, None), P("dp"), rows) + (P(),) * 11
    placed += (P(None, "mp"), P("mp"), P("mp", None), P(), rows)
    return jax.shard_map(
        local,
        mesh=mesh,
        in_specs=placed,
        out_specs=(rows, rows) + (P(),) * 11 + (P(None, "mp"), P("mp"), P("mp", None), P()),
        check_vma=False,
    )
```

```python
import math

import jax
import jax.numpy as jnp
from jax import lax
from jax.experimental import pallas as pl
from jax.experimental.pallas import tpu as pltpu
from jax.sharding import PartitionSpec as P

HD = 64
NORM_EPSILON = 1e-05
RIDGE_WEIGHT = 0.1
NOTHING = -1e30
GELU_SLOPE = math.sqrt(2.0 / math.pi)
GELU_CUBE = 0.044715
F32 = jnp.float32
BF16 = jnp.bfloat16
MEBI = 1 << 20


def mm(left, right):
    return jnp.dot(left, right, preferred_element_type=F32)


def mt(left, right):
    return lax.dot_general(left, right, (((1,), (1,)), ((), ())), preferred_element_type=F32)


def tm(left, right):
    return lax.dot_general(left, right, (((0,), (0,)), ((), ())), preferred_element_type=F32)


def summed(first, *others):
    total = first.astype(F32)
    for other in others:
        total = total + other.astype(F32)
    return total.astype(BF16)


def column_sum(values):
    return jnp.sum(values, axis=0, keepdims=True)


def normalized(values):
    row_mean = jnp.mean(values, axis=-1, keepdims=True)
    centered = values - row_mean
    row_var = jnp.mean(centered * centered, axis=-1, keepdims=True)
    inverse = lax.rsqrt(row_var + NORM_EPSILON)
    return centered * inverse, inverse


def norm_back(xhat, inverse, incoming, gain):
    g = incoming * gain
    mean_g = jnp.mean(g, axis=-1, keepdims=True)
    mean_gx = jnp.mean(g * xhat, axis=-1, keepdims=True)
    return inverse * (g - mean_g - xhat * mean_gx)


SMALL = pl.BlockSpec(memory_space=pltpu.SMEM)
VMEM = pl.BlockSpec(memory_space=pltpu.VMEM)
ANY = pl.BlockSpec(memory_space=pl.ANY)
HBM = pl.BlockSpec(memory_space=pltpu.HBM)


class Arriving:
    def __init__(self, source, held, sem):
        self.held, self.copy = held, pltpu.make_async_copy(source, held, sem)
        self.shape, self.dtype = held.shape, held.dtype
        self.here = False
        self.copy.start()

    def wait(self):
        if not self.here:
            self.copy.wait()
            self.here = True
        return self.held

    @property
    def at(self):
        return self.wait().at

    def __getitem__(self, index):
        return self.wait()[index]


class Leaving:
    def __init__(self, target, held, sem):
        self.held, self.copy = held, pltpu.make_async_copy(held, target, sem)
        self.shape, self.dtype = held.shape, held.dtype
        self.gone = False

    def leave(self):
        if not self.gone:
            self.copy.start()
            self.gone = True

    def __getitem__(self, index):
        return self.held[index]

    def __setitem__(self, index, value):
        self.held[index] = value
        if index is Ellipsis:
            self.leave()


class Line:
    def __init__(self):
        self.last = None

    def start(self, body, outs, name, operands, grid, in_specs, out_specs, scratch, after=(), aliases=None, far=(), limit=32, there=()):
        waits = list(after) + ([] if self.last is None else [self.last])
        operands = [pltpu.with_memory_space_constraint(o, pltpu.HBM) if i in there else o for i, o in enumerate(operands)]
        known, gone = len(operands), len(operands) + len(waits)
        results = pl.pallas_call(
            lambda *refs: body(*refs[:known], *refs[gone : gone + len(outs)], *refs[gone + len(outs) + 1 :]),
            out_shape=[(pltpu.HBM if i in far else pltpu.VMEM)(shape, dtype) for i, (shape, dtype) in enumerate(outs)]
            + [pltpu.VMEM((8, 128), F32)],
            grid=grid,
            in_specs=list(in_specs) + [ANY] * len(waits),
            out_specs=list(out_specs) + [VMEM],
            scratch_shapes=list(scratch),
            input_output_aliases=aliases or {},
            compiler_params=pltpu.CompilerParams(vmem_limit_bytes=limit * MEBI),
            cost_estimate=pl.CostEstimate(flops=0, bytes_accessed=0, transcendentals=0),
            name=name,
        )(*operands, *waits)
        *results, self.last = results
        return results

    def blocks(self, body, outs, name, operands, grid, in_specs, out_specs, scratch=(), **more):
        return self.start(body, outs, name, operands, grid, in_specs, out_specs, scratch, **more)

    def call(self, body, outs, name, operands, small=0, load=(), far=(), scratch=(), after=(), limit=16):
        outs = list(outs) + [(operands[i].shape, operands[i].dtype) for i in load]
        own, kept = len(scratch), len(outs) - len(load)
        in_specs = [SMALL if i < small else HBM if i in load else VMEM for i in range(len(operands))]
        out_specs = [HBM if i in far else VMEM for i in range(len(outs))]
        held = [pltpu.VMEM(*outs[i]) for i in far]
        sems = [pltpu.SemaphoreType.DMA((len(far) + len(load),))] if far or load else []

        def run(*refs):
            ins, targets, rest = refs[: len(operands)], refs[len(operands) : len(operands) + len(outs)], refs[len(operands) + len(outs) :]
            mine, buffers, sem = rest[:own], rest[own:], rest[-1] if sems else None
            ins, targets = list(ins), list(targets)
            for slot, i in enumerate(load):
                ins[i] = Arriving(ins[i], targets[kept + slot], sem.at[len(far) + slot])
            for slot, i in enumerate(far):
                targets[i] = Leaving(targets[i], buffers[slot], sem.at[slot])
            body(*ins, *targets[:kept], *mine)
            for i in load:
                ins[i].wait()
            for i in far:
                targets[i].leave()
            for i in far:
                targets[i].copy.wait()

        return self.start(
            run, outs, name, operands, (1,), in_specs, out_specs, list(scratch) + held + sems, after, far=far, limit=limit,
            there=tuple(load),
        )


def hold(value, *until):
    return lax.optimization_barrier((value,) + until)[0]


def at_half(bit, count):
    return pl.ds(pl.multiple_of(bit * count, count), count)


def fit_at_positions(size, fit_ref):
    half = size // 2
    spread = 1.0 / size
    row = lax.broadcasted_iota(jnp.int32, (half, half), 0)
    col = lax.broadcasted_iota(jnp.int32, (half, half), 1)
    eye = jnp.where(row == col, 1.0, 0.0).astype(F32)
    flip = jnp.where(row + col == half - 1, 1.0, 0.0).astype(BF16)

    def design(columns):
        apart = (row.astype(F32) + 0.5) / size - (columns.astype(F32) + 0.5) / size
        return jnp.exp(-(apart * apart) / (2.0 * spread * spread))

    def pieces(value):
        high = value.astype(BF16)
        return high, (value - high.astype(F32)).astype(BF16)

    def exact(left, right):
        (left_high, left_low), (right_high, right_low) = pieces(left), pieces(right)
        return mm(left_high, right_high) + (mm(left_high, right_low) + mm(left_low, right_high))

    def full(left, right):
        return jnp.dot(left, right, precision=lax.Precision.HIGHEST, preferred_element_type=F32)

    direct, mirrored = design(col), design(size - 1 - col)
    brackets, guesses = [], []
    for part in (direct + mirrored, direct - mirrored):
        bracket = full(part, part) + RIDGE_WEIGHT * eye
        low = bracket.astype(BF16)
        brackets.append(bracket)
        guesses.append(2.39060839 * eye - 0.96134588 * bracket + 0.09859958 * mm(low, low))
    for step in range(6):
        for which in range(2):
            bracket, guess = brackets[which], guesses[which]
            if step < 4:
                low = guess.astype(BF16)
                left = 2.0 * eye - mm(bracket.astype(BF16), low)
                guesses[which] = mm(low, left.astype(BF16))
            else:
                guesses[which] = exact(guess, 2.0 * eye - exact(bracket, guess))
    even, odd = (eye - RIDGE_WEIGHT * guess for guess in guesses)
    inner = (0.5 * (even + odd)).astype(BF16)
    outer = (0.5 * (even - odd)).astype(BF16)
    fit_ref[0:half, 0:half] = inner
    fit_ref[0:half, half:size] = mm(outer, flip).astype(BF16)
    fit_ref[half:size, 0:half] = mm(flip, outer).astype(BF16)
    fit_ref[half:size, half:size] = mm(flip, mm(inner, flip).astype(BF16)).astype(BF16)


VECTORS = ("gain1", "shift1", "b_q", "b_v", "b_o", "gain2", "shift2", "b_in", "b_out")


def vector(table, name):
    at = VECTORS.index(name)
    return table[at : at + 1, :]


def start_kernel(info, w_in, w_out, *refs):
    vectors, (fit, table, cut_in, cut_out) = refs[: len(VECTORS)], refs[-4:]
    fit_at_positions(fit.shape[0], fit)
    table[...] = jnp.zeros_like(table)
    for at, value in enumerate(vectors):
        table[at, :] = value[...]
    count = cut_in.shape[1]
    mine = at_half(scalar(info, "half"), count)
    cut_in[...] = w_in[:, mine]
    bias, pieces = vector(table, "b_in"), []
    for _ in range(3):
        pieces.append(bias.astype(BF16))
        bias = bias - pieces[-1].astype(F32)
    cut_out[0:count, :] = w_out[mine, :]
    cut_out[count:, :] = jnp.concatenate(pieces + [jnp.zeros((13, table.shape[1]), BF16)], axis=0)


def front_kernel(hidden, table, wq, wk, wv, normed, q, k, v):
    xhat, _ = normalized(hidden[...].astype(F32))
    low = (xhat * vector(table, "gain1") + vector(table, "shift1")).astype(BF16)
    normed[...] = low
    scale = 1.0 / math.sqrt(HD)
    q[...] = (mm(low, wq[...]) + vector(table, "b_q")).astype(BF16) * jnp.asarray(scale, BF16)
    k[...] = mm(low, wk[...]).astype(BF16)
    v[...] = (mm(low, wv[...]) + vector(table, "b_v")).astype(BF16)


def memory_kernel(info, arrived, past, positions, table, fit, wk, wv, recalled, km, vm, often):
    size = fit.shape[0]
    xhat, _ = normalized(arrived[...].astype(F32))
    before = xhat * vector(table, "gain1") + vector(table, "shift1")
    kept = past[...].astype(F32) * (1 - scalar(info, "reset")).astype(F32)
    earlier = jnp.where(scalar(info, "first") > 0, kept, before).astype(BF16)
    low = mm(fit[...], earlier).astype(BF16)
    recalled[...] = low
    km[...] = mm(low, wk[...]).astype(BF16)
    vm[...] = (mm(low, wv[...]) + vector(table, "b_v")).astype(BF16)
    place = lax.broadcasted_iota(jnp.int32, (size, positions.shape[1]), 0)
    hit = jnp.where(place == positions[...], 1.0, 0.0).astype(BF16)
    count = mt(jnp.ones((8, positions.shape[1]), BF16), hit)
    often[...] = jnp.where(count > 0.5, jnp.log(jnp.maximum(count, 1.0)), NOTHING)


def attend_pair(q, k, v, km, vm, often, e, mixed, linv):
    rows = q.shape[0]
    half = rows // 2
    lane = lax.broadcasted_iota(jnp.int32, (1, 2 * HD), 1)
    row = lax.broadcasted_iota(jnp.int32, (half, half), 0)
    col = lax.broadcasted_iota(jnp.int32, (half, half), 1)
    log_count = often[0:1, :]
    units = [(part, head) for part in range(2) for head in range(2)]
    scores = {}
    for part, head in units:
        here = slice(part * half, (part + 1) * half)
        mine = (lane >= head * HD) & (lane < (head + 1) * HD)
        query = jnp.where(mine, q[here, :], jnp.zeros((), BF16))
        near = mt(query, k[0 : (part + 1) * half, :])
        far = mt(query, km[...]) + log_count
        edge = jnp.where(col > row, NOTHING, near[:, part * half :])
        top = jnp.maximum(jnp.max(edge, axis=-1, keepdims=True), jnp.max(far, axis=-1, keepdims=True))
        if part:
            top = jnp.maximum(top, jnp.max(near[:, : part * half], axis=-1, keepdims=True))
        scores[part, head] = (near, edge, far, top)
    for part in range(2):
        here = slice(part * half, (part + 1) * half)
        seen = (part + 1) * half
        results = []
        for head in range(2):
            near, edge, far, top = scores[part, head]
            edge = jnp.exp(edge - top)
            far = jnp.exp(far - top)
            total = jnp.sum(edge, axis=-1, keepdims=True) + jnp.sum(far, axis=-1, keepdims=True)
            edge_low, far_low = edge.astype(BF16), far.astype(BF16)
            e[head, here, part * half : seen] = edge_low
            e[head, here, rows:] = far_low
            out = mm(edge_low, v[part * half : seen, :]) + mm(far_low, vm[...])
            if part:
                start = jnp.exp(near[:, : part * half] - top)
                total = total + jnp.sum(start, axis=-1, keepdims=True)
                start_low = start.astype(BF16)
                e[head, here, 0 : part * half] = start_low
                out = out + mm(start_low, v[0 : part * half, :])
            inverse = 1.0 / total
            results.append((out * inverse, inverse))
        first = lane < HD
        mixed[here, :] = jnp.where(first, results[0][0], results[1][0]).astype(BF16)
        linv[here, :] = jnp.where(first, results[0][1], results[1][1])


def attend_kernel(q, k, v, km, vm, often, *refs):
    e, mixed, linv = refs[-3:]
    attend_pair(q, k, v, km, vm, often, e, mixed, linv)


def attend_more_kernel(
    q, k, v, km, vm, often, e_done, mixed_done, linv_done, wo, table, hidden,
    e, mixed, linv, resid, normed2_a, normed2_b, every,
):
    step, rows = pl.program_id(0), q.shape[0]
    attend_pair(q, k, v, km, vm, often, e, mixed, linv)
    done, block = mixed_done.shape[1], mixed.shape[1]
    every[:, pl.ds(pl.multiple_of(done + step * block, block), block)] = mixed[...]

    @pl.when(step == pl.num_programs(0) - 1)
    def _():
        every[:, 0:done] = mixed_done[...]
        total = hidden[...].astype(F32) + mm(every[...], wo[...]) + vector(table, "b_o")
        resid[...] = total
        xhat, _ = normalized(total)
        normed2 = (xhat * vector(table, "gain2") + vector(table, "shift2")).astype(BF16)
        normed2_a[...] = normed2[: rows // 2]
        normed2_b[...] = normed2[rows // 2 :]


def mlp_block(x, cot, w_in, b_in, w_out):
    pre = mm(x, w_in) + b_in
    square = pre * pre
    bend = jnp.tanh(GELU_SLOPE * pre * (1.0 + GELU_CUBE * square))
    act = (0.5 * pre * (1.0 + bend)).astype(BF16)
    slope = 0.5 * (1.0 + bend) + (0.5 * GELU_SLOPE) * pre * (1.0 - bend * bend) * (1.0 + 3.0 * GELU_CUBE * square)
    gpre = (mt(cot, w_out) * slope).astype(BF16)
    return mm(act, w_out), mt(gpre, w_in), act, gpre


def mlp_kernel(xa, xb, xc, xd, cot0, cot1, w_in, b_in, w_out, out, gx, grads, g_bias, acts, gpres):
    block, width, units = xa.shape[0], xa.shape[1], acts.shape[1]
    bias = b_in[...] if b_in.shape[0] == 1 else vector(b_in, "b_in")
    parts = []
    for which, x in enumerate((xa, xb, xc, xd)):
        here, there = slice(which % 2 * block, (which % 2 + 1) * block), slice(which * block, (which + 1) * block)
        cot = (cot0, cot1)[which // 2]
        o, g, act, gpre = mlp_block(x[...], cot[here, :], w_in[...], bias, w_out[...])
        out[which // 2, here, :], gx[which // 2, here, :] = o.astype(BF16), g.astype(BF16)
        acts[there, :] = act
        gpres[there, :] = gpre
        parts.append((x, there))
    total = tm(xa[...], gpres[0:block, :])
    for x, there in parts[1:]:
        total = total + tm(x[...], gpres[there, :])
    grads[0:width, :] = total.astype(BF16)
    half = 2 * block
    grads[width : width + units, :] = (tm(acts[:half, :], cot0[...]) + tm(acts[half:, :], cot1[...])).astype(BF16)
    g_bias[...] = column_sum(gpres[...].astype(F32))


def mlp_far_kernel(other, info, xa, xb, xc, xd, cot0, cot1, w_in, w_out, *refs):
    out, gx, grads, g_bias, acts, gpres = refs[-6:]
    block, width, units = xa.shape[0], xa.shape[1], w_in.shape[1]
    half = scalar(info, "half")
    half = 1 - half if other else half
    mine = at_half(half, units)
    pieces = w_out[units : units + 16, mine].astype(F32)
    bias = pieces[0:1] + pieces[1:2] + pieces[2:3]
    parts = []
    for which, x in enumerate((xa, xb, xc, xd)):
        here, there = slice(which % 2 * block, (which % 2 + 1) * block), slice(which * block, (which + 1) * block)
        cot = (cot0, cot1)[which // 2]
        o, g, act, gpre = mlp_block(x[...], cot[here, :], w_in[...], bias, w_out[0:units, :])
        out[which // 2, here, :], gx[which // 2, here, :] = o.astype(BF16), g.astype(BF16)
        acts[there, :] = act
        gpres[there, :] = gpre
        parts.append((x, there))
    total = tm(xa[...], gpres[0:block, :])
    for x, there in parts[1:]:
        total = total + tm(x[...], gpres[there, :])
    grads[0:width, mine] = total.astype(BF16)
    total = tm(acts[: 2 * block, :], cot0[...]) + tm(acts[2 * block :, :], cot1[...])
    grads[pl.ds(pl.multiple_of(width + half * units, 128), units), :] = total.astype(BF16)
    g_bias[...] = column_sum(gpres[...].astype(F32))


def merge_kernel(gx, gx_far, gx_other, keep_gx, send_gx):
    keep_gx[...] = summed(gx[0], gx_far[0], gx_other[0])
    send_gx[...] = summed(gx[1], gx_far[1], gx_other[1])


def middle_kernel(
    gx, gx_more, resid, cot, table, mixed, wo, out_own, out_far, out_other, grad_mixed, grad_resid, gwo, vecs,
    send_a, send_b
):
    half = send_a.shape[0]
    send_a[...] = summed(out_own[1, 0:half, :], out_far[1, 0:half, :], out_other[1, 0:half, :])
    send_b[...] = summed(out_own[1, half:, :], out_far[1, half:, :], out_other[1, half:, :])
    xhat, inverse = normalized(resid[...])
    n = gx[...].astype(F32) + gx_more[...].astype(F32)
    cot_full = cot[...].astype(F32)
    total = cot_full + norm_back(xhat, inverse, n, vector(table, "gain2"))
    grad_resid[...] = total
    low = total.astype(BF16)
    grad_mixed[...] = mt(low, wo[...]).astype(BF16)
    gwo[...] = tm(mixed[...], low).astype(BF16)
    vecs[...] = jnp.concatenate(
        [
            column_sum(low.astype(F32)),
            column_sum(n * xhat),
            column_sum(n),
            column_sum(cot_full),
            jnp.zeros((4, n.shape[1]), F32),
        ],
        axis=0,
    )


def attend_back_kernel(q, k, v, km, vm, e, linv, mixed, gmix, *refs):
    dq, dk, dv, dkm, dvm, ds, queries, grads = refs[-8:]
    rows = q.shape[0]
    half = rows // 2
    lane = lax.broadcasted_iota(jnp.int32, (1, 2 * HD), 1)
    scale = 1.0 / math.sqrt(HD)
    grad = gmix[...].astype(F32) * linv[...]
    product = grad * mixed[...].astype(F32)
    for head in range(2):
        mine = (lane >= head * HD) & (lane < (head + 1) * HD)
        all_rows = slice(head * rows, (head + 1) * rows)
        queries[all_rows, :] = jnp.where(mine, q[...], jnp.zeros((), BF16))
        grads[all_rows, :] = jnp.where(mine, grad, 0.0).astype(BF16)
    for head in range(2):
        mine = (lane >= head * HD) & (lane < (head + 1) * HD)
        dots = jnp.sum(jnp.where(mine, product, 0.0), axis=-1, keepdims=True)
        for part in range(2):
            here = slice(part * half, (part + 1) * half)
            there = slice(head * rows + part * half, head * rows + (part + 1) * half)
            seen = (part + 1) * half
            dot, grad_low = dots[here], grads[there, :]
            near = e[head, here, 0:seen].astype(F32) * (mt(grad_low, v[0:seen, :]) - dot)
            far = e[head, here, rows:].astype(F32) * (mt(grad_low, vm[...]) - dot)
            ds[there, 0:seen] = near.astype(BF16)
            ds[there, rows:] = far.astype(BF16)
    for part in range(2):
        here = slice(part * half, (part + 1) * half)
        seen = (part + 1) * half
        parts = []
        for head in range(2):
            there = slice(head * rows + part * half, head * rows + (part + 1) * half)
            parts.append(mm(ds[there, 0:seen], k[0:seen, :]) + mm(ds[there, rows:], km[...]))
        dq[here, :] = (jnp.where(lane < HD, parts[0], parts[1]) * scale).astype(BF16)
    late = [slice(head * rows + half, (head + 1) * rows) for head in range(2)]

    def both(left, right):
        first = tm(left[...], right(slice(0, half)))
        second = sum(tm(left[at, :], right(slice(half, rows), head)) for head, at in enumerate(late))
        return first, second, tm(left[...], right(slice(rows, None)))

    def scores(columns, head=None):
        return ds[:, columns] if head is None else ds[late[head], columns]

    def weights(columns, head=None):
        if head is None:
            return e[:, :, columns].reshape(2 * rows, -1)
        return e[head, half:, columns]

    for left, right, near, far in ((queries, scores, dk, dkm), (grads, weights, dv, dvm)):
        first, second, rest = both(left, right)
        near[0:half, :] = first.T.astype(BF16)
        near[half:, :] = second.T.astype(BF16)
        far[...] = rest.T.astype(BF16)


def recall_back_kernel(info, dkm, dvm, wk, wv, fit, arrived, grad_memory, vecs):
    grad_recalled = (mt(dkm[...], wk[...]) + mt(dvm[...], wv[...])).astype(BF16)
    handed = tm(fit[...], grad_recalled).astype(BF16)
    grad_memory[...] = handed
    xhat, _ = normalized(arrived[...].astype(F32))
    n = jnp.where(scalar(info, "first") > 0, 0.0, handed.astype(F32))
    vecs[...] = jnp.concatenate([column_sum(n * xhat), column_sum(n), jnp.zeros((6, n.shape[1]), F32)], axis=0)


def weight_grads_kernel(info, normed, recalled, dq, dk, dv, dkm, dvm, gwo, send, *refs):
    low, rec = normed[...], recalled[...]
    *parts, whole = refs
    half = whole.shape[0] // 2
    core = scalar(info, "core")
    grads = (
        lambda: tm(low, dq[...]),
        lambda: tm(low, dk[...]) + tm(rec, dkm[...]),
        lambda: tm(low, dv[...]) + tm(rec, dvm[...]),
        None,
    )
    for which, grad in enumerate(grads):
        source = gwo
        if grad is not None:
            whole[...] = grad().astype(BF16)
            source = whole
        start = begin = 0
        for part in parts:
            piece = part.shape[0] // 8
            for first in range(2):
                at = (4 * first + which) * piece
                send[begin + at : begin + at + piece, :] = source[
                    pl.ds(pl.multiple_of((1 - core) * half + start, 16), piece), :
                ]
                part[at : at + piece, :] = source[pl.ds(pl.multiple_of(core * half + start, 16), piece), :]
                start += piece
            begin += part.shape[0]


def project_back_kernel(info, hidden, dq, dk, dv, dvm, wq, wk, wv, vecs_mid, vecs_rec, gb_own, gb_far, gb_other, gn, vecs):
    width = hidden.shape[1]
    n = mt(dq[...], wq[...]) + mt(dk[...], wk[...]) + mt(dv[...], wv[...])
    gn[...] = n
    xhat, _ = normalized(hidden[...].astype(F32))
    shard = lax.broadcasted_iota(jnp.int32, (4, 1), 0)
    halves = [gb_far[...], gb_other[...]]
    far = jnp.where(scalar(info, "half") == 0, jnp.concatenate(halves, axis=1), jnp.concatenate(halves[::-1], axis=1))
    bias_rows = jnp.where(shard == scalar(info, "me"), gb_own[...], 0.0) + jnp.where(shard == scalar(info, "far"), far, 0.0)
    vecs[...] = jnp.concatenate(
        [
            column_sum(n * xhat) + vecs_rec[0:1, :],
            column_sum(n) + vecs_rec[1:2, :],
            column_sum(dq[...].astype(F32)),
            column_sum(dv[...].astype(F32)) + column_sum(dvm[...].astype(F32)),
            vecs_mid[0:4, :],
            bias_rows,
            jnp.zeros((4, width), F32),
        ],
        axis=0,
    ).astype(BF16)


def last_kernel(hidden, table, gn, handed, grad_resid, grad_hidden):
    xhat, inverse = normalized(hidden[...].astype(F32))
    n = gn[...] + handed[...].astype(F32)
    grad_hidden[...] = grad_resid[...] + norm_back(xhat, inverse, n, vector(table, "gain1"))


def added(left, right):
    return (left.astype(F32) + right.astype(F32)).astype(BF16)


MLP_PARTS = (
    (("y", "x", "z2", "z1"), 384), (("y", "z1", "x", "z2"), 128), (("x", "y", "z2", "z1"), 128),
    (("x", "z1", "y", "z2"), 384), (("z1", "y", "x", "z2"), 384), (("z1", "x", "y", "z2"), 128),
)
ATTN_PARTS = ((("y", "z1", "x", "z2"), 512), (("x", "y", "z1", "z2"), 512), (("z1", "x", "y", "z2"), 512))
AXES = {"core": ("mp", 1), "y": ("mp", 2), "x": ("dp", 1), "z1": ("dp", 2), "z2": ("dp", 4)}


def swap(value, link):
    axis, mask = AXES[link] if link in AXES else ("dp", int(link))
    return lax.ppermute(value, axis, [(i, i ^ mask) for i in range(lax.axis_size(axis))])


def bit_of(link):
    axis, mask = AXES[link]
    return (lax.axis_index(axis) // mask) % 2


SCALAR = {"core": 0, "y": 1, "x": 2, "z1": 3, "z2": 4, "me": 5, "far": 6, "first": 7, "reset": 8, "half": 9}


def scalar_array(reset):
    bit = {link: bit_of(link) for link in AXES}
    me = lax.axis_index("mp")
    values = dict(bit, me=me, far=me ^ 2, first=me == 0, reset=reset, half=bit["x"] ^ bit["z1"])
    row = lax.broadcasted_iota(jnp.int32, (1, 16), 1)
    packed = jnp.zeros((1, 16), jnp.int32)
    for name, value in values.items():
        packed = jnp.where(row == SCALAR[name], jnp.asarray(value, jnp.int32), packed)
    return packed


def scalar(info, name):
    return info[0, SCALAR[name]]


class Item:
    def __init__(self, steps, *kept, now=None, came=None):
        self.steps, self.kept, self.now, self.came = list(steps), list(kept), now, came


class Rounds:
    def __init__(self, line, info):
        self.line, self.info = line, info

    def go(self, name, items, mirror=False):
        arrays, sends, outs, jobs = [], {}, [], []

        def slot(array):
            for which, known in enumerate(arrays):
                if known is array:
                    return which
            arrays.append(array)
            return len(arrays) - 1

        for item in items:
            kind, link = item.now or ("start", None)
            came, at = (slot(item.came[0]), item.came[1]) if link else (None, 0)
            sources = []
            for array, first, rows in item.kept:
                sources.append((slot(array), first, came, at, rows, kind, link))
                at += rows
            rows = item.kept[0][2] * (2 if kind == "double" else 1)
            step = item.steps.pop(0) if item.steps else None
            sent = sends.setdefault(step[1], [0]) if step else None
            if step is None:
                jobs.append((sources[0], "all", None, len(outs), 0, rows))
                item.kept = [("out", len(outs), rows)]
                outs.append(rows)
            elif step[0] in ("swap", "double"):
                jobs.append((sources[0], "all", None, step[1], sent[0], rows))
                item.came, item.kept = (None, sent[0]), [(step[1], sent[0], rows)]
                sent[0] += rows
                if mirror:
                    again = sends.setdefault("core", [0])
                    jobs.append((sources[0], "all", None, "core", again[0], rows))
                    again[0] += rows
            elif step[0] == "pair":
                jobs.append((sources[0], "all", None, len(outs), 0, rows))
                jobs.append((sources[1], "all", None, step[1], sent[0], rows))
                item.came, item.kept = (None, sent[0]), [("out", len(outs), rows)]
                sent[0] += rows
                outs.append(rows)
            else:
                half, kept = rows // 2, []
                item.came = (None, sent[0])
                for source in sources:
                    jobs.append((source, "mine", step[1], len(outs), 0, half))
                    jobs.append((source, "other", step[1], step[1], sent[0], half))
                    kept.append(("out", len(outs), half))
                    sent[0] += half
                    outs.append(half)
                item.kept = kept
            item.now = step
        links = list(sends)
        width = arrays[0].shape[1]
        shapes = [((rows, width), BF16) for rows in outs] + [((sends[link][0], width), BF16) for link in links]

        def body(info, *refs):
            ins, results = refs[: len(arrays)], refs[len(arrays) :]
            for (kept, first, came, at, rows, kind, over), what, link, target, base, count in jobs:
                out = results[len(outs) + links.index(target) if isinstance(target, str) else target]
                if kind == "double":
                    for bit, ref, start in ((scalar(info, over), kept, first), (1 - scalar(info, over), came, at)):
                        out[pl.ds(pl.multiple_of(base + bit * rows, 16), rows), :] = ins[ref][start : start + rows, :]
                    continue
                start = 0
                if what != "all":
                    bit = scalar(info, link)
                    start = (bit if what == "mine" else 1 - bit) * count

                def here(base):
                    if what == "all":
                        return slice(base, base + count)
                    return pl.ds(pl.multiple_of(base + start, 16), count)

                value = ins[kept][here(first), :]
                if kind != "start":
                    value = added(value, ins[came][here(at), :])
                out[base : base + count, :] = value

        results = self.line.call(body, shapes, f"round_{name}", (self.info, *arrays), small=1, limit=4)
        sent = dict(zip(links, results[len(outs) :]))
        arrived = {link: swap(array, link) for link, array in sent.items()}
        self.mirror = arrived.get("core")
        for item in items:
            if item.now:
                item.came = (arrived[item.now[1]], item.came[1])
            item.kept = [
                (results[first], 0, rows) if where == "out" else (sent[where], first, rows) for where, first, rows in item.kept
            ]


def more_links():
    return [str(8 << bit) for bit in range((lax.axis_size("dp") // 8).bit_length() - 1)]


def steps_of(order, paired):
    first = [("pair" if link == "y" and paired else "half", link) for link in order[:3]]
    back = [("double", link) for link in order[2::-1] if not (link == "y" and paired)]
    return first + [("swap", link) for link in [order[3]] + more_links()] + back


def squares_kernel(plan, count, skip, vectors, info, *refs):
    ins, rest = refs[:count], refs[count + skip :]
    outs, rest = rest[:4], rest[4:]
    vecs, rest = (rest[:9], rest[9:]) if vectors else ((), rest)
    buffers, sems = rest[: 4 * len(plan)], rest[4 * len(plan)]
    copies = []

    def leave(buffer, target):
        copies.append(pltpu.make_async_copy(buffer, target, sems.at[len(copies)]))
        copies[-1].start()

    half = outs[0].shape[0] // 2
    for block, (part, this_core, this_half, array, first, start, piece) in enumerate(plan):
        core, bit = scalar(info, "core"), scalar(info, ATTN_PARTS[part][0][0])
        core, bit = core if this_core else 1 - core, bit if this_half else 1 - bit
        at = pl.ds(pl.multiple_of(core * half + start + bit * piece, 16), piece)
        for which, out in enumerate(outs):
            buffer = buffers[4 * block + which]
            buffer[...] = ins[array][first + which * piece : first + (which + 1) * piece, :].astype(F32)
            leave(buffer, out.at[at, :])
    if vectors:
        rows = [ins[array][first : first + 16, :].astype(F32) for array, first in vectors]
        total = (rows[0] + rows[1]) + (rows[2] + rows[3])
        me, row = scalar(info, "me"), total[8:9, :]
        for at in range(1, 4):
            row = jnp.where(me == at, total[8 + at : 9 + at, :], row)
        held = rest[4 * len(plan) + 1 :]
        for at, (buffer, out) in enumerate(zip(held, vecs)):
            buffer[...] = total[at, :] if at < 8 else row[0, :]
            leave(buffer, out)
    for copy in copies:
        copy.wait()


def mlp_grads_kernel(plan, info, *refs):
    ins, (gw_in, gw_out, whole) = refs[: 2 * len(plan)], refs[2 * len(plan) :]
    for which, (link, rows, own_at, came_at, base) in enumerate(plan):
        for bit, ref, at in ((scalar(info, link), ins[2 * which], own_at), (1 - scalar(info, link), ins[2 * which + 1], came_at)):
            whole[pl.ds(pl.multiple_of(base + bit * rows, 16), rows), :] = ref[at : at + rows, :]
    count = gw_in.shape[0]
    gw_in[...] = whole[:count, :].astype(F32)
    gw_out[...] = whole[count:, :].astype(F32)


def emit_kernel(resid, out_own, out_far, out_other, came_a, came_b, table, output):
    came = jnp.concatenate([came_a[...], came_b[...]], axis=0).astype(F32)
    total = resid[...] + summed(out_own[0], out_far[0], out_other[0]).astype(F32) + came + vector(table, "b_out")
    output[...] = total.astype(BF16)


def from_behind(value, axis, steps):
    count = lax.axis_size(axis)
    leading, last = (max(0, -steps), min(count, count - steps))
    return lax.ppermute(value, axis, [(source, source + steps) for source in range(leading, last)])


def local(
    hidden,
    past_states,
    reset_flags,
    sample_positions,
    norm1_gain,
    norm1_shift,
    w_query,
    bias_query,
    w_key,
    w_value,
    bias_value,
    w_attn_out,
    bias_attn_out,
    norm2_gain,
    norm2_shift,
    w_mlp_in,
    bias_mlp_in,
    w_mlp_out,
    bias_mlp_out,
    cotangent,
):
    rows, width = hidden.shape[1], hidden.shape[2]
    size = past_states.shape[1]
    units = w_mlp_in.shape[1]
    assert rows == size and sample_positions.shape[2] == size
    pairs = width // (2 * HD)
    arr, cot = hidden[0], cotangent[0]
    half_bf = ((rows // 2, width), BF16)
    row_bf, row_f = ((rows, width), BF16), ((rows, width), F32)
    square_f, square_bf, vec_f = ((width, width), F32), ((width, width), BF16), ((8, width), F32)

    line = Line()
    info = scalar_array(reset_flags[0])
    half_w, third = width // 2, 2 * width // 3

    arrived = from_behind(arr, "mp", 1)
    (
        fit, table, cut_in, cut_out,
        w_mlp_in, w_mlp_out, arr, w_query, w_key, w_value, past, positions, w_attn_out, cot, *_
    ) = line.call(
        start_kernel,
        [((size, size), BF16), ((16, width), F32), ((width, units // 2), BF16), ((units // 2 + 16, width), BF16)], "start",
        (
            info, w_mlp_in, w_mlp_out, norm1_gain, norm1_shift, bias_query, bias_value, bias_attn_out, norm2_gain,
            norm2_shift, bias_mlp_in, bias_mlp_out, arr, w_query, w_key, w_value, past_states[0], sample_positions[0],
            w_attn_out, cot,
        ),
        small=1, load=(1, 2, 12, 13, 14, 15, 16, 17, 18, 19) + tuple(range(3, 12)), far=(2, 3),
    )
    far_cut, far_out = swap(cut_in, "y"), swap(cut_out, "y")
    normed, q, k, v = line.call(front_kernel, [row_bf] * 4, "front", (arr, table, w_query, w_key, w_value))
    recalled, km, vm, often = line.call(
        memory_kernel, [row_bf] * 3 + [((8, size), F32)], "memory",
        (info, arrived, past, positions, table, fit, w_key, w_value), small=1,
    )

    calls = 3 if pairs % 3 == 0 else 1
    per = pairs // calls
    blocks = [pl.BlockSpec((rows, 2 * HD), lambda i, c=c: (0, i + c * per)) for c in range(calls)]
    e_blocks = [pl.BlockSpec((2, rows, rows + size), lambda i, c=c: (i + c * per, 0, 0)) for c in range(calls)]
    grid = (per,)
    shared = (q, k, v, km, vm, often)
    results = [((2 * pairs, rows, rows + size), BF16), row_bf, row_f]
    begun = ()
    for call in range(calls - 1):
        e, mixed, linv = line.blocks(
            attend_kernel, results, f"attend_{call}", shared + begun, grid,
            [blocks[call]] * 5 + [VMEM] + [ANY] * len(begun), [e_blocks[call]] + [blocks[call]] * 2,
            far=(0,), limit=20, aliases={6 + i: i for i in range(len(begun))}, there=(6,) if begun else (),
        )
        begun = (e, mixed, linv)
    cot_sib = swap(cot, "core")
    e, mixed, linv, resid, *normed2 = line.blocks(
        attend_more_kernel, results + [row_f, half_bf, half_bf], "attend_more",
        shared + begun + (w_attn_out, table, arr), grid,
        [blocks[-1]] * 5 + [VMEM, ANY, pl.BlockSpec((rows, (calls - 1) * per * 2 * HD), lambda i: (0, 0)), ANY] + [VMEM] * 3,
        [e_blocks[-1]] + [blocks[-1]] * 2 + [VMEM] * 3,
        scratch=[pltpu.VMEM((rows, width), BF16)], aliases={6: 0, 7: 1, 8: 2}, far=(0,), limit=24, there=(6,),
        after=(cot_sib,),
    )
    normed2 += [swap(half, "core") for half in normed2]
    far_in, far_out = hold(far_cut, *normed2[2:]), hold(far_out, *normed2[2:])
    more_in, more_out = swap(far_in, "x"), swap(far_out, "z1")
    part, both = ((third, width), BF16), ((2, rows, width), BF16)
    bias_f, stacked = ((1, units), F32), ((width + units, width), BF16)
    out_own, gx_own, g_own, gb_own = line.call(
        mlp_kernel, [both, both, stacked, bias_f], "mlp_own",
        (*normed2, cot, cot_sib, w_mlp_in, table, w_mlp_out), limit=18,
        scratch=[pltpu.VMEM((2 * rows, units), BF16)] * 2,
    )
    half_bias, rows_of = ((1, units // 2), F32), (*normed2, cot, cot_sib)
    scratch = [pltpu.VMEM((2 * rows, units // 2), BF16)] * 2
    out_far, gx_far, g_far, gb_far = line.call(
        lambda *refs: mlp_far_kernel(False, *refs), [both, both, stacked, half_bias], "mlp_far",
        (info, *rows_of, far_in, far_out), small=1, limit=14, scratch=scratch,
    )
    out_other, gx_other, g_far, gb_other = line.start(
        lambda *refs: mlp_far_kernel(True, *refs), [both, both, stacked, half_bias], "mlp_other",
        (info, *rows_of, more_in, more_out, g_far), (1,), [SMALL] + [VMEM] * 9, [VMEM] * 4, scratch, limit=14, aliases={9: 2},
    )
    gx_keep, gx_send = line.call(merge_kernel, [row_bf] * 2, "merge", (gx_own, gx_far, gx_other))
    gx_came = swap(gx_send, "core")
    rounds = Rounds(line, info)
    mlp_items, at = [], 0
    for order, count in MLP_PARTS:
        mlp_items.append(Item(steps_of(order, True), (g_own, at, count), (g_far, at, count)))
        at += count
    rounds.go("a", mlp_items)

    grad_mixed, grad_resid, gwo, vecs_mid, *out_send = line.call(
        middle_kernel, [row_bf, row_f, square_bf, vec_f, half_bf, half_bf], "middle",
        (gx_keep, gx_came, resid, cot, table, mixed, w_attn_out, out_own, out_far, out_other),
    )
    out_came = [swap(half, "core") for half in out_send]
    grads = ()
    back = 2 if pairs % 2 == 0 else 1
    per = pairs // back
    blocks = [pl.BlockSpec((rows, 2 * HD), lambda i, c=c: (0, i + c * per)) for c in range(back)]
    e_blocks = [pl.BlockSpec((2, rows, rows + size), lambda i, c=c: (i + c * per, 0, 0)) for c in range(back)]
    grid = (per,)
    for which in range(back):
        grads = line.blocks(
            attend_back_kernel, [row_bf] * 5, f"attend_back_{which}", (q, k, v, km, vm, e, linv, mixed, grad_mixed) + tuple(grads),
            grid, [blocks[which]] * 5 + [e_blocks[which]] + [blocks[which]] * 3 + [ANY] * len(grads),
            [blocks[which]] * 5, there=(5,), limit=20, after=out_came if which else (),
            scratch=[pltpu.VMEM((2 * rows, rows + size), BF16)] + [pltpu.VMEM((2 * rows, 2 * HD), BF16)] * 2, aliases={9 + i: i for i in range(len(grads))},
        )
    dq, dk, dv, dkm, dvm = grads
    rounds.go("b", mlp_items)
    send, *keeps = line.call(
        weight_grads_kernel, [((2 * width, width), BF16)] + [((count, width), BF16) for _, count in ATTN_PARTS], "weight_grads",
        (info, normed, recalled, dq, dk, dv, dkm, dvm, gwo), small=1, scratch=[pltpu.VMEM((width, width), BF16)],
    )
    core_came = swap(send, "core")
    attn_items, at = [], 0
    for (order, count), kept in zip(ATTN_PARTS, keeps):
        attn_items.append(Item(steps_of(order, False), (kept, 0, count), now=("half", "core"), came=(core_came, at)))
        at += count
    grad_memory, vecs_rec = line.call(
        recall_back_kernel, [row_bf, vec_f], "recall_back", (info, dkm, dvm, w_key, w_value, fit, arrived), small=1,
    )
    handed = from_behind(grad_memory, "mp", -1)
    gn, vecs = line.call(
        project_back_kernel, [row_f, ((16, width), BF16)], "project_back",
        (info, arr, dq, dk, dv, dvm, w_query, w_key, w_value, vecs_mid, vecs_rec, gb_own, gb_far, gb_other), small=1,
    )
    rounds.go("c", mlp_items + attn_items)
    (output,) = line.call(emit_kernel, [row_bf], "emit", (resid, out_own, out_far, out_other, *out_came, table), far=(0,))
    (grad_hidden,) = line.call(
        last_kernel, [row_f], "last", (arr, table, gn, handed, grad_resid), far=(0,)
    )
    vec_item = Item([("swap", link) for link in ["z2"] + more_links() + ["x", "z1", "y"]], (vecs, 0, 16))
    rounds.go("d", mlp_items + attn_items)
    for link in more_links():
        rounds.go("d" + link, mlp_items)
    rounds.go("e", mlp_items + attn_items)
    rounds.go("f", mlp_items + attn_items + [vec_item])
    for link in more_links():
        rounds.go("f" + link, attn_items + [vec_item])
    mlp_now = [(*item.kept[0], *item.came, item.now[1]) for item in mlp_items]
    rounds.go("g", attn_items + [vec_item])
    rounds.go("h", attn_items + [vec_item])
    plan, operands, at = [], [], 0
    for own, first, count, came, came_at, link in mlp_now:
        plan.append((link, count, first, came_at, at))
        operands += [own, came]
        at += 2 * count
    gw_in, gw_out = line.call(
        lambda *refs: mlp_grads_kernel(plan, *refs), [((width, units), F32), ((units, width), F32)], "mlp_grads",
        (info, *operands), small=1, far=(0, 1), scratch=[pltpu.VMEM((width + units, width), BF16)], limit=24,
    )
    rounds.go("i", attn_items + [vec_item], mirror=True)
    mirror = rounds.mirror

    def squares(name, arrays, plan, begun=(), vectors=()):
        starts, at = [], 0
        for _, rows_of in ATTN_PARTS:
            starts.append((at, rows_of // 8))
            at += rows_of // 4
        plan = [block + starts[block[0]] for block in plan]
        count, more = len(arrays), 9 if vectors else 0
        scratch = [pltpu.VMEM((block[-1], width), F32) for block in plan for _ in range(4)] + [pltpu.SemaphoreType.DMA((4 * len(plan) + more,))]
        return line.start(
            lambda *refs: squares_kernel(plan, count, len(begun), vectors, *refs), [square_f] * 4 + [((width,), F32)] * more, name,
            (info, *arrays, *begun), (1,), [SMALL] + [VMEM] * count + [HBM] * len(begun), [HBM] * (4 + more),
            scratch + [pltpu.VMEM((width,), F32)] * more, far=tuple(range(4 + more)), limit=16,
            there=tuple(range(1 + count, 1 + count + len(begun))), aliases={1 + count + i: i for i in range(len(begun))},
        )

    own = [item.kept[0] for item in attn_items]
    parts = range(len(ATTN_PARTS))
    plan = [(part, True, True, part, own[part][1]) for part in parts]
    at = 0
    for part, item in enumerate(attn_items):
        plan.append((part, False, True, len(parts), at))
        at += item.kept[0][2]
    begun = squares("squares_1", [array for array, _, _ in own] + [mirror], plan)
    came = [(hold(item.came[0], line.last), item.came[1]) for item in attn_items]
    passed = [swap(array, "core") for array, _ in came]
    begun = squares(
        "squares_2", [array for array, _ in came], [(part, True, False, part, came[part][1]) for part in parts], begun
    )
    vec_part = [item.now[1] for item in attn_items].index(vec_item.now[1])
    vec_own, vec_came = vec_item.kept[0], vec_item.came
    gwq, gwk, gwv, gwo, *vecs = squares(
        "squares_3", passed + [vec_own[0], vec_came[0], mirror],
        [(part, False, False, part, came[part][1]) for part in parts], begun,
        (
            (len(parts), vec_own[1]), (len(parts) + 1, vec_came[1]), (len(parts) + 2, at), (vec_part, vec_came[1])
        ),
    )
    return (
        output[None],
        grad_hidden[None],
        vecs[0],
        vecs[1],
        gwq,
        vecs[2],
        gwk,
        gwv,
        vecs[3],
        gwo,
        vecs[4],
        vecs[5],
        vecs[6],
        gw_in,
        vecs[8],
        gw_out,
        vecs[7],
    )


def solution(mesh):
    rows = P("dp", "mp", None)
    placed = (rows, P("dp", None, None), P("dp"), rows) + (P(),) * 11
    placed += (P(None, "mp"), P("mp"), P("mp", None), P(), rows)
    return jax.shard_map(
        local,
        mesh=mesh,
        in_specs=placed,
        out_specs=(rows, rows) + (P(),) * 11 + (P(None, "mp"), P("mp"), P("mp", None), P()),
        check_vma=False,
    )
```

```python
import math

import jax
import jax.numpy as jnp
from jax import lax
from jax.experimental import pallas as pl
from jax.experimental.pallas import tpu as pltpu
from jax.sharding import PartitionSpec as P

HD = 64
NORM_EPSILON = 1e-05
RIDGE_WEIGHT = 0.1
NOTHING = -1e30
GELU_SLOPE = math.sqrt(2.0 / math.pi)
GELU_CUBE = 0.044715
F32 = jnp.float32
BF16 = jnp.bfloat16
MEBI = 1 << 20


def mm(left, right):
    return jnp.dot(left, right, preferred_element_type=F32)


def mt(left, right):
    return lax.dot_general(left, right, (((1,), (1,)), ((), ())), preferred_element_type=F32)


def tm(left, right):
    return lax.dot_general(left, right, (((0,), (0,)), ((), ())), preferred_element_type=F32)


def summed(first, *others):
    total = first.astype(F32)
    for other in others:
        total = total + other.astype(F32)
    return total.astype(BF16)


def column_sum(values):
    return jnp.sum(values, axis=0, keepdims=True)


def normalized(values):
    row_mean = jnp.mean(values, axis=-1, keepdims=True)
    centered = values - row_mean
    row_var = jnp.mean(centered * centered, axis=-1, keepdims=True)
    inverse = lax.rsqrt(row_var + NORM_EPSILON)
    return centered * inverse, inverse


def norm_back(xhat, inverse, incoming, gain):
    g = incoming * gain
    mean_g = jnp.mean(g, axis=-1, keepdims=True)
    mean_gx = jnp.mean(g * xhat, axis=-1, keepdims=True)
    return inverse * (g - mean_g - xhat * mean_gx)


SMALL = pl.BlockSpec(memory_space=pltpu.SMEM)
VMEM = pl.BlockSpec(memory_space=pltpu.VMEM)
ANY = pl.BlockSpec(memory_space=pl.ANY)
HBM = pl.BlockSpec(memory_space=pltpu.HBM)


class Arriving:
    def __init__(self, source, held, sem):
        self.held, self.copy = held, pltpu.make_async_copy(source, held, sem)
        self.shape, self.dtype = held.shape, held.dtype
        self.here = False
        self.copy.start()

    def wait(self):
        if not self.here:
            self.copy.wait()
            self.here = True
        return self.held

    @property
    def at(self):
        return self.wait().at

    def __getitem__(self, index):
        return self.wait()[index]


class Leaving:
    def __init__(self, target, held, sem):
        self.held, self.copy = held, pltpu.make_async_copy(held, target, sem)
        self.shape, self.dtype = held.shape, held.dtype
        self.gone = False

    def leave(self):
        if not self.gone:
            self.copy.start()
            self.gone = True

    def __getitem__(self, index):
        return self.held[index]

    def __setitem__(self, index, value):
        self.held[index] = value
        if index is Ellipsis:
            self.leave()


class Line:
    def __init__(self):
        self.last = None

    def start(self, body, outs, name, operands, grid, in_specs, out_specs, scratch, after=(), aliases=None, far=(), limit=32, there=()):
        waits = list(after) + ([] if self.last is None else [self.last])
        operands = [pltpu.with_memory_space_constraint(o, pltpu.HBM) if i in there else o for i, o in enumerate(operands)]
        known, gone = len(operands), len(operands) + len(waits)
        results = pl.pallas_call(
            lambda *refs: body(*refs[:known], *refs[gone : gone + len(outs)], *refs[gone + len(outs) + 1 :]),
            out_shape=[(pltpu.HBM if i in far else pltpu.VMEM)(shape, dtype) for i, (shape, dtype) in enumerate(outs)]
            + [pltpu.VMEM((8, 128), F32)],
            grid=grid,
            in_specs=list(in_specs) + [ANY] * len(waits),
            out_specs=list(out_specs) + [VMEM],
            scratch_shapes=list(scratch),
            input_output_aliases=aliases or {},
            compiler_params=pltpu.CompilerParams(vmem_limit_bytes=limit * MEBI),
            cost_estimate=pl.CostEstimate(flops=0, bytes_accessed=0, transcendentals=0),
            name=name,
        )(*operands, *waits)
        *results, self.last = results
        return results

    def blocks(self, body, outs, name, operands, grid, in_specs, out_specs, scratch=(), **more):
        return self.start(body, outs, name, operands, grid, in_specs, out_specs, scratch, **more)

    def call(self, body, outs, name, operands, small=0, load=(), far=(), scratch=(), after=(), limit=16):
        outs = list(outs) + [(operands[i].shape, operands[i].dtype) for i in load]
        own, kept = len(scratch), len(outs) - len(load)
        in_specs = [SMALL if i < small else HBM if i in load else VMEM for i in range(len(operands))]
        out_specs = [HBM if i in far else VMEM for i in range(len(outs))]
        held = [pltpu.VMEM(*outs[i]) for i in far]
        sems = [pltpu.SemaphoreType.DMA((len(far) + len(load),))] if far or load else []

        def run(*refs):
            ins, targets, rest = refs[: len(operands)], refs[len(operands) : len(operands) + len(outs)], refs[len(operands) + len(outs) :]
            mine, buffers, sem = rest[:own], rest[own:], rest[-1] if sems else None
            ins, targets = list(ins), list(targets)
            for slot, i in enumerate(load):
                ins[i] = Arriving(ins[i], targets[kept + slot], sem.at[len(far) + slot])
            for slot, i in enumerate(far):
                targets[i] = Leaving(targets[i], buffers[slot], sem.at[slot])
            body(*ins, *targets[:kept], *mine)
            for i in load:
                ins[i].wait()
            for i in far:
                targets[i].leave()
            for i in far:
                targets[i].copy.wait()

        return self.start(
            run, outs, name, operands, (1,), in_specs, out_specs, list(scratch) + held + sems, after, far=far, limit=limit,
            there=tuple(load),
        )


def hold(value, *until):
    return lax.optimization_barrier((value,) + until)[0]


def at_half(bit, count):
    return pl.ds(pl.multiple_of(bit * count, count), count)


def fit_at_positions(size, fit_ref):
    half = size // 2
    spread = 1.0 / size
    row = lax.broadcasted_iota(jnp.int32, (half, half), 0)
    col = lax.broadcasted_iota(jnp.int32, (half, half), 1)
    eye = jnp.where(row == col, 1.0, 0.0).astype(F32)
    flip = jnp.where(row + col == half - 1, 1.0, 0.0).astype(BF16)

    def design(columns):
        apart = (row.astype(F32) + 0.5) / size - (columns.astype(F32) + 0.5) / size
        return jnp.exp(-(apart * apart) / (2.0 * spread * spread))

    def pieces(value):
        high = value.astype(BF16)
        return high, (value - high.astype(F32)).astype(BF16)

    def exact(left, right):
        (left_high, left_low), (right_high, right_low) = pieces(left), pieces(right)
        return mm(left_high, right_high) + (mm(left_high, right_low) + mm(left_low, right_high))

    def full(left, right):
        return jnp.dot(left, right, precision=lax.Precision.HIGHEST, preferred_element_type=F32)

    direct, mirrored = design(col), design(size - 1 - col)
    brackets, guesses = [], []
    for part in (direct + mirrored, direct - mirrored):
        bracket = full(part, part) + RIDGE_WEIGHT * eye
        low = bracket.astype(BF16)
        brackets.append(bracket)
        guesses.append(2.39060839 * eye - 0.96134588 * bracket + 0.09859958 * mm(low, low))
    for step in range(6):
        for which in range(2):
            bracket, guess = brackets[which], guesses[which]
            if step < 4:
                low = guess.astype(BF16)
                left = 2.0 * eye - mm(bracket.astype(BF16), low)
                guesses[which] = mm(low, left.astype(BF16))
            else:
                guesses[which] = exact(guess, 2.0 * eye - exact(bracket, guess))
    even, odd = (eye - RIDGE_WEIGHT * guess for guess in guesses)
    inner = (0.5 * (even + odd)).astype(BF16)
    outer = (0.5 * (even - odd)).astype(BF16)
    fit_ref[0:half, 0:half] = inner
    fit_ref[0:half, half:size] = mm(outer, flip).astype(BF16)
    fit_ref[half:size, 0:half] = mm(flip, outer).astype(BF16)
    fit_ref[half:size, half:size] = mm(flip, mm(inner, flip).astype(BF16)).astype(BF16)


VECTORS = ("gain1", "shift1", "b_q", "b_v", "b_o", "gain2", "shift2", "b_in", "b_out")


def vector(table, name):
    at = VECTORS.index(name)
    return table[at : at + 1, :]


def start_kernel(info, w_in, w_out, *refs):
    vectors, (fit, table, cut_in, cut_out) = refs[: len(VECTORS)], refs[-4:]
    fit_at_positions(fit.shape[0], fit)
    table[...] = jnp.zeros_like(table)
    for at, value in enumerate(vectors):
        table[at, :] = value[...]
    count = cut_in.shape[1]
    mine = at_half(scalar(info, "half"), count)
    cut_in[...] = w_in[:, mine]
    bias, pieces = vector(table, "b_in"), []
    for _ in range(3):
        pieces.append(bias.astype(BF16))
        bias = bias - pieces[-1].astype(F32)
    cut_out[0:count, :] = w_out[mine, :]
    cut_out[count:, :] = jnp.concatenate(pieces + [jnp.zeros((13, table.shape[1]), BF16)], axis=0)


def front_kernel(hidden, table, wq, wk, wv, normed, q, k, v):
    xhat, _ = normalized(hidden[...].astype(F32))
    low = (xhat * vector(table, "gain1") + vector(table, "shift1")).astype(BF16)
    normed[...] = low
    scale = 1.0 / math.sqrt(HD)
    q[...] = (mm(low, wq[...]) + vector(table, "b_q")).astype(BF16) * jnp.asarray(scale, BF16)
    k[...] = mm(low, wk[...]).astype(BF16)
    v[...] = (mm(low, wv[...]) + vector(table, "b_v")).astype(BF16)


def memory_kernel(info, arrived, past, positions, table, fit, wk, wv, recalled, km, vm, often):
    size = fit.shape[0]
    xhat, _ = normalized(arrived[...].astype(F32))
    before = xhat * vector(table, "gain1") + vector(table, "shift1")
    kept = past[...].astype(F32) * (1 - scalar(info, "reset")).astype(F32)
    earlier = jnp.where(scalar(info, "first") > 0, kept, before).astype(BF16)
    low = mm(fit[...], earlier).astype(BF16)
    recalled[...] = low
    km[...] = mm(low, wk[...]).astype(BF16)
    vm[...] = (mm(low, wv[...]) + vector(table, "b_v")).astype(BF16)
    place = lax.broadcasted_iota(jnp.int32, (size, positions.shape[1]), 0)
    hit = jnp.where(place == positions[...], 1.0, 0.0).astype(BF16)
    count = mt(jnp.ones((8, positions.shape[1]), BF16), hit)
    often[...] = jnp.where(count > 0.5, jnp.log(jnp.maximum(count, 1.0)), NOTHING)


def attend_pair(q, k, v, km, vm, often, e, mixed, linv):
    rows = q.shape[0]
    half = rows // 2
    lane = lax.broadcasted_iota(jnp.int32, (1, 2 * HD), 1)
    row = lax.broadcasted_iota(jnp.int32, (half, half), 0)
    col = lax.broadcasted_iota(jnp.int32, (half, half), 1)
    log_count = often[0:1, :]
    units = [(part, head) for part in range(2) for head in range(2)]
    scores = {}
    for part, head in units:
        here = slice(part * half, (part + 1) * half)
        mine = (lane >= head * HD) & (lane < (head + 1) * HD)
        query = jnp.where(mine, q[here, :], jnp.zeros((), BF16))
        near = mt(query, k[0 : (part + 1) * half, :])
        far = mt(query, km[...]) + log_count
        edge = jnp.where(col > row, NOTHING, near[:, part * half :])
        top = jnp.maximum(jnp.max(edge, axis=-1, keepdims=True), jnp.max(far, axis=-1, keepdims=True))
        if part:
            top = jnp.maximum(top, jnp.max(near[:, : part * half], axis=-1, keepdims=True))
        scores[part, head] = (near, edge, far, top)
    for part in range(2):
        here = slice(part * half, (part + 1) * half)
        seen = (part + 1) * half
        results = []
        for head in range(2):
            near, edge, far, top = scores[part, head]
            edge = jnp.exp(edge - top)
            far = jnp.exp(far - top)
            total = jnp.sum(edge, axis=-1, keepdims=True) + jnp.sum(far, axis=-1, keepdims=True)
            edge_low, far_low = edge.astype(BF16), far.astype(BF16)
            e[head, here, part * half : seen] = edge_low
            e[head, here, rows:] = far_low
            out = mm(edge_low, v[part * half : seen, :]) + mm(far_low, vm[...])
            if part:
                start = jnp.exp(near[:, : part * half] - top)
                total = total + jnp.sum(start, axis=-1, keepdims=True)
                start_low = start.astype(BF16)
                e[head, here, 0 : part * half] = start_low
                out = out + mm(start_low, v[0 : part * half, :])
            inverse = 1.0 / total
            results.append((out * inverse, inverse))
        first = lane < HD
        mixed[here, :] = jnp.where(first, results[0][0], results[1][0]).astype(BF16)
        linv[here, :] = jnp.where(first, results[0][1], results[1][1])


def attend_kernel(q, k, v, km, vm, often, *refs):
    e, mixed, linv = refs[-3:]
    attend_pair(q, k, v, km, vm, often, e, mixed, linv)


def attend_more_kernel(
    q, k, v, km, vm, often, e_done, mixed_done, linv_done, wo, table, hidden,
    e, mixed, linv, resid, normed2_a, normed2_b, every,
):
    step, rows = pl.program_id(0), q.shape[0]
    attend_pair(q, k, v, km, vm, often, e, mixed, linv)
    done, block = mixed_done.shape[1], mixed.shape[1]
    every[:, pl.ds(pl.multiple_of(done + step * block, block), block)] = mixed[...]

    @pl.when(step == pl.num_programs(0) - 1)
    def _():
        every[:, 0:done] = mixed_done[...]
        total = hidden[...].astype(F32) + mm(every[...], wo[...]) + vector(table, "b_o")
        resid[...] = total
        xhat, _ = normalized(total)
        normed2 = (xhat * vector(table, "gain2") + vector(table, "shift2")).astype(BF16)
        normed2_a[...] = normed2[: rows // 2]
        normed2_b[...] = normed2[rows // 2 :]


def mlp_block(x, cot, w_in, b_in, w_out):
    pre = mm(x, w_in) + b_in
    square = pre * pre
    bend = jnp.tanh(GELU_SLOPE * pre * (1.0 + GELU_CUBE * square))
    act = (0.5 * pre * (1.0 + bend)).astype(BF16)
    slope = 0.5 * (1.0 + bend) + (0.5 * GELU_SLOPE) * pre * (1.0 - bend * bend) * (1.0 + 3.0 * GELU_CUBE * square)
    gpre = (mt(cot, w_out) * slope).astype(BF16)
    return mm(act, w_out), mt(gpre, w_in), act, gpre


def mlp_kernel(xa, xb, xc, xd, cot0, cot1, w_in, b_in, w_out, out, gx, grads, g_bias, acts, gpres):
    block, width, units = xa.shape[0], xa.shape[1], acts.shape[1]
    bias = b_in[...] if b_in.shape[0] == 1 else vector(b_in, "b_in")
    parts = []
    for which, x in enumerate((xa, xb, xc, xd)):
        here, there = slice(which % 2 * block, (which % 2 + 1) * block), slice(which * block, (which + 1) * block)
        cot = (cot0, cot1)[which // 2]
        o, g, act, gpre = mlp_block(x[...], cot[here, :], w_in[...], bias, w_out[...])
        out[which // 2, here, :], gx[which // 2, here, :] = o.astype(BF16), g.astype(BF16)
        acts[there, :] = act
        gpres[there, :] = gpre
        parts.append((x, there))
    total = tm(xa[...], gpres[0:block, :])
    for x, there in parts[1:]:
        total = total + tm(x[...], gpres[there, :])
    grads[0:width, :] = total.astype(BF16)
    half = 2 * block
    grads[width : width + units, :] = (tm(acts[:half, :], cot0[...]) + tm(acts[half:, :], cot1[...])).astype(BF16)
    g_bias[...] = column_sum(gpres[...].astype(F32))


def mlp_far_kernel(other, info, xa, xb, xc, xd, cot0, cot1, w_in, w_out, *refs):
    out, gx, grads, g_bias, acts, gpres = refs[-6:]
    block, width, units = xa.shape[0], xa.shape[1], w_in.shape[1]
    half = scalar(info, "half")
    half = 1 - half if other else half
    mine = at_half(half, units)
    pieces = w_out[units : units + 16, mine].astype(F32)
    bias = pieces[0:1] + pieces[1:2] + pieces[2:3]
    parts = []
    for which, x in enumerate((xa, xb, xc, xd)):
        here, there = slice(which % 2 * block, (which % 2 + 1) * block), slice(which * block, (which + 1) * block)
        cot = (cot0, cot1)[which // 2]
        o, g, act, gpre = mlp_block(x[...], cot[here, :], w_in[...], bias, w_out[0:units, :])
        out[which // 2, here, :], gx[which // 2, here, :] = o.astype(BF16), g.astype(BF16)
        acts[there, :] = act
        gpres[there, :] = gpre
        parts.append((x, there))
    total = tm(xa[...], gpres[0:block, :])
    for x, there in parts[1:]:
        total = total + tm(x[...], gpres[there, :])
    grads[0:width, mine] = total.astype(BF16)
    total = tm(acts[: 2 * block, :], cot0[...]) + tm(acts[2 * block :, :], cot1[...])
    grads[pl.ds(pl.multiple_of(width + half * units, 128), units), :] = total.astype(BF16)
    g_bias[...] = column_sum(gpres[...].astype(F32))


def merge_kernel(gx, gx_far, gx_other, keep_gx, send_gx):
    keep_gx[...] = summed(gx[0], gx_far[0], gx_other[0])
    send_gx[...] = summed(gx[1], gx_far[1], gx_other[1])


def middle_kernel(
    gx, gx_more, resid, cot, table, mixed, wo, out_own, out_far, out_other, grad_mixed, grad_resid, gwo, vecs,
    send_a, send_b
):
    half = send_a.shape[0]
    send_a[...] = summed(out_own[1, 0:half, :], out_far[1, 0:half, :], out_other[1, 0:half, :])
    send_b[...] = summed(out_own[1, half:, :], out_far[1, half:, :], out_other[1, half:, :])
    xhat, inverse = normalized(resid[...])
    n = gx[...].astype(F32) + gx_more[...].astype(F32)
    cot_full = cot[...].astype(F32)
    total = cot_full + norm_back(xhat, inverse, n, vector(table, "gain2"))
    grad_resid[...] = total
    low = total.astype(BF16)
    grad_mixed[...] = mt(low, wo[...]).astype(BF16)
    gwo[...] = tm(mixed[...], low).astype(BF16)
    vecs[...] = jnp.concatenate(
        [
            column_sum(low.astype(F32)),
            column_sum(n * xhat),
            column_sum(n),
            column_sum(cot_full),
            jnp.zeros((4, n.shape[1]), F32),
        ],
        axis=0,
    )


def attend_back_kernel(q, k, v, km, vm, e, linv, mixed, gmix, *refs):
    dq, dk, dv, dkm, dvm, ds, queries, grads = refs[-8:]
    rows = q.shape[0]
    half = rows // 2
    lane = lax.broadcasted_iota(jnp.int32, (1, 2 * HD), 1)
    scale = 1.0 / math.sqrt(HD)
    grad = gmix[...].astype(F32) * linv[...]
    product = grad * mixed[...].astype(F32)
    for head in range(2):
        mine = (lane >= head * HD) & (lane < (head + 1) * HD)
        all_rows = slice(head * rows, (head + 1) * rows)
        queries[all_rows, :] = jnp.where(mine, q[...], jnp.zeros((), BF16))
        grads[all_rows, :] = jnp.where(mine, grad, 0.0).astype(BF16)
    for head in range(2):
        mine = (lane >= head * HD) & (lane < (head + 1) * HD)
        dots = jnp.sum(jnp.where(mine, product, 0.0), axis=-1, keepdims=True)
        for part in range(2):
            here = slice(part * half, (part + 1) * half)
            there = slice(head * rows + part * half, head * rows + (part + 1) * half)
            seen = (part + 1) * half
            dot, grad_low = dots[here], grads[there, :]
            near = e[head, here, 0:seen].astype(F32) * (mt(grad_low, v[0:seen, :]) - dot)
            far = e[head, here, rows:].astype(F32) * (mt(grad_low, vm[...]) - dot)
            ds[there, 0:seen] = near.astype(BF16)
            ds[there, rows:] = far.astype(BF16)
    for part in range(2):
        here = slice(part * half, (part + 1) * half)
        seen = (part + 1) * half
        parts = []
        for head in range(2):
            there = slice(head * rows + part * half, head * rows + (part + 1) * half)
            parts.append(mm(ds[there, 0:seen], k[0:seen, :]) + mm(ds[there, rows:], km[...]))
        dq[here, :] = (jnp.where(lane < HD, parts[0], parts[1]) * scale).astype(BF16)
    late = [slice(head * rows + half, (head + 1) * rows) for head in range(2)]

    def both(left, right):
        first = tm(left[...], right(slice(0, half)))
        second = sum(tm(left[at, :], right(slice(half, rows), head)) for head, at in enumerate(late))
        return first, second, tm(left[...], right(slice(rows, None)))

    def scores(columns, head=None):
        return ds[:, columns] if head is None else ds[late[head], columns]

    def weights(columns, head=None):
        if head is None:
            return e[:, :, columns].reshape(2 * rows, -1)
        return e[head, half:, columns]

    for left, right, near, far in ((queries, scores, dk, dkm), (grads, weights, dv, dvm)):
        first, second, rest = both(left, right)
        near[0:half, :] = first.T.astype(BF16)
        near[half:, :] = second.T.astype(BF16)
        far[...] = rest.T.astype(BF16)


def recall_back_kernel(info, dkm, dvm, wk, wv, fit, arrived, grad_memory, vecs):
    grad_recalled = (mt(dkm[...], wk[...]) + mt(dvm[...], wv[...])).astype(BF16)
    handed = tm(fit[...], grad_recalled).astype(BF16)
    grad_memory[...] = handed
    xhat, _ = normalized(arrived[...].astype(F32))
    n = jnp.where(scalar(info, "first") > 0, 0.0, handed.astype(F32))
    vecs[...] = jnp.concatenate([column_sum(n * xhat), column_sum(n), jnp.zeros((6, n.shape[1]), F32)], axis=0)


def weight_grads_kernel(info, normed, recalled, dq, dk, dv, dkm, dvm, gwo, send, *refs):
    low, rec = normed[...], recalled[...]
    *parts, whole = refs
    half = whole.shape[0] // 2
    core = scalar(info, "core")
    grads = (
        lambda: tm(low, dq[...]),
        lambda: tm(low, dk[...]) + tm(rec, dkm[...]),
        lambda: tm(low, dv[...]) + tm(rec, dvm[...]),
        None,
    )
    for which, grad in enumerate(grads):
        source = gwo
        if grad is not None:
            whole[...] = grad().astype(BF16)
            source = whole
        start = begin = 0
        for part in parts:
            piece = part.shape[0] // 8
            for first in range(2):
                at = (4 * first + which) * piece
                send[begin + at : begin + at + piece, :] = source[
                    pl.ds(pl.multiple_of((1 - core) * half + start, 16), piece), :
                ]
                part[at : at + piece, :] = source[pl.ds(pl.multiple_of(core * half + start, 16), piece), :]
                start += piece
            begin += part.shape[0]


def project_back_kernel(info, hidden, dq, dk, dv, dvm, wq, wk, wv, vecs_mid, vecs_rec, gb_own, gb_far, gb_other, gn, vecs):
    width = hidden.shape[1]
    n = mt(dq[...], wq[...]) + mt(dk[...], wk[...]) + mt(dv[...], wv[...])
    gn[...] = n
    xhat, _ = normalized(hidden[...].astype(F32))
    shard = lax.broadcasted_iota(jnp.int32, (4, 1), 0)
    halves = [gb_far[...], gb_other[...]]
    far = jnp.where(scalar(info, "half") == 0, jnp.concatenate(halves, axis=1), jnp.concatenate(halves[::-1], axis=1))
    bias_rows = jnp.where(shard == scalar(info, "me"), gb_own[...], 0.0) + jnp.where(shard == scalar(info, "far"), far, 0.0)
    vecs[...] = jnp.concatenate(
        [
            column_sum(n * xhat) + vecs_rec[0:1, :],
            column_sum(n) + vecs_rec[1:2, :],
            column_sum(dq[...].astype(F32)),
            column_sum(dv[...].astype(F32)) + column_sum(dvm[...].astype(F32)),
            vecs_mid[0:4, :],
            bias_rows,
            jnp.zeros((4, width), F32),
        ],
        axis=0,
    ).astype(BF16)


def last_kernel(hidden, table, gn, handed, grad_resid, grad_hidden):
    xhat, inverse = normalized(hidden[...].astype(F32))
    n = gn[...] + handed[...].astype(F32)
    grad_hidden[...] = grad_resid[...] + norm_back(xhat, inverse, n, vector(table, "gain1"))


def added(left, right):
    return (left.astype(F32) + right.astype(F32)).astype(BF16)


MLP_PARTS = (
    (("y", "x", "z2", "z1"), 384), (("y", "z1", "x", "z2"), 128), (("x", "y", "z2", "z1"), 128),
    (("x", "z1", "y", "z2"), 384), (("z1", "y", "x", "z2"), 384), (("z1", "x", "y", "z2"), 128),
)
ATTN_PARTS = ((("y", "x", "z1", "z2"), 512), (("x", "z1", "y", "z2"), 512), (("z1", "y", "x", "z2"), 512))
AXES = {"core": ("mp", 1), "y": ("mp", 2), "x": ("dp", 1), "z1": ("dp", 2), "z2": ("dp", 4)}


def swap(value, link):
    axis, mask = AXES[link] if link in AXES else ("dp", int(link))
    return lax.ppermute(value, axis, [(i, i ^ mask) for i in range(lax.axis_size(axis))])


def bit_of(link):
    axis, mask = AXES[link]
    return (lax.axis_index(axis) // mask) % 2


SCALAR = {"core": 0, "y": 1, "x": 2, "z1": 3, "z2": 4, "me": 5, "far": 6, "first": 7, "reset": 8, "half": 9}


def scalar_array(reset):
    bit = {link: bit_of(link) for link in AXES}
    me = lax.axis_index("mp")
    values = dict(bit, me=me, far=me ^ 2, first=me == 0, reset=reset, half=bit["x"] ^ bit["z1"])
    row = lax.broadcasted_iota(jnp.int32, (1, 16), 1)
    packed = jnp.zeros((1, 16), jnp.int32)
    for name, value in values.items():
        packed = jnp.where(row == SCALAR[name], jnp.asarray(value, jnp.int32), packed)
    return packed


def scalar(info, name):
    return info[0, SCALAR[name]]


class Item:
    def __init__(self, steps, *kept, now=None, came=None):
        self.steps, self.kept, self.now, self.came = list(steps), list(kept), now, came


class Rounds:
    def __init__(self, line, info):
        self.line, self.info = line, info

    def go(self, name, items, mirror=False):
        arrays, sends, outs, jobs = [], {}, [], []

        def slot(array):
            for which, known in enumerate(arrays):
                if known is array:
                    return which
            arrays.append(array)
            return len(arrays) - 1

        for item in items:
            kind, link = item.now or ("start", None)
            came, at = (slot(item.came[0]), item.came[1]) if link else (None, 0)
            sources = []
            for array, first, rows in item.kept:
                sources.append((slot(array), first, came, at, rows, kind, link))
                at += rows
            rows = item.kept[0][2] * (2 if kind == "double" else 1)
            step = item.steps.pop(0) if item.steps else None
            sent = sends.setdefault(step[1], [0]) if step else None
            if step is None:
                jobs.append((sources[0], "all", None, len(outs), 0, rows))
                item.kept = [("out", len(outs), rows)]
                outs.append(rows)
            elif step[0] in ("swap", "double"):
                jobs.append((sources[0], "all", None, step[1], sent[0], rows))
                item.came, item.kept = (None, sent[0]), [(step[1], sent[0], rows)]
                sent[0] += rows
                if mirror:
                    again = sends.setdefault("core", [0])
                    jobs.append((sources[0], "all", None, "core", again[0], rows))
                    again[0] += rows
            elif step[0] == "pair":
                jobs.append((sources[0], "all", None, len(outs), 0, rows))
                jobs.append((sources[1], "all", None, step[1], sent[0], rows))
                item.came, item.kept = (None, sent[0]), [("out", len(outs), rows)]
                sent[0] += rows
                outs.append(rows)
            else:
                half, kept = rows // 2, []
                item.came = (None, sent[0])
                for source in sources:
                    jobs.append((source, "mine", step[1], len(outs), 0, half))
                    jobs.append((source, "other", step[1], step[1], sent[0], half))
                    kept.append(("out", len(outs), half))
                    sent[0] += half
                    outs.append(half)
                item.kept = kept
            item.now = step
        links = list(sends)
        width = arrays[0].shape[1]
        shapes = [((rows, width), BF16) for rows in outs] + [((sends[link][0], width), BF16) for link in links]

        def body(info, *refs):
            ins, results = refs[: len(arrays)], refs[len(arrays) :]
            for (kept, first, came, at, rows, kind, over), what, link, target, base, count in jobs:
                out = results[len(outs) + links.index(target) if isinstance(target, str) else target]
                if kind == "double":
                    for bit, ref, start in ((scalar(info, over), kept, first), (1 - scalar(info, over), came, at)):
                        out[pl.ds(pl.multiple_of(base + bit * rows, 16), rows), :] = ins[ref][start : start + rows, :]
                    continue
                start = 0
                if what != "all":
                    bit = scalar(info, link)
                    start = (bit if what == "mine" else 1 - bit) * count

                def here(base):
                    if what == "all":
                        return slice(base, base + count)
                    return pl.ds(pl.multiple_of(base + start, 16), count)

                value = ins[kept][here(first), :]
                if kind != "start":
                    value = added(value, ins[came][here(at), :])
                out[base : base + count, :] = value

        results = self.line.call(body, shapes, f"round_{name}", (self.info, *arrays), small=1, limit=4)
        sent = dict(zip(links, results[len(outs) :]))
        arrived = {link: swap(array, link) for link, array in sent.items()}
        self.mirror = arrived.get("core")
        for item in items:
            if item.now:
                item.came = (arrived[item.now[1]], item.came[1])
            item.kept = [
                (results[first], 0, rows) if where == "out" else (sent[where], first, rows) for where, first, rows in item.kept
            ]


def more_links():
    return [str(8 << bit) for bit in range((lax.axis_size("dp") // 8).bit_length() - 1)]


def steps_of(order, paired):
    first = [("pair" if link == "y" and paired else "half", link) for link in order[:3]]
    back = [("double", link) for link in order[2::-1] if not (link == "y" and paired)]
    return first + [("swap", link) for link in [order[3]] + more_links()] + back


def squares_kernel(plan, count, skip, vectors, info, *refs):
    ins, rest = refs[:count], refs[count + skip :]
    outs, rest = rest[:4], rest[4:]
    vecs, rest = (rest[:9], rest[9:]) if vectors else ((), rest)
    buffers, sems = rest[: 4 * len(plan)], rest[4 * len(plan)]
    copies = []

    def leave(buffer, target):
        copies.append(pltpu.make_async_copy(buffer, target, sems.at[len(copies)]))
        copies[-1].start()

    half = outs[0].shape[0] // 2
    for block, (part, this_core, this_half, array, first, start, piece) in enumerate(plan):
        core, bit = scalar(info, "core"), scalar(info, ATTN_PARTS[part][0][0])
        core, bit = core if this_core else 1 - core, bit if this_half else 1 - bit
        at = pl.ds(pl.multiple_of(core * half + start + bit * piece, 16), piece)
        for which, out in enumerate(outs):
            buffer = buffers[4 * block + which]
            buffer[...] = ins[array][first + which * piece : first + (which + 1) * piece, :].astype(F32)
            leave(buffer, out.at[at, :])
    if vectors:
        rows = [ins[array][first : first + 16, :].astype(F32) for array, first in vectors]
        total = (rows[0] + rows[1]) + (rows[2] + rows[3])
        me, row = scalar(info, "me"), total[8:9, :]
        for at in range(1, 4):
            row = jnp.where(me == at, total[8 + at : 9 + at, :], row)
        held = rest[4 * len(plan) + 1 :]
        for at, (buffer, out) in enumerate(zip(held, vecs)):
            buffer[...] = total[at, :] if at < 8 else row[0, :]
            leave(buffer, out)
    for copy in copies:
        copy.wait()


def mlp_grads_kernel(plan, info, *refs):
    ins, (gw_in, gw_out, whole) = refs[: 2 * len(plan)], refs[2 * len(plan) :]
    for which, (link, rows, own_at, came_at, base) in enumerate(plan):
        for bit, ref, at in ((scalar(info, link), ins[2 * which], own_at), (1 - scalar(info, link), ins[2 * which + 1], came_at)):
            whole[pl.ds(pl.multiple_of(base + bit * rows, 16), rows), :] = ref[at : at + rows, :]
    count = gw_in.shape[0]
    gw_in[...] = whole[:count, :].astype(F32)
    gw_out[...] = whole[count:, :].astype(F32)


def emit_kernel(resid, out_own, out_far, out_other, came_a, came_b, table, output):
    came = jnp.concatenate([came_a[...], came_b[...]], axis=0).astype(F32)
    total = resid[...] + summed(out_own[0], out_far[0], out_other[0]).astype(F32) + came + vector(table, "b_out")
    output[...] = total.astype(BF16)


def from_behind(value, axis, steps):
    count = lax.axis_size(axis)
    leading, last = (max(0, -steps), min(count, count - steps))
    return lax.ppermute(value, axis, [(source, source + steps) for source in range(leading, last)])


def local(
    hidden,
    past_states,
    reset_flags,
    sample_positions,
    norm1_gain,
    norm1_shift,
    w_query,
    bias_query,
    w_key,
    w_value,
    bias_value,
    w_attn_out,
    bias_attn_out,
    norm2_gain,
    norm2_shift,
    w_mlp_in,
    bias_mlp_in,
    w_mlp_out,
    bias_mlp_out,
    cotangent,
):
    rows, width = hidden.shape[1], hidden.shape[2]
    size = past_states.shape[1]
    units = w_mlp_in.shape[1]
    assert rows == size and sample_positions.shape[2] == size
    pairs = width // (2 * HD)
    arr, cot = hidden[0], cotangent[0]
    half_bf = ((rows // 2, width), BF16)
    row_bf, row_f = ((rows, width), BF16), ((rows, width), F32)
    square_f, square_bf, vec_f = ((width, width), F32), ((width, width), BF16), ((8, width), F32)

    line = Line()
    info = scalar_array(reset_flags[0])
    half_w, third = width // 2, 2 * width // 3

    arrived = from_behind(arr, "mp", 1)
    (
        fit, table, cut_in, cut_out,
        w_mlp_in, w_mlp_out, arr, w_query, w_key, w_value, past, positions, w_attn_out, cot, *_
    ) = line.call(
        start_kernel,
        [((size, size), BF16), ((16, width), F32), ((width, units // 2), BF16), ((units // 2 + 16, width), BF16)], "start",
        (
            info, w_mlp_in, w_mlp_out, norm1_gain, norm1_shift, bias_query, bias_value, bias_attn_out, norm2_gain,
            norm2_shift, bias_mlp_in, bias_mlp_out, arr, w_query, w_key, w_value, past_states[0], sample_positions[0],
            w_attn_out, cot,
        ),
        small=1, load=(1, 2, 12, 13, 14, 15, 16, 17, 18, 19) + tuple(range(3, 12)), far=(2, 3),
    )
    far_cut, far_out = swap(cut_in, "y"), swap(cut_out, "y")
    normed, q, k, v = line.call(front_kernel, [row_bf] * 4, "front", (arr, table, w_query, w_key, w_value))
    recalled, km, vm, often = line.call(
        memory_kernel, [row_bf] * 3 + [((8, size), F32)], "memory",
        (info, arrived, past, positions, table, fit, w_key, w_value), small=1,
    )

    calls = 3 if pairs % 3 == 0 else 1
    per = pairs // calls
    blocks = [pl.BlockSpec((rows, 2 * HD), lambda i, c=c: (0, i + c * per)) for c in range(calls)]
    e_blocks = [pl.BlockSpec((2, rows, rows + size), lambda i, c=c: (i + c * per, 0, 0)) for c in range(calls)]
    grid = (per,)
    shared = (q, k, v, km, vm, often)
    results = [((2 * pairs, rows, rows + size), BF16), row_bf, row_f]
    begun = ()
    for call in range(calls - 1):
        e, mixed, linv = line.blocks(
            attend_kernel, results, f"attend_{call}", shared + begun, grid,
            [blocks[call]] * 5 + [VMEM] + [ANY] * len(begun), [e_blocks[call]] + [blocks[call]] * 2,
            far=(0,), limit=20, aliases={6 + i: i for i in range(len(begun))}, there=(6,) if begun else (),
        )
        begun = (e, mixed, linv)
    cot_sib = swap(cot, "core")
    e, mixed, linv, resid, *normed2 = line.blocks(
        attend_more_kernel, results + [row_f, half_bf, half_bf], "attend_more",
        shared + begun + (w_attn_out, table, arr), grid,
        [blocks[-1]] * 5 + [VMEM, ANY, pl.BlockSpec((rows, (calls - 1) * per * 2 * HD), lambda i: (0, 0)), ANY] + [VMEM] * 3,
        [e_blocks[-1]] + [blocks[-1]] * 2 + [VMEM] * 3,
        scratch=[pltpu.VMEM((rows, width), BF16)], aliases={6: 0, 7: 1, 8: 2}, far=(0,), limit=24, there=(6,),
        after=(cot_sib,),
    )
    normed2 += [swap(half, "core") for half in normed2]
    far_in, far_out = hold(far_cut, *normed2[2:]), hold(far_out, *normed2[2:])
    more_in, more_out = swap(far_in, "x"), swap(far_out, "z1")
    part, both = ((third, width), BF16), ((2, rows, width), BF16)
    bias_f, stacked = ((1, units), F32), ((width + units, width), BF16)
    out_own, gx_own, g_own, gb_own = line.call(
        mlp_kernel, [both, both, stacked, bias_f], "mlp_own",
        (*normed2, cot, cot_sib, w_mlp_in, table, w_mlp_out), limit=18,
        scratch=[pltpu.VMEM((2 * rows, units), BF16)] * 2,
    )
    half_bias, rows_of = ((1, units // 2), F32), (*normed2, cot, cot_sib)
    scratch = [pltpu.VMEM((2 * rows, units // 2), BF16)] * 2
    out_far, gx_far, g_far, gb_far = line.call(
        lambda *refs: mlp_far_kernel(False, *refs), [both, both, stacked, half_bias], "mlp_far",
        (info, *rows_of, far_in, far_out), small=1, limit=14, scratch=scratch,
    )
    out_other, gx_other, g_far, gb_other = line.start(
        lambda *refs: mlp_far_kernel(True, *refs), [both, both, stacked, half_bias], "mlp_other",
        (info, *rows_of, more_in, more_out, g_far), (1,), [SMALL] + [VMEM] * 9, [VMEM] * 4, scratch, limit=14, aliases={9: 2},
    )
    gx_keep, gx_send = line.call(merge_kernel, [row_bf] * 2, "merge", (gx_own, gx_far, gx_other))
    gx_came = swap(gx_send, "core")
    rounds = Rounds(line, info)
    mlp_items, at = [], 0
    for order, count in MLP_PARTS:
        mlp_items.append(Item(steps_of(order, True), (g_own, at, count), (g_far, at, count)))
        at += count
    rounds.go("a", mlp_items)

    grad_mixed, grad_resid, gwo, vecs_mid, *out_send = line.call(
        middle_kernel, [row_bf, row_f, square_bf, vec_f, half_bf, half_bf], "middle",
        (gx_keep, gx_came, resid, cot, table, mixed, w_attn_out, out_own, out_far, out_other),
    )
    out_came = [swap(half, "core") for half in out_send]
    grads = ()
    back = 2 if pairs % 2 == 0 else 1
    per = pairs // back
    blocks = [pl.BlockSpec((rows, 2 * HD), lambda i, c=c: (0, i + c * per)) for c in range(back)]
    e_blocks = [pl.BlockSpec((2, rows, rows + size), lambda i, c=c: (i + c * per, 0, 0)) for c in range(back)]
    grid = (per,)
    for which in range(back):
        grads = line.blocks(
            attend_back_kernel, [row_bf] * 5, f"attend_back_{which}", (q, k, v, km, vm, e, linv, mixed, grad_mixed) + tuple(grads),
            grid, [blocks[which]] * 5 + [e_blocks[which]] + [blocks[which]] * 3 + [ANY] * len(grads),
            [blocks[which]] * 5, there=(5,), limit=20, after=out_came if which else (),
            scratch=[pltpu.VMEM((2 * rows, rows + size), BF16)] + [pltpu.VMEM((2 * rows, 2 * HD), BF16)] * 2, aliases={9 + i: i for i in range(len(grads))},
        )
    dq, dk, dv, dkm, dvm = grads
    rounds.go("b", mlp_items)
    send, *keeps = line.call(
        weight_grads_kernel, [((2 * width, width), BF16)] + [((count, width), BF16) for _, count in ATTN_PARTS], "weight_grads",
        (info, normed, recalled, dq, dk, dv, dkm, dvm, gwo), small=1, scratch=[pltpu.VMEM((width, width), BF16)],
    )
    core_came = swap(send, "core")
    attn_items, at = [], 0
    for (order, count), kept in zip(ATTN_PARTS, keeps):
        attn_items.append(Item(steps_of(order, False), (kept, 0, count), now=("half", "core"), came=(core_came, at)))
        at += count
    grad_memory, vecs_rec = line.call(
        recall_back_kernel, [row_bf, vec_f], "recall_back", (info, dkm, dvm, w_key, w_value, fit, arrived), small=1,
    )
    handed = from_behind(grad_memory, "mp", -1)
    gn, vecs = line.call(
        project_back_kernel, [row_f, ((16, width), BF16)], "project_back",
        (info, arr, dq, dk, dv, dvm, w_query, w_key, w_value, vecs_mid, vecs_rec, gb_own, gb_far, gb_other), small=1,
    )
    rounds.go("c", mlp_items + attn_items)
    (output,) = line.call(emit_kernel, [row_bf], "emit", (resid, out_own, out_far, out_other, *out_came, table), far=(0,))
    (grad_hidden,) = line.call(
        last_kernel, [row_f], "last", (arr, table, gn, handed, grad_resid), far=(0,)
    )
    vec_item = Item([("swap", link) for link in ["z2"] + more_links() + ["x", "z1", "y"]], (vecs, 0, 16))
    rounds.go("d", mlp_items + attn_items)
    for link in more_links():
        rounds.go("d" + link, mlp_items)
    rounds.go("e", mlp_items + attn_items)
    rounds.go("f", mlp_items + attn_items + [vec_item])
    for link in more_links():
        rounds.go("f" + link, attn_items + [vec_item])
    mlp_now = [(*item.kept[0], *item.came, item.now[1]) for item in mlp_items]
    rounds.go("g", attn_items + [vec_item])
    rounds.go("h", attn_items + [vec_item])
    plan, operands, at = [], [], 0
    for own, first, count, came, came_at, link in mlp_now:
        plan.append((link, count, first, came_at, at))
        operands += [own, came]
        at += 2 * count
    gw_in, gw_out = line.call(
        lambda *refs: mlp_grads_kernel(plan, *refs), [((width, units), F32), ((units, width), F32)], "mlp_grads",
        (info, *operands), small=1, far=(0, 1), scratch=[pltpu.VMEM((width + units, width), BF16)], limit=24,
    )
    rounds.go("i", attn_items + [vec_item], mirror=True)
    mirror = rounds.mirror

    def squares(name, arrays, plan, begun=(), vectors=()):
        starts, at = [], 0
        for _, rows_of in ATTN_PARTS:
            starts.append((at, rows_of // 8))
            at += rows_of // 4
        plan = [block + starts[block[0]] for block in plan]
        count, more = len(arrays), 9 if vectors else 0
        scratch = [pltpu.VMEM((block[-1], width), F32) for block in plan for _ in range(4)] + [pltpu.SemaphoreType.DMA((4 * len(plan) + more,))]
        return line.start(
            lambda *refs: squares_kernel(plan, count, len(begun), vectors, *refs), [square_f] * 4 + [((width,), F32)] * more, name,
            (info, *arrays, *begun), (1,), [SMALL] + [VMEM] * count + [HBM] * len(begun), [HBM] * (4 + more),
            scratch + [pltpu.VMEM((width,), F32)] * more, far=tuple(range(4 + more)), limit=16,
            there=tuple(range(1 + count, 1 + count + len(begun))), aliases={1 + count + i: i for i in range(len(begun))},
        )

    own = [item.kept[0] for item in attn_items]
    parts = range(len(ATTN_PARTS))
    plan = [(part, True, True, part, own[part][1]) for part in parts]
    at = 0
    for part, item in enumerate(attn_items):
        plan.append((part, False, True, len(parts), at))
        at += item.kept[0][2]
    begun = squares("squares_1", [array for array, _, _ in own] + [mirror], plan)
    came = [(hold(item.came[0], line.last), item.came[1]) for item in attn_items]
    passed = [swap(array, "core") for array, _ in came]
    begun = squares(
        "squares_2", [array for array, _ in came], [(part, True, False, part, came[part][1]) for part in parts], begun
    )
    vec_part = [item.now[1] for item in attn_items].index(vec_item.now[1])
    vec_own, vec_came = vec_item.kept[0], vec_item.came
    gwq, gwk, gwv, gwo, *vecs = squares(
        "squares_3", passed + [vec_own[0], vec_came[0], mirror],
        [(part, False, False, part, came[part][1]) for part in parts], begun,
        (
            (len(parts), vec_own[1]), (len(parts) + 1, vec_came[1]), (len(parts) + 2, at), (vec_part, vec_came[1])
        ),
    )
    return (
        output[None],
        grad_hidden[None],
        vecs[0],
        vecs[1],
        gwq,
        vecs[2],
        gwk,
        gwv,
        vecs[3],
        gwo,
        vecs[4],
        vecs[5],
        vecs[6],
        gw_in,
        vecs[8],
        gw_out,
        vecs[7],
    )


def solution(mesh):
    rows = P("dp", "mp", None)
    placed = (rows, P("dp", None, None), P("dp"), rows) + (P(),) * 11
    placed += (P(None, "mp"), P("mp"), P("mp", None), P(), rows)
    return jax.shard_map(
        local,
        mesh=mesh,
        in_specs=placed,
        out_specs=(rows, rows) + (P(),) * 11 + (P(None, "mp"), P("mp"), P("mp", None), P()),
        check_vma=False,
    )
```
